32 devices in a mesh: dp: 4 (over y, core), heads: 2 (over x), hidden: 4 (over z).
Axes of the slice: x: 2, y: 2, z: 4, core: 2. Of those that a mesh axis runs over, the one named last changes fastest.
Arguments:
- patches: bfloat16 [32, 196, 768], P(('dp', 'heads', 'hidden')), may hold values from -6 to 6
- labels: int32 [32], P('dp'), may hold values from 0 to 999
- w_patch: float32 [768, 768], P(None, ('dp', 'heads', 'hidden')), may hold values from -0.21875 to 0.21875
- table: float32 [200, 768], P(None, ('dp', 'heads', 'hidden')), may hold values from -3 to 3
- gains: float32 [4, 768], P(None, ('dp', 'heads', 'hidden')), may hold values from 0.5 to 1.5
- w_head: float32 [768, 1000], P(('dp', 'heads', 'hidden')), may hold values from -6 to 6
- w_qkv: float32 [768, 3, 768], P(('dp', 'hidden'), None, 'heads'), may hold values from -0.21875 to 0.21875
- w_out: float32 [768, 768], P(('heads', 'hidden'), 'dp'), may hold values from -1.75 to 1.75
- w_up: float32 [768, 3072], P('dp', ('heads', 'hidden')), may hold values from -0.21875 to 0.21875
- w_down: float32 [3072, 768], P(('heads', 'hidden'), 'dp'), may hold values from -0.109375 to 0.109375
- first_patch: float32 [768, 768], P(None, ('dp', 'heads', 'hidden')), may hold values from -2.3841858e-07 to 2.3841858e-07
- first_table: float32 [200, 768], P(None, ('dp', 'heads', 'hidden')), may hold values from -2.3841858e-07 to 2.3841858e-07
- first_gains: float32 [4, 768], P(None, ('dp', 'heads', 'hidden')), may hold values from -7.1525574e-07 to 7.1525574e-07
- first_head: float32 [768, 1000], P(('dp', 'heads', 'hidden')), may hold values from -2.3841858e-07 to 2.3841858e-07
- first_qkv: float32 [768, 3, 768], P(('dp', 'hidden'), None, 'heads'), may hold values from -2.3841858e-07 to 2.3841858e-07
- first_out: float32 [768, 768], P(('heads', 'hidden'), 'dp'), may hold values from -2.3841858e-07 to 2.3841858e-07
- first_up: float32 [768, 3072], P('dp', ('heads', 'hidden')), may hold values from -2.3841858e-07 to 2.3841858e-07
- first_down: float32 [3072, 768], P(('heads', 'hidden'), 'dp'), may hold values from -2.3841858e-07 to 2.3841858e-07
- second_patch: float32 [768, 768], P(None, ('dp', 'heads', 'hidden')), may hold values from 1.1638214e-16 to 4.6552857e-16
- second_table: float32 [200, 768], P(None, ('dp', 'heads', 'hidden')), may hold values from 1.4547768e-17 to 5.819107e-17
- second_gains: float32 [4, 768], P(None, ('dp', 'heads', 'hidden')), may hold values from 1.0474392e-15 to 4.189757e-15
- second_head: float32 [768, 1000], P(('dp', 'heads', 'hidden')), may hold values from 1.1638214e-16 to 4.6552857e-16
- second_qkv: float32 [768, 3, 768], P(('dp', 'hidden'), None, 'heads'), may hold values from 1.1638214e-16 to 4.6552857e-16
- second_out: float32 [768, 768], P(('heads', 'hidden'), 'dp'), may hold values from 1.1638214e-16 to 4.6552857e-16
- second_up: float32 [768, 3072], P('dp', ('heads', 'hidden')), may hold values from 5.819107e-18 to 2.3276427e-17
- second_down: float32 [3072, 768], P(('heads', 'hidden'), 'dp'), may hold values from 1.1638214e-16 to 4.6552857e-16
Outputs:
- loss_sum: float32 [], replicated
- grad_norm: float32 [], replicated
- new_first_patch: float32 [768, 768], P(None, ('dp', 'heads', 'hidden'))
- new_first_table: float32 [200, 768], P(None, ('dp', 'heads', 'hidden'))
- new_first_gains: float32 [4, 768], P(None, ('dp', 'heads', 'hidden'))
- new_first_head: float32 [768, 1000], P(('dp', 'heads', 'hidden'))
- new_first_qkv: float32 [768, 3, 768], P(('dp', 'hidden'), None, 'heads')
- new_first_out: float32 [768, 768], P(('heads', 'hidden'), 'dp')
- new_first_up: float32 [768, 3072], P('dp', ('heads', 'hidden'))
- new_first_down: float32 [3072, 768], P(('heads', 'hidden'), 'dp')
- new_second_patch: float32 [768, 768], P(None, ('dp', 'heads', 'hidden'))
- new_second_table: float32 [200, 768], P(None, ('dp', 'heads', 'hidden'))
- new_second_gains: float32 [4, 768], P(None, ('dp', 'heads', 'hidden'))
- new_second_head: float32 [768, 1000], P(('dp', 'heads', 'hidden'))
- new_second_qkv: float32 [768, 3, 768], P(('dp', 'hidden'), None, 'heads')
- new_second_out: float32 [768, 768], P(('heads', 'hidden'), 'dp')
- new_second_up: float32 [768, 3072], P('dp', ('heads', 'hidden'))
- new_second_down: float32 [3072, 768], P(('heads', 'hidden'), 'dp')
- new_w_patch: float32 [768, 768], P(None, ('dp', 'heads', 'hidden'))
- new_table: float32 [200, 768], P(None, ('dp', 'heads', 'hidden'))
- new_gains: float32 [4, 768], P(None, ('dp', 'heads', 'hidden'))
- new_w_head: float32 [768, 1000], P(('dp', 'heads', 'hidden'))
- new_w_qkv: float32 [768, 3, 768], P(('dp', 'hidden'), None, 'heads')
- new_w_out: float32 [768, 768], P(('heads', 'hidden'), 'dp')
- new_w_up: float32 [768, 3072], P('dp', ('heads', 'hidden'))
- new_w_down: float32 [3072, 768], P(('heads', 'hidden'), 'dp')
The draws below stay inside these ranges and needn't reach their ends.
All inputs are finite; a program needn't handle non-finite values.
Results may differ from the reference program's by a relative error of at most 0.014.
The reference program's roundings to bfloat16 on the way (of `stream_in`, `normed`, `heads_out`, `hidden` and `pooled`) count: a program that leaves them out, or rounds other values in their place, can miss the bound.
Values may be sent and summed in bfloat16 or wider, within the bound.
A program may use at most 128 MiB of HBM per device.

```python
import math
import jax
import jax.numpy as jnp
from jax import lax

D = 768
HEADS = 12
HD = 64
FF = 3072
PD = 768
NP = 196
REG = 4
NCLS = 1000
IMG_PATCH = 1
STEP = 10
S = 200
IMAGES = 32
P_TOTAL = 8592384
N_HEADS = 2


def touch_ends(drawn, key, low, top_value):
    longest = drawn.shape.index(max(drawn.shape))
    spots = []
    for shift in (0, 1):
        where = [jax.random.randint(jax.random.fold_in(key, axis), (), 0, length) for axis, length in enumerate(drawn.shape)]
        where[longest] = (where[longest] + shift) % drawn.shape[longest]
        spots.append(tuple(where))
    return drawn.at[spots[0]].set(low).at[spots[1]].set(top_value)


def levels(key, dims, shards, smallest, largest):
    factor_of = 1.0
    for position, shards_of in shards:
        heights = jax.random.uniform(jax.random.fold_in(jax.random.fold_in(key, 6), position), (shards_of,), jnp.float32, smallest / len(shards), largest / len(shards))
        factor_of = factor_of * jnp.repeat(jnp.exp(heights), dims[position] // shards_of).reshape((-1,) + (1,) * (len(dims) - 1 - position))
    return factor_of


def noise(own_key, shape, deviation, bound, split=(), dtype=jnp.bfloat16):
    loudness = levels(own_key, shape, split, -0.22, 0.18) if split else 1.0
    entries = jax.random.normal(own_key, shape, jnp.float32) * deviation * loudness
    return jnp.minimum(jnp.maximum(entries, -bound), bound).astype(dtype)


def setup_inputs(seed: int = 0) -> dict:
    key_of = jax.random.split(jax.random.key(seed), 27)
    patches = noise(key_of[0], (IMAGES, NP, PD), 1.0, 6.0, ((0, 32),))
    labels = touch_ends(jax.random.randint(key_of[1], (IMAGES,), 0, NCLS), jax.random.fold_in(key_of[1], 1), 0, NCLS - 1).astype(jnp.int32)
    w_patch = noise(key_of[2], (PD, D), PD ** -0.5, 0.21875, ((1, 32),), jnp.float32)
    table = noise(key_of[3], (S, D), 0.5, 3.0, ((1, 32),), jnp.float32)
    gains = jnp.clip(1.0 + 0.1 * jax.random.normal(key_of[4], (4, D), jnp.float32), 0.5, 1.5)
    w_head = noise(key_of[5], (D, NCLS), (15.0 * D ** -0.5), 6.0, ((0, 32),), jnp.float32)
    w_qkv = noise(key_of[6], (D, 3, D), D ** -0.5, 0.21875, ((0, 16), (2, 2)), jnp.float32)
    w_out = noise(key_of[7], (D, D), (D // 64) ** -0.5, 1.75, ((0, 8), (1, 4)), jnp.float32)
    w_up = noise(key_of[8], (D, FF), D ** -0.5, 0.21875, ((0, 4), (1, 8)), jnp.float32)
    w_down = noise(key_of[9], (FF, D), FF ** -0.5, 0.109375, ((0, 8), (1, 4)), jnp.float32)
    first_patch = noise(key_of[10], (PD, D), (1.1e-4 * P_TOTAL ** -0.5), 2.384185791015625e-07, ((1, 32),), jnp.float32)
    first_table = noise(key_of[11], (S, D), (1.1e-4 * P_TOTAL ** -0.5), 2.384185791015625e-07, ((1, 32),), jnp.float32)
    first_gains = noise(key_of[12], (4, D), (3.3e-4 * P_TOTAL ** -0.5), 7.152557373046875e-07, ((1, 32),), jnp.float32)
    first_head = noise(key_of[13], (D, NCLS), (1.1e-4 * P_TOTAL ** -0.5), 2.384185791015625e-07, ((0, 32),), jnp.float32)
    first_qkv = noise(key_of[14], (D, 3, D), (1.1e-4 * P_TOTAL ** -0.5), 2.384185791015625e-07, ((0, 16), (2, 2)), jnp.float32)
    first_out = noise(key_of[15], (D, D), (1.1e-4 * P_TOTAL ** -0.5), 2.384185791015625e-07, ((0, 8), (1, 4)), jnp.float32)
    first_up = noise(key_of[16], (D, FF), (1.1e-4 * P_TOTAL ** -0.5), 2.384185791015625e-07, ((0, 4), (1, 8)), jnp.float32)
    first_down = noise(key_of[17], (FF, D), (1.1e-4 * P_TOTAL ** -0.5), 2.384185791015625e-07, ((0, 8), (1, 4)), jnp.float32)
    second_patch = jnp.clip(jnp.exp(math.log(4.655285666571346e-16) - 1.3862944 * jax.random.uniform(key_of[18], (PD, D), jnp.float32) ** levels(key_of[18], (PD, D), ((1, 32),), -0.2, 0.2)), 1.1638214166428365e-16, 4.655285666571346e-16)
    second_table = jnp.clip(jnp.exp(math.log(5.819107083214183e-17) - 1.3862944 * jax.random.uniform(key_of[19], (S, D), jnp.float32) ** levels(key_of[19], (S, D), ((1, 32),), -0.2, 0.2)), 1.4547767708035457e-17, 5.819107083214183e-17)
    second_gains = jnp.clip(jnp.exp(math.log(4.189756994035093e-15) - 1.3862944 * jax.random.uniform(key_of[20], (4, D), jnp.float32) ** levels(key_of[20], (4, D), ((1, 32),), -0.2, 0.2)), 1.0474392485087733e-15, 4.189756994035093e-15)
    second_head = jnp.clip(jnp.exp(math.log(4.655285666571346e-16) - 1.3862944 * jax.random.uniform(key_of[21], (D, NCLS), jnp.float32) ** levels(key_of[21], (D, NCLS), ((0, 32),), -0.2, 0.2)), 1.1638214166428365e-16, 4.655285666571346e-16)
    second_qkv = jnp.clip(jnp.exp(math.log(4.655285666571346e-16) - 1.3862944 * jax.random.uniform(key_of[22], (D, 3, D), jnp.float32) ** levels(key_of[22], (D, 3, D), ((0, 16), (2, 2)), -0.2, 0.2)), 1.1638214166428365e-16, 4.655285666571346e-16)
    second_out = jnp.clip(jnp.exp(math.log(4.655285666571346e-16) - 1.3862944 * jax.random.uniform(key_of[23], (D, D), jnp.float32) ** levels(key_of[23], (D, D), ((0, 8), (1, 4)), -0.2, 0.2)), 1.1638214166428365e-16, 4.655285666571346e-16)
    second_up = jnp.clip(jnp.exp(math.log(2.3276427340239996e-17) - 1.3862944 * jax.random.uniform(key_of[24], (D, FF), jnp.float32) ** levels(key_of[24], (D, FF), ((0, 4), (1, 8)), -0.2, 0.2)), 5.819106835059999e-18, 2.3276427340239996e-17)
    second_down = jnp.clip(jnp.exp(math.log(4.655285666571346e-16) - 1.3862944 * jax.random.uniform(key_of[25], (FF, D), jnp.float32) ** levels(key_of[25], (FF, D), ((0, 8), (1, 4)), -0.2, 0.2)), 1.1638214166428365e-16, 4.655285666571346e-16)
    return dict(patches=patches, labels=labels, w_patch=w_patch, table=table, gains=gains, w_head=w_head, w_qkv=w_qkv, w_out=w_out, w_up=w_up, w_down=w_down, first_patch=first_patch, first_table=first_table, first_gains=first_gains, first_head=first_head, first_qkv=first_qkv, first_out=first_out, first_up=first_up, first_down=first_down, second_patch=second_patch, second_table=second_table, second_gains=second_gains, second_head=second_head, second_qkv=second_qkv, second_out=second_out, second_up=second_up, second_down=second_down)


@jax.custom_vjp
def low(v):
    return lax.optimization_barrier(v.astype(jnp.bfloat16)).astype(jnp.float32)

@jax.custom_vjp
def low_back(v):
    return v

def low_keep(v):
    return (low(v), None)

def low_pass(kept, grad):
    return (grad,)

def back_keep(v):
    return (v, None)

def back_low(kept, grad):
    return (low(grad),)
low.defvjp(low_keep, low_pass)
low_back.defvjp(back_keep, back_low)
beta_one = 0.9
beta_two = 0.999
adam_eps = 1e-08
decay_rate = 0.01
learn_rate = 0.5
clip_at = 0.001
norm_eps = 1e-06
highest = lax.Precision.HIGHEST

def layer_norm(values):
    center = values - lax.optimization_barrier(jnp.mean(values, axis=-1, keepdims=True))
    return center * lax.rsqrt(lax.optimization_barrier(jnp.mean(center * center, axis=-1, keepdims=True)) + norm_eps)

def attend(normed, qkv_weight, query_gain, key_gain):
    count = normed.shape[0]
    mixed = jnp.einsum('bsd,dcf->bscf', normed, qkv_weight, precision=highest)
    mixed = low_back(mixed).reshape(count, S, 3, HEADS, HD)
    queries = low(layer_norm(mixed[:, :, 0]) * query_gain)
    keys = low(layer_norm(mixed[:, :, 1]) * key_gain)
    values = low(mixed[:, :, 2])
    scores = jnp.einsum('bqhd,bkhd->bhqk', queries, keys, precision=highest) * HD ** (-0.5)
    scores = low_back(scores)
    probs = jax.nn.softmax(scores, axis=-1)
    heads_out = jnp.einsum('bhqk,bkhd->bqhd', low(probs), values, precision=highest)
    return low(low_back(heads_out)).reshape(count, S, D)

def forward(weights, patches, labels):
    patch_w, table, gains, head_w, qkv_w, out_w, up_w, down_w = [low(weight) for weight in weights]
    images = patches.shape[0]
    embedded = jnp.einsum('inp,pd->ind', patches, patch_w, precision=highest)
    stream_in = jnp.concatenate([embedded + table[:NP], jnp.broadcast_to(table[NP:], (images, REG, D))], axis=1)
    stream_in = low(stream_in)
    normed = low(layer_norm(stream_in) * gains[0])
    block = IMG_PATCH * N_HEADS
    shaped = normed.reshape(images // block, block, S, D)
    query_gain = gains[2].reshape(HEADS, HD)
    key_gain = gains[3].reshape(HEADS, HD)
    heads_out = lax.map(jax.checkpoint(lambda piece: attend(piece, qkv_w, query_gain, key_gain)), shaped)
    heads_out = heads_out.reshape(images * S, D)
    flat = normed.reshape(images * S, D)
    attn = jnp.dot(heads_out, out_w, precision=highest)
    upper = low_back(jnp.dot(flat, up_w, precision=highest))
    hidden = low(jax.nn.gelu(upper))
    branch = low_back(attn + jnp.dot(hidden, down_w, precision=highest))
    stream_out = stream_in.reshape(images * S, D) + branch
    final = (layer_norm(stream_out) * gains[1]).reshape(images, S, D)
    pooled = low(lax.optimization_barrier(jnp.mean(final[:, :NP], axis=1)))
    logits = jnp.dot(pooled, head_w, precision=highest)
    picked = jnp.take_along_axis(logits, labels[:, None], axis=1)[:, 0]
    terms = jax.nn.logsumexp(logits, axis=-1) - picked
    return (jnp.mean(terms), jnp.sum(terms))

def reference(patches, labels, w_patch, table, gains, w_head, w_qkv, w_out, w_up, w_down, first_patch, first_table, first_gains, first_head, first_qkv, first_out, first_up, first_down, second_patch, second_table, second_gains, second_head, second_qkv, second_out, second_up, second_down):
    weights = [w_patch, table, gains, w_head, w_qkv, w_out, w_up, w_down]
    firsts = [first_patch, first_table, first_gains, first_head, first_qkv, first_out, first_up, first_down]
    seconds = [second_patch, second_table, second_gains, second_head, second_qkv, second_out, second_up, second_down]
    patches_f = patches.astype(jnp.float32)

    def objective(*params):
        return forward(list(params), patches_f, labels)
    loss_mean, back_fn, loss_sum = jax.vjp(objective, *weights, has_aux=True)
    grads = back_fn(jnp.float32(1.0))
    grad_norm = jnp.sqrt(sum((jnp.sum(grad * grad) for grad in grads)))
    clip = jnp.minimum(1.0, clip_at / grad_norm)
    new_firsts, new_seconds, new_weights = ([], [], [])
    for weight, first, second, grad in zip(weights, firsts, seconds, grads):
        clipped = grad * clip
        first_new = beta_one * first + (1.0 - beta_one) * clipped
        second_new = beta_two * second + (1.0 - beta_two) * clipped * clipped
        update = first_new / (1.0 - beta_one ** STEP) / (jnp.sqrt(second_new / (1.0 - beta_two ** STEP)) + adam_eps)
        update = update + decay_rate * weight
        ratio = jnp.sqrt(jnp.sum(weight * weight)) / jnp.sqrt(jnp.sum(update * update))
        new_firsts.append(first_new)
        new_seconds.append(second_new)
        new_weights.append(weight - learn_rate * ratio * update)
    return (loss_sum, grad_norm, new_firsts[0], new_firsts[1], new_firsts[2], new_firsts[3], new_firsts[4], new_firsts[5], new_firsts[6], new_firsts[7], new_seconds[0], new_seconds[1], new_seconds[2], new_seconds[3], new_seconds[4], new_seconds[5], new_seconds[6], new_seconds[7], new_weights[0], new_weights[1], new_weights[2], new_weights[3], new_weights[4], new_weights[5], new_weights[6], new_weights[7])
```

```python
import functools
import types

import jax
import jax.numpy as jnp
from jax import lax
from jax.experimental import pallas as pl
from jax.experimental.pallas import tpu as pltpu
from jax.sharding import PartitionSpec as P

HD = 64
PD = 768
STEP = 10
MESH = pl.DeviceIdType.MESH
ALL = ("dp", "heads", "hidden")
DATA = ("dp", "hidden")
MODEL = ("heads", "hidden")


beta_one = 0.9
beta_two = 0.999
adam_eps = 1e-08
decay_rate = 0.01
learn_rate = 0.5
clip_at = 0.001
norm_eps = 1e-06
highest = lax.Precision.HIGHEST


def layer_norm(values):
    center = values - jnp.mean(values, axis=-1, keepdims=True)
    return center * lax.rsqrt(jnp.mean(center * center, axis=-1, keepdims=True) + norm_eps)


def head_loss(stream_out, targets, final_gain, head_weight, npatch, total_images):
    normed_out, norm_back = jax.vjp(layer_norm, stream_out)
    final = normed_out * final_gain
    pooled_b = jnp.mean(final[:, :npatch], axis=1).astype(jnp.bfloat16)
    logits = jnp.dot(pooled_b, head_weight, preferred_element_type=jnp.float32)
    log_total = jax.nn.logsumexp(logits, axis=-1)
    onehot = (targets[:, None] == lax.broadcasted_iota(jnp.int32, logits.shape, 1)).astype(
        jnp.float32
    )
    terms = log_total - jnp.sum(logits * onehot, axis=-1)
    d_logits = (jnp.exp(logits - log_total[:, None]) - onehot) / total_images
    d_pooled = jnp.dot(d_logits, head_weight.astype(jnp.float32).T, precision=highest)
    count, seq_len, width = stream_out.shape
    spread = jnp.broadcast_to(d_pooled[:, None, :] / npatch, (count, npatch, width))
    d_final = jnp.concatenate(
        [spread, jnp.zeros((count, seq_len - npatch, width), jnp.float32)], axis=1
    )
    d_stream = norm_back(d_final * final_gain)[0]
    d_gain_rows = jnp.sum(d_final * normed_out, axis=1)
    return (terms, pooled_b, d_logits, d_stream, d_gain_rows)


def per_device(
    patches,
    labels,
    w_patch,
    table,
    gains,
    w_head,
    w_qkv,
    w_out,
    w_up,
    w_down,
    first_patch,
    first_table,
    first_gains,
    first_head,
    first_qkv,
    first_out,
    first_up,
    first_down,
    second_patch,
    second_table,
    second_gains,
    second_head,
    second_qkv,
    second_out,
    second_up,
    second_down,
):
    masters = [w_patch, table, gains, w_head, w_qkv, w_out, w_up, w_down]
    firsts = [
        first_patch,
        first_table,
        first_gains,
        first_head,
        first_qkv,
        first_out,
        first_up,
        first_down,
    ]
    seconds = [
        second_patch,
        second_table,
        second_gains,
        second_head,
        second_qkv,
        second_out,
        second_up,
        second_down,
    ]
    bfloat = jnp.bfloat16
    single = jnp.float32
    patch_b, table_b, gains_b, head_b = (
        lax.all_gather(w_patch.astype(bfloat), ALL, axis=1, tiled=True),
        lax.all_gather(table.astype(bfloat), ALL, axis=1, tiled=True),
        lax.all_gather(gains.astype(bfloat), ALL, axis=1, tiled=True),
        lax.all_gather(w_head.astype(bfloat), ALL, axis=0, tiled=True),
    )
    qkv_b = lax.all_gather(w_qkv.astype(bfloat), DATA, axis=0, tiled=True)
    out_b, up_b, down_b = (
        lax.all_gather(w_out.astype(bfloat), "dp", axis=1, tiled=True),
        lax.all_gather(w_up.astype(bfloat), "dp", axis=0, tiled=True),
        lax.all_gather(w_down.astype(bfloat), "dp", axis=1, tiled=True),
    )
    gain_vals = gains_b.astype(single)
    table_vals = table_b.astype(single)
    n_hidden = lax.axis_size("hidden")
    n_own = patches.shape[0]
    npatch = patches.shape[1]
    seq_len = table_b.shape[0]
    width = patch_b.shape[1]
    group_width = qkv_b.shape[2]
    group_heads = group_width // HD
    own_index = lax.axis_index("heads") * n_hidden + lax.axis_index("hidden")
    total_images = labels.shape[0] * lax.axis_size("dp")
    embedded = jnp.dot(patches.reshape(n_own * npatch, PD), patch_b, preferred_element_type=single)
    embedded = embedded.reshape(n_own, npatch, width) + table_vals[:npatch]
    registers = jnp.broadcast_to(table_vals[npatch:], (n_own, seq_len - npatch, width))
    stream_own = jnp.concatenate([embedded, registers], axis=1).astype(bfloat)
    stream_in = lax.all_gather(stream_own, MODEL, axis=0, tiled=True)
    n_img = stream_in.shape[0]
    row_count = n_img * seq_len
    stream_flat = stream_in.astype(single).reshape(row_count, width)
    normed_b = (layer_norm(stream_flat) * gain_vals[0]).astype(bfloat)
    n_att = n_img // n_hidden
    att_start = lax.axis_index("hidden") * n_att
    normed_att = lax.dynamic_slice_in_dim(
        normed_b.reshape(n_img, seq_len, width), att_start, n_att, 0
    )
    query_gain = lax.dynamic_slice_in_dim(
        gain_vals[2], lax.axis_index("heads") * group_width, group_width, 0
    ).reshape(group_heads, HD)
    key_gain = lax.dynamic_slice_in_dim(
        gain_vals[3], lax.axis_index("heads") * group_width, group_width, 0
    ).reshape(group_heads, HD)
    mixed = jnp.einsum("bsd,dcf->bscf", normed_att, qkv_b, preferred_element_type=single)
    mixed = mixed.reshape(n_att, seq_len, 3, group_heads, HD)
    query_norm, query_back = jax.vjp(layer_norm, mixed[:, :, 0])
    key_norm, key_back = jax.vjp(layer_norm, mixed[:, :, 1])
    queries = (query_norm * query_gain).astype(bfloat)
    keys = (key_norm * key_gain).astype(bfloat)
    values = mixed[:, :, 2].astype(bfloat)
    scale = HD ** (-0.5)
    scores = jnp.einsum("bqhd,bkhd->bhqk", queries, keys, preferred_element_type=single) * scale
    probs = jax.nn.softmax(scores, axis=-1)
    probs_b = probs.astype(bfloat)
    heads_out = jnp.einsum("bhqk,bkhd->bqhd", probs_b, values, preferred_element_type=single)
    heads_out = heads_out.astype(bfloat).reshape(n_att * seq_len, group_width)
    columns = lax.all_to_all(heads_out, "hidden", split_axis=1, concat_axis=0, tiled=True)
    attn_part = jnp.dot(columns, out_b, preferred_element_type=single)
    upper = jnp.dot(normed_b, up_b, preferred_element_type=single)
    activated, gelu_back = jax.vjp(jax.nn.gelu, upper)
    activated_b = activated.astype(bfloat)
    partial_sum = attn_part + jnp.dot(activated_b, down_b, preferred_element_type=single)
    total = lax.psum(partial_sum, MODEL)
    stream_out = (stream_flat + total).reshape(n_img, seq_len, width)
    terms, pooled_b, d_logits, d_stream, d_gain_rows = head_loss(
        stream_out, labels, gain_vals[1], head_b, npatch, total_images
    )
    loss_terms = lax.dynamic_slice_in_dim(terms, own_index * n_own, n_own, 0)
    pooled_own = lax.dynamic_slice_in_dim(pooled_b, own_index * n_own, n_own, 0)
    logits_own = lax.dynamic_slice_in_dim(d_logits, own_index * n_own, n_own, 0)
    d_head = jnp.dot(pooled_own.astype(single).T, logits_own, precision=highest)
    d_final_gain = jnp.sum(
        lax.dynamic_slice_in_dim(d_gain_rows, own_index * n_own, n_own, 0), axis=0
    )
    d_stream_own = lax.dynamic_slice_in_dim(d_stream, own_index * n_own, n_own, 0)
    d_branch = d_stream.reshape(row_count, width).astype(bfloat)
    d_activated = jnp.dot(d_branch, down_b.T, preferred_element_type=single)
    d_upper = gelu_back(d_activated)[0].astype(bfloat)
    d_down = jnp.dot(activated_b.T, d_branch, preferred_element_type=single)
    d_up = jnp.dot(normed_b.T, d_upper, preferred_element_type=single)
    d_normed = jnp.dot(d_upper, up_b.T, preferred_element_type=single)
    d_out = jnp.dot(columns.T, d_branch, preferred_element_type=single)
    d_columns = jnp.dot(d_branch, out_b.T, preferred_element_type=single).astype(bfloat)
    d_heads = lax.all_to_all(d_columns, "hidden", split_axis=0, concat_axis=1, tiled=True).reshape(
        n_att, seq_len, group_heads, HD
    )
    d_probs = jnp.einsum("bqhd,bkhd->bhqk", d_heads, values, preferred_element_type=single)
    d_values = jnp.einsum("bhqk,bqhd->bkhd", probs_b, d_heads, preferred_element_type=single)
    d_scores = (probs * (d_probs - jnp.sum(probs * d_probs, axis=-1, keepdims=True))).astype(bfloat)
    d_query_norm = (
        jnp.einsum("bhqk,bkhd->bqhd", d_scores, keys, preferred_element_type=single) * scale
    )
    d_key_norm = (
        jnp.einsum("bhqk,bqhd->bkhd", d_scores, queries, preferred_element_type=single) * scale
    )
    d_queries = query_back(d_query_norm * query_gain)[0]
    d_keys = key_back(d_key_norm * key_gain)[0]
    d_query_gain = jnp.sum(d_query_norm * query_norm, axis=(0, 1)).reshape(group_width)
    d_key_gain = jnp.sum(d_key_norm * key_norm, axis=(0, 1)).reshape(group_width)
    d_mixed = (
        jnp.stack([d_queries, d_keys, d_values], axis=2)
        .astype(bfloat)
        .reshape(n_att, seq_len, 3, group_width)
    )
    d_qkv = jnp.einsum("bsd,bscf->dcf", normed_att, d_mixed, preferred_element_type=single)
    d_att_in = jnp.einsum("bscf,dcf->bsd", d_mixed, qkv_b, preferred_element_type=single)
    d_normed = d_normed.reshape(n_img, seq_len, width)
    d_normed = lax.dynamic_update_slice_in_dim(
        d_normed, lax.dynamic_slice_in_dim(d_normed, att_start, n_att, 0) + d_att_in, att_start, 0
    )
    d_normed_own = lax.psum_scatter(
        d_normed.reshape(row_count, width).astype(jnp.bfloat16),
        MODEL,
        scatter_dimension=0,
        tiled=True,
    ).astype(jnp.float32)
    d_normed_own = d_normed_own.reshape(n_own, seq_len, width)
    normed_own, block_back = jax.vjp(layer_norm, stream_own.astype(single))
    d_stream_in = d_stream_own + block_back(d_normed_own * gain_vals[0])[0]
    d_block_gain = jnp.sum(d_normed_own * normed_own, axis=(0, 1))
    d_patch = jnp.dot(
        patches.reshape(n_own * npatch, PD).astype(single).T,
        d_stream_in[:, :npatch].reshape(n_own * npatch, width),
        precision=highest,
    )
    d_table = jnp.sum(d_stream_in, axis=0)
    zero_row = jnp.zeros((width,), single)
    gain_offset = lax.axis_index("heads") * group_width
    d_gains = jnp.stack(
        [
            d_block_gain,
            d_final_gain,
            lax.dynamic_update_slice_in_dim(zero_row, d_query_gain, gain_offset, 0),
            lax.dynamic_update_slice_in_dim(zero_row, d_key_gain, gain_offset, 0),
        ]
    )
    grad_patch, grad_table, grad_gains, grad_head = (
        lax.psum_scatter(d_patch, ALL, scatter_dimension=1, tiled=True),
        lax.psum_scatter(d_table, ALL, scatter_dimension=1, tiled=True),
        lax.psum_scatter(d_gains, ALL, scatter_dimension=1, tiled=True),
        lax.psum_scatter(d_head, ALL, scatter_dimension=0, tiled=True),
    )
    grad_qkv = lax.psum_scatter(d_qkv, DATA, scatter_dimension=0, tiled=True)
    grad_out, grad_up, grad_down = (
        lax.psum_scatter(d_out.astype(jnp.bfloat16), "dp", scatter_dimension=1, tiled=True).astype(
            jnp.float32
        ),
        lax.psum_scatter(d_up.astype(jnp.bfloat16), "dp", scatter_dimension=0, tiled=True).astype(
            jnp.float32
        ),
        lax.psum_scatter(d_down.astype(jnp.bfloat16), "dp", scatter_dimension=1, tiled=True).astype(
            jnp.float32
        ),
    )
    grads = [grad_patch, grad_table, grad_gains, grad_head, grad_qkv, grad_out, grad_up, grad_down]
    grad_squares = jnp.stack([jnp.sum(grad * grad) for grad in grads])
    weight_squares = jnp.stack([jnp.sum(master * master) for master in masters])
    grad_squares, weight_squares, loss_sum = lax.psum(
        (grad_squares, weight_squares, jnp.sum(loss_terms)), ALL
    )
    grad_norm = jnp.sqrt(jnp.sum(grad_squares))
    clip = jnp.minimum(1.0, clip_at / grad_norm)
    new_firsts, new_seconds, updates = ([], [], [])
    for master, first, second, grad in zip(masters, firsts, seconds, grads):
        clipped = grad * clip
        first_new = beta_one * first + (1.0 - beta_one) * clipped
        second_new = beta_two * second + (1.0 - beta_two) * clipped * clipped
        update = (
            first_new
            / (1.0 - beta_one**STEP)
            / (jnp.sqrt(second_new / (1.0 - beta_two**STEP)) + adam_eps)
        )
        updates.append(update + decay_rate * master)
        new_firsts.append(first_new)
        new_seconds.append(second_new)
    update_squares = lax.psum(
        jnp.stack([jnp.sum(update * update) for update in updates]), ALL
    )
    ratios = jnp.sqrt(weight_squares) / jnp.sqrt(update_squares)
    new_weights = [
        master - learn_rate * ratios[number] * update
        for number, (master, update) in enumerate(zip(masters, updates))
    ]
    return (
        loss_sum,
        grad_norm,
        new_firsts[0],
        new_firsts[1],
        new_firsts[2],
        new_firsts[3],
        new_firsts[4],
        new_firsts[5],
        new_firsts[6],
        new_firsts[7],
        new_seconds[0],
        new_seconds[1],
        new_seconds[2],
        new_seconds[3],
        new_seconds[4],
        new_seconds[5],
        new_seconds[6],
        new_seconds[7],
        new_weights[0],
        new_weights[1],
        new_weights[2],
        new_weights[3],
        new_weights[4],
        new_weights[5],
        new_weights[6],
        new_weights[7],
    )


def dot(a, b):
    return jnp.dot(a, b, preferred_element_type=jnp.float32)


def dot_nt(a, b, precision=None):
    return lax.dot_general(
        a, b, (((1,), (1,)), ((), ())), precision=precision, preferred_element_type=jnp.float32
    )


def dot_tn(a, b, precision=None):
    return lax.dot_general(
        a, b, (((0,), (0,)), ((), ())), precision=precision, preferred_element_type=jnp.float32
    )


def norm_parts(values):
    center = values - jnp.mean(values, axis=-1, keepdims=True)
    scale = lax.rsqrt(jnp.mean(center * center, axis=-1, keepdims=True) + norm_eps)
    return center * scale, scale


def norm_back(normed, scale, grad):
    inner = jnp.mean(grad * normed, axis=-1, keepdims=True)
    return scale * (grad - jnp.mean(grad, axis=-1, keepdims=True) - normed * inner)


gelu_c = 0.7978845608028654


def gelu_tanh(u):
    return jnp.tanh(gelu_c * (u + 0.044715 * (u * u * u)))


def iota(shape, axis):
    return lax.broadcasted_iota(jnp.int32, shape, axis)


def one_update(master, first, second, grad, clip):
    clipped = grad * clip
    first_new = beta_one * first + (1.0 - beta_one) * clipped
    second_new = beta_two * second + (1.0 - beta_two) * clipped * clipped
    update = (
        first_new
        / (1.0 - beta_one**STEP)
        / (jnp.sqrt(second_new / (1.0 - beta_two**STEP)) + adam_eps)
    )
    return first_new, second_new, update + decay_rate * master


def square_sum(values):
    return jnp.sum(values * values, axis=(0, 1), keepdims=True)


KINDS = ("patch", "table", "gains", "head", "qkv", "out", "up", "down")
ROWS = 208
N_HID = 4


def step_kernel(sizes, names, *refs):
    npatch, seq_len, classes, total_images = sizes
    r = types.SimpleNamespace(**dict(zip(names, refs)))
    bfloat, single = jnp.bfloat16, jnp.float32
    dp, h, z = (lax.axis_index(a) for a in ALL)
    core, y = lax.rem(dp, 2), dp // 2
    y_dp, core_dp = (1 - y) * 2 + core, y * 2 + (1 - core)
    x_dev, y_dev, core_dev = (dp, 1 - h, z), (y_dp, h, z), (core_dp, h, z)
    z_up = [lax.rem(z + k, N_HID) for k in range(N_HID)]
    z_down = [lax.rem(z + N_HID - k, N_HID) for k in range(N_HID)]
    z_dev = [(dp, h, z_up[k]) for k in range(N_HID)]
    group = []
    for a in (0, 1):
        for b in (0, 1):
            for c in (0, 1):
                if a + b + c:
                    gh = 1 - h if a else h
                    gy = 1 - y if b else y
                    gc = 1 - core if c else core
                    group.append((gh, gy * 2 + gc))
    group_dev = [(gd, gh, z) for gh, gd in group]

    barrier = pltpu.get_barrier_semaphore()
    for device in z_dev[1:] + group_dev:
        pl.semaphore_signal(barrier, inc=1, device_id=device, device_id_type=MESH)

    ssem, rsem = r.ssem, r.rsem
    count = [0]
    sends = []

    def send(source, target, device):
        number = count[0]
        count[0] += 1
        copy = pltpu.make_async_remote_copy(
            src_ref=source,
            dst_ref=target,
            send_sem=ssem.at[number],
            recv_sem=rsem.at[number],
            device_id=device,
            device_id_type=MESH,
        )
        copy.start()
        sends.append(copy)
        return number

    def arrive(target, number, device):
        pltpu.make_async_remote_copy(
            src_ref=target,
            dst_ref=target,
            send_sem=ssem.at[number],
            recv_sem=rsem.at[number],
            device_id=device,
            device_id_type=MESH,
        ).wait_recv()

    gext, gqkv, gout, gup, gdn, ghd = r.gext, r.gqkv, r.gout, r.gup, r.gdn, r.ghd
    x0, x1 = r.x0, r.x1
    x1[0:24, :] = jnp.zeros((24, 512), single)
    x1[0:24, 256 : 256 + seq_len] = r.w_table[...]
    pick = (iota((4, 256), 1) == iota((4, 256), 0) + seq_len).astype(bfloat)
    table_part = x1[0:24, 256:512] + dot_tn(r.w_gains[...].astype(bfloat), pick)
    wp = r.w_patch[...]
    gext[dp, z] = jnp.concatenate(
        [wp[:, 0:512], jnp.concatenate([wp[:, 512:768], table_part], axis=1)], axis=0
    ).astype(bfloat)
    gqkv[:, z // 2, dp, lax.rem(z, 2)] = r.w_qkv[...].astype(bfloat)
    gup[z, :, dp] = r.w_up[...].astype(bfloat).reshape(2, 96, 384)
    gdn[z, :, dp] = r.w_down[...].astype(bfloat).reshape(2, 96, 384)
    gout[dp, z] = jnp.zeros((96, 256), bfloat)
    gout[dp, z, :, 0:192] = r.w_out[...].astype(bfloat)
    x0[0:24, :] = r.w_head[:, 0:512]
    x1[0:24, :] = jnp.zeros((24, 512), single)
    x1[0:24, 0 : classes - 512] = r.w_head[:, 512:classes]
    ghd[h, dp, z] = jnp.concatenate([x0[0:24, :], x1[0:24, :]], axis=0).astype(bfloat)
    px = r.px
    row, col = iota((ROWS, 256), 0), iota((ROWS, 256), 1)
    spot = jnp.where((row == col) & (row < seq_len), 1.0, 0.0).astype(bfloat)
    px[0, :, 768:1024] = spot
    px[1, :, 768:1024] = spot
    px[0, :, 0:768] = jnp.zeros((ROWS, 768), bfloat)
    px[0, 0:npatch, 0:768] = r.patches[0]

    pl.semaphore_wait(barrier, len(z_dev) - 1 + len(group_dev))

    def at_ext(d, w):
        return gext.at[d, w]

    def at_qkv(d, w):
        return gqkv.at[:, w // 2, d, lax.rem(w, 2)]

    def at_out(d, w):
        return gout.at[d, w]

    def at_up(half):
        return lambda d, w: gup.at[w, half, d]

    def at_dn(half):
        return lambda d, w: gdn.at[w, half, d]

    def at_hd(d, w):
        return ghd.at[h, d, w]

    slot = {
        "ext": at_ext,
        "qkv": at_qkv,
        "out": at_out,
        "up0": at_up(0),
        "up1": at_up(1),
        "dn0": at_dn(0),
        "dn1": at_dn(1),
        "hd": at_hd,
    }
    lines = {
        "ext": lambda d: gext.at[d],
        "qkv": lambda d: gqkv.at[:, :, d],
        "out": lambda d: gout.at[d],
        "up0": lambda d: gup.at[:, 0, d],
        "up1": lambda d: gup.at[:, 1, d],
        "dn0": lambda d: gdn.at[:, 0, d],
        "dn1": lambda d: gdn.at[:, 1, d],
        "hd": lambda d: ghd.at[h, d],
    }
    tags = {}

    def first_send(name):
        at = slot[name]
        own = at(dp, z)
        for k in range(1, N_HID):
            tags[name, "z", k] = send(own, own, z_dev[k])
        tags[name, "y", 0] = send(own, own, y_dev)

    def pass_on(name):
        at = slot[name]
        for k in range(1, N_HID):
            theirs = at(dp, z_down[k])
            arrive(theirs, tags[name, "z", k], z_dev[k])
            tags[name, "y", k] = send(theirs, theirs, y_dev)
        if name != "hd":
            line = lines[name](dp)
            tags[name, "c", 0] = send(line, line, core_dev)

    def pass_core(name):
        at = slot[name]
        for k in range(N_HID):
            arrive(at(y_dp, z_down[k]), tags[name, "y", k], y_dev)
        line = lines[name](y_dp)
        if name != "hd":
            tags[name, "c", 1] = send(line, line, core_dev)
        else:
            own = lines[name](dp)
            tags[name, "x", 0] = send(own, own, x_dev)
            tags[name, "x", 1] = send(line, line, x_dev)

    def complete(name):
        far = (1 - y) * 2 + (1 - core)
        arrive(lines[name](core_dp), tags[name, "c", 0], core_dev)
        arrive(lines[name](far), tags[name, "c", 1], core_dev)

    def head_core():
        for i, d in enumerate((dp, y_dp)):
            arrive(ghd.at[1 - h, d], tags["hd", "x", i], x_dev)
        for i, d in enumerate((dp, y_dp)):
            block = ghd.at[:, d]
            tags["hd", "c", i] = send(block, block, core_dev)

    def head_complete():
        far = (1 - y) * 2 + (1 - core)
        for i, d in enumerate((core_dp, far)):
            arrive(ghd.at[:, d], tags["hd", "c", i], core_dev)

    first_send("ext")
    images = px.at[0, :, pl.ds(0, 768)]
    tag_px = send(images, px.at[1, :, pl.ds(0, 768)], x_dev)
    first_send("qkv")
    pass_on("ext")
    first_send("up0")
    pass_core("ext")
    complete("ext")

    for d in range(4):
        for w in range(N_HID):
            s = (d * N_HID + w) * 24
            block = gext[d, w].astype(single)
            x0[s : s + 24, :] = block[0:24]
            x1[s : s + 24, :] = block[24:48]
    x1b = x1[...].astype(bfloat)
    ga = r.ga
    rows_of = (iota((8, 512), 1) == iota((8, 512), 0) + (256 + seq_len)) & (iota((8, 512), 0) < 4)
    ga[h] = dot_nt(rows_of.astype(bfloat), x1b)
    tag_ga = send(ga.at[h], ga.at[h], x_dev)
    x0b = x0[...].astype(bfloat)
    st = r.st
    st[h, 0] = (dot_nt(px[0, :, 0:512], x0b) + dot_nt(px[0, :, 512:1024], x1b)).astype(bfloat)
    tag_st0 = send(st.at[h, 0], st.at[h, 1], x_dev)
    arrive(px.at[1, :, pl.ds(0, 768)], tag_px, x_dev)
    st[h, 1] = (dot_nt(px[1, :, 0:512], x0b) + dot_nt(px[1, :, 512:1024], x1b)).astype(bfloat)
    tag_st1 = send(st.at[h, 1], st.at[h, 0], x_dev)
    pass_on("qkv")
    first_send("up1")
    arrive(ga.at[1 - h], tag_ga, x_dev)
    arrive(st.at[1 - h, 1], tag_st0, x_dev)
    arrive(st.at[1 - h, 0], tag_st1, x_dev)

    def gain_row(i):
        return jnp.concatenate([ga[0, i : i + 1, :], ga[1, i : i + 1, :]], axis=1)

    def head_gain(i):
        pieces = []
        both = [ga[0, i : i + 1, :], ga[1, i : i + 1, :]]
        for d in range(4):
            pieces.extend(half[:, d * 96 : d * 96 + 96] for half in both)
        low = jnp.concatenate(pieces[0:4], axis=1)
        high = jnp.concatenate(pieces[4:8], axis=1)
        return jnp.where(h == 0, low, high)

    nb, nbt = r.nb, r.nbt
    block_gain = gain_row(0)
    for i in range(2):
        stream = jnp.concatenate([st[0, i], st[1, i]], axis=1).astype(single)
        nb[i * ROWS : (i + 1) * ROWS, :] = (norm_parts(stream)[0] * block_gain).astype(bfloat)
    pass_core("qkv")
    first_send("hd")
    pass_on("up0")
    first_send("out")
    complete("qkv")

    qn, kn, qr, kr = r.qn, r.kn, r.qr, r.kr
    q_ref, k_ref, v_ref = r.q, r.k, r.v
    q_gain, k_gain = head_gain(2), head_gain(3)
    for c, (keep, scales, out, gain) in enumerate(
        ((qn, qr, q_ref, q_gain), (kn, kr, k_ref, k_gain), (None, None, v_ref, None))
    ):
        mixed = dot(nb[...], gqkv[c].reshape(768, 384))
        for n in range(6):
            part = mixed[:, n * HD : (n + 1) * HD]
            if keep is not None:
                part, scale = norm_parts(part)
                keep[n] = part
                scales[n] = scale
                part = part * gain[:, n * HD : (n + 1) * HD]
            part = part.astype(bfloat)
            out[2 * n] = part[0:ROWS]
            out[2 * n + 1] = part[ROWS : 2 * ROWS]
        if c == 0:
            pass_on("up1")
            first_send("dn0")

    pr, ho = r.pr, r.ho
    dead = iota((ROWS, ROWS), 1) >= seq_len

    def attend(i, carry):
        scores = dot_nt(q_ref[i], k_ref[i]) * HD ** (-0.5)
        scores = jnp.where(dead, -1e30, scores)
        scores = scores - jnp.max(scores, axis=-1, keepdims=True)
        weights = jnp.exp(scores)
        probs = weights / jnp.sum(weights, axis=-1, keepdims=True)
        pr[i] = probs
        ho[i] = dot(probs.astype(bfloat), v_ref[i])
        return carry

    lax.fori_loop(0, 4, attend, 0)
    pass_core("up0")
    pass_on("hd")
    first_send("dn1")
    lax.fori_loop(4, 8, attend, 0)
    pass_on("out")
    lax.fori_loop(8, 12, attend, 0)
    pass_core("up1")
    pass_core("hd")
    hof = r.hof
    for i in range(2):
        joined = jnp.concatenate([ho[2 * n + i] for n in range(6)], axis=1)
        hof[i * ROWS : (i + 1) * ROWS, :] = joined.astype(bfloat)
    complete("up0")
    complete("up1")
    pass_on("dn0")

    us, hb, br = r.us, r.hb, r.br

    def rise(w, carry):
        upper = dot(nb[...], gup[w].reshape(768, 384))
        us[w] = upper
        hb[w] = (0.5 * upper * (1.0 + gelu_tanh(upper))).astype(bfloat)
        return carry

    lax.fori_loop(0, N_HID, rise, 0)
    head_core()
    pass_core("out")
    pass_on("dn1")
    complete("out")
    lefts, rights = [], []
    for d in range(4):
        part = dot(hof[...], gout[d].reshape(384, 256))
        lefts.append(part[:, 0:96])
        rights.append(part[:, 96:192])
    br[:, 0:384] = jnp.concatenate(lefts, axis=1)
    br[:, 384:768] = jnp.concatenate(rights, axis=1)
    nbt[...] = nb[...].T
    brs, brr = r.brs, r.brr
    tag_br = []
    for half in range(2):
        name = "dn%d" % half
        lanes = slice(half * 384, half * 384 + 384)
        pass_core(name)
        complete(name)

        def fall(w, carry):
            br[:, lanes] += dot_nt(hb[w], gdn[w, half].reshape(384, 384))
            return carry

        lax.fori_loop(0, N_HID, fall, 0)
        brs[half] = br[ROWS : 2 * ROWS, lanes].astype(bfloat)
        tag_br.append(send(brs.at[half], brr.at[half], x_dev))
    head_complete()
    x2, x3 = r.x2, r.x3
    for a in range(2):
        for d in range(4):
            for w in range(N_HID):
                s = (a * 16 + d * 4 + w) * 24
                block = ghd[a, d, w].astype(single)
                x2[s : s + 24, :] = block[0:24]
                x3[s : s + 24, :] = block[24:48]
    for half in range(2):
        arrive(brr.at[half], tag_br[half], x_dev)

    stream0 = jnp.concatenate([st[0, 0], st[1, 0]], axis=1).astype(single)
    theirs = jnp.concatenate([brr[0], brr[1]], axis=1).astype(single)
    out_n, out_scale = norm_parts(stream0 + (br[0:ROWS, :] + theirs))
    is_patch = iota((ROWS, 1), 0) < npatch
    final_gain = gain_row(1)
    n_sum = jnp.sum(jnp.where(is_patch, out_n, 0.0), axis=0, keepdims=True)
    pooled = n_sum * final_gain / npatch
    pooled_b = pooled.astype(bfloat)
    heads_b = [x2[...].astype(bfloat), x3[...].astype(bfloat)]
    pooled_8 = jnp.broadcast_to(pooled_b, (16, 768))
    logits = jnp.concatenate([dot(pooled_8, m)[0:1] for m in heads_b], axis=1)
    lane = iota((1, 1024), 1)
    logits = jnp.where(lane < classes, logits, -1e30)
    top = jnp.max(logits, axis=-1, keepdims=True)
    log_total = top + jnp.log(jnp.sum(jnp.exp(logits - top), axis=-1, keepdims=True))
    onehot = jnp.where(lane == r.labels[h * N_HID + z], 1.0, 0.0)
    term = log_total - jnp.sum(jnp.where(lane < classes, logits, 0.0) * onehot, axis=-1, keepdims=True)
    d_logits = (jnp.exp(logits - log_total) - onehot) / total_images
    hi = d_logits.astype(bfloat).astype(single)
    both = jnp.concatenate([hi, d_logits - hi, jnp.zeros((14, 1024), single)], axis=0).astype(bfloat)
    back = dot_nt(both[:, 0:512], heads_b[0]) + dot_nt(both[:, 512:1024], heads_b[1])
    d_pooled = (back[0:1] + back[1:2]) / npatch
    d_row = d_pooled * final_gain
    d_stream = jnp.where(is_patch, norm_back(out_n, out_scale, d_row), 0.0)
    ds, db, dbt = r.ds, r.db, r.dbt
    ds[...] = d_stream
    db[0] = d_stream.astype(bfloat)
    tag_db = send(db.at[0], db.at[1], x_dev)
    d_final_gain = d_pooled * n_sum
    al = r.al
    pooled_f = pooled_b.astype(single)
    al[h, dp, z] = jnp.concatenate(
        [d_logits[:, q * 256 : q * 256 + 256] for q in range(4)]
        + [pooled_f[:, q * 256 : q * 256 + 256] for q in range(3)]
        + [jnp.zeros((1, 256), single)],
        axis=0,
    )
    tag_al = [send(al.at[h, dp, z], al.at[h, dp, z], z_dev[k]) for k in range(1, N_HID)]
    dbt[:, 0:ROWS] = d_stream.T.astype(bfloat)
    arrive(db.at[1], tag_db, x_dev)
    dbt[:, ROWS : 2 * ROWS] = db[1].astype(single).T.astype(bfloat)
    db2 = db[...].reshape(2 * ROWS, 768)

    rff, f1, f2, ft, f3 = r.rff, r.f1, r.f2, r.ft, r.f3
    dn = br
    ff_tags = {}

    def ff_block(k):
        w = z_up[k]
        upper = us[w]
        t = gelu_tanh(upper)
        slope = 0.5 * (1.0 + t) + 0.5 * upper * (1.0 - t * t) * gelu_c * (
            1.0 + 3 * 0.044715 * (upper * upper)
        )
        d_hidden = dot(db2, gdn[w].reshape(768, 384))
        d_upper = (d_hidden * slope).astype(bfloat)
        rff[k, 1] = dot(dbt[...], hb[w]).astype(bfloat).reshape(2, 2, 2, 96, 384)
        rff[k, 0] = dot(nbt[...], d_upper).astype(bfloat).reshape(2, 2, 2, 96, 384)
        ff_tags[k, 0] = send(rff.at[k, :, :, :, 1 - core], f1.at[k], core_dev)
        part = dot_nt(d_upper, gup[w].reshape(768, 384))
        if k == 1:
            dn[...] = part
        else:
            dn[...] += part

    def ff_y(k):
        arrive(f1.at[k], ff_tags[k, 0], core_dev)
        f1[k] = f1[k] + rff[k, :, :, :, core]
        ff_tags[k, 1] = send(f1.at[k, :, :, 1 - y], f2.at[k], y_dev)

    def ff_z(k):
        arrive(f2.at[k], ff_tags[k, 1], y_dev)
        if k:
            ft[k - 1] = f1[k, :, :, y] + f2[k]
            ff_tags[k, 2] = send(ft.at[k - 1], f3.at[k - 1], z_dev[k])

    def ff_end():
        total = f1[0, :, :, y].astype(single) + f2[0].astype(single)
        for k in range(1, N_HID):
            arrive(f3.at[k - 1], ff_tags[k, 2], z_dev[k])
            total = total + f3[k - 1].astype(single)
        r.g_up[...] = total[0].reshape(192, 384)
        r.g_down[...] = total[1].reshape(192, 384)

    ff_block(1)
    ff_block(2)
    ff_y(1)
    for k in range(1, N_HID):
        arrive(al.at[h, dp, z_down[k]], tag_al[k - 1], z_dev[k])
    tag_ag = [send(al.at[h, dp], al.at[h, dp], device) for device in group_dev]
    ff_block(3)
    ff_y(2)
    ff_z(1)
    ff_block(0)
    ff_y(3)
    ff_z(2)

    rout, o1, o2, ot, o3 = r.rout, r.o1, r.o2, r.ot, r.o3
    pieces = [
        jnp.concatenate([db2[:, d * 96 : d * 96 + 96], db2[:, 384 + d * 96 : 384 + d * 96 + 96]], axis=1)
        for d in range(4)
    ]
    hot = hof[...].T
    d_heads = None
    for d in range(4):
        rout[:, d // 2, d % 2] = jnp.zeros((N_HID, 96, 256), bfloat)
        rout[:, d // 2, d % 2, :, 0:192] = dot(hot, pieces[d]).astype(bfloat).reshape(N_HID, 96, 192)
        part = dot_nt(pieces[d], gout[d].reshape(384, 256)[:, 0:192])
        d_heads = part if d_heads is None else d_heads + part
    tag_o1 = send(rout.at[:, :, 1 - core], o1, core_dev)
    dh = r.dh
    for n in range(6):
        part = d_heads[:, n * HD : (n + 1) * HD].astype(bfloat)
        dh[2 * n] = part[0:ROWS]
        dh[2 * n + 1] = part[ROWS : 2 * ROWS]
    ff_y(0)

    dq, dk, dv = ho, r.dk, r.dv

    def attend_back(i, carry):
        probs = pr[i]
        d_out = dh[i]
        d_probs = dot_nt(d_out, v_ref[i])
        dv[i] = dot_tn(probs.astype(bfloat), d_out)
        inner = jnp.sum(probs * d_probs, axis=-1, keepdims=True)
        d_scores = (probs * (d_probs - inner)).astype(bfloat)
        dq[i] = dot(d_scores, k_ref[i]) * HD ** (-0.5)
        dk[i] = dot_tn(d_scores, q_ref[i]) * HD ** (-0.5)
        return carry

    lax.fori_loop(0, 4, attend_back, 0)
    ff_z(3)
    arrive(o1, tag_o1, core_dev)
    o1[...] = o1[...] + rout[:, :, core]
    tag_o2 = send(o1.at[:, 1 - y], o2, y_dev)
    lax.fori_loop(4, 8, attend_back, 0)
    ff_z(0)
    lax.fori_loop(8, 12, attend_back, 0)

    rqkv, q1, q2, qt, q3 = r.rqkv, r.q1, r.q2, r.qt, r.q3
    gain_sums = []
    for c, (grads, normed, scales, gain) in enumerate(
        ((dq, qn, qr, q_gain), (dk, kn, kr, k_gain), (dv, None, None, None))
    ):
        parts, sums = [], []
        for n in range(6):
            grad = jnp.concatenate([grads[2 * n], grads[2 * n + 1]], axis=0)
            if normed is not None:
                sums.append(jnp.sum(grad * normed[n], axis=0, keepdims=True))
                grad = norm_back(normed[n], scales[n], grad * gain[:, n * HD : (n + 1) * HD])
            parts.append(grad)
        if sums:
            gain_sums.append(jnp.concatenate(sums, axis=1))
        d_mixed = jnp.concatenate(parts, axis=1).astype(bfloat)
        rqkv[c] = dot(nbt[...], d_mixed).astype(bfloat).reshape(2, 2, 2, 2, 48, 384)
        dn[...] += dot_nt(d_mixed, gqkv[c].reshape(768, 384))
    tag_q1 = send(rqkv.at[:, :, :, 1 - core], q1, core_dev)
    dns, dnr = r.dns, r.dnr
    dns[...] = dn[ROWS : 2 * ROWS, :].astype(bfloat)
    tag_dn = send(dns, dnr, x_dev)
    arrive(o2, tag_o2, y_dev)
    ot[...] = o1[:, y] + o2[...]
    tag_o3 = [send(ot.at[z_up[k]], o3.at[k - 1], z_dev[k]) for k in range(1, N_HID)]
    arrive(q1, tag_q1, core_dev)
    q1[...] = q1[...] + rqkv[:, :, :, core]
    tag_q2 = send(q1.at[:, :, 1 - y], q2, y_dev)

    for i, (gh, gd) in enumerate(group):
        arrive(al.at[gh, gd], tag_ag[i], group_dev[i])
    rows_all = al[...].reshape(32, 8, 256)
    d_logits_all = jnp.concatenate([rows_all[:, q, :] for q in range(4)], axis=1)
    pooled_all = jnp.concatenate([rows_all[:, 4 + q, :] for q in range(3)], axis=1)
    start = ((h * 4 + dp) * N_HID + z) * 24
    chosen = (iota((24, 768), 1) == iota((24, 768), 0) + start).astype(bfloat)
    mine = dot_nt(chosen, pooled_all.astype(bfloat))
    g_head = jnp.dot(mine, d_logits_all, precision=highest, preferred_element_type=single)
    r.g_head[...] = g_head[:, 0:classes]

    arrive(dnr, tag_dn, x_dev)
    d_normed = dn[0:ROWS, :] + dnr[...].astype(single)
    block_n, block_scale = norm_parts(stream0)
    d_block_gain = jnp.sum(d_normed * block_n, axis=0, keepdims=True)
    d_in = ds[...] + norm_back(block_n, block_scale, d_normed * block_gain)
    dx, gg = r.dx, r.gg
    low, high = d_in[:, 0:384], d_in[:, 384:768]
    dx[0] = jnp.where(h == 0, low, high).astype(bfloat)
    dx[2] = jnp.where(h == 0, high, low).astype(bfloat)
    tag_dx = send(dx.at[2], dx.at[1], x_dev)

    def spread(row):
        blank = jnp.zeros((1, 192), single)
        halves = []
        for a in range(2):
            part = jnp.concatenate([row[:, a * 96 : a * 96 + 96], row[:, 192 + a * 96 : 288 + a * 96]], axis=1)
            halves.append(
                jnp.where(
                    h == 0,
                    jnp.concatenate([part, blank], axis=1),
                    jnp.concatenate([blank, part], axis=1),
                )
            )
        return jnp.concatenate(halves, axis=1)

    d_gains = jnp.concatenate(
        [d_block_gain, d_final_gain, spread(gain_sums[0]), spread(gain_sums[1]), jnp.zeros((4, 768), single)],
        axis=0,
    )
    low, high = d_gains[:, 0:384], d_gains[:, 384:768]
    gg[0] = jnp.where(h == 0, low, high)
    gg[2] = jnp.where(h == 0, high, low)
    tag_gg = send(gg.at[2], gg.at[1], x_dev)
    arrive(dx.at[1], tag_dx, x_dev)
    arrive(gg.at[1], tag_gg, x_dev)
    rext, e1, e2, et, e3 = r.rext, r.e1, r.e2, r.et, r.e3
    dxt = jnp.concatenate([dx[0].astype(single), dx[1].astype(single)], axis=0).T.astype(bfloat)
    px2 = px[...].reshape(2 * ROWS, 1024)
    d_gains = (gg[0] + gg[1]).astype(bfloat)
    x0[...] = dot(dxt, px2[:, 0:512])
    x1[...] = dot(dxt, px2[:, 512:1024]) + dot_tn(d_gains, rows_of.astype(bfloat))
    for d in range(4):
        for w in range(N_HID):
            s = (d * N_HID + w) * 24
            rext[d // 2, d % 2, w] = jnp.concatenate(
                [x0[s : s + 24, :], x1[s : s + 24, :]], axis=0
            ).astype(bfloat)
    tag_e1 = send(rext.at[:, 1 - core], e1, core_dev)
    arrive(q2, tag_q2, y_dev)
    qt[...] = q1[:, :, y] + q2[...]
    tag_q3 = [
        send(qt.at[:, z_up[k] // 2, lax.rem(z_up[k], 2)], q3.at[k - 1], z_dev[k])
        for k in range(1, N_HID)
    ]
    arrive(e1, tag_e1, core_dev)
    e1[...] = e1[...] + rext[:, core]
    tag_e2 = send(e1.at[1 - y], e2, y_dev)
    ff_end()
    total = ot[z].astype(single)
    for k in range(1, N_HID):
        arrive(o3.at[k - 1], tag_o3[k - 1], z_dev[k])
        total = total + o3[k - 1].astype(single)
    r.g_out[...] = total[:, 0:192]
    arrive(e2, tag_e2, y_dev)
    et[...] = e1[y] + e2[...]
    tag_e3 = [send(et.at[z_up[k]], e3.at[k - 1], z_dev[k]) for k in range(1, N_HID)]
    total = qt[:, z // 2, lax.rem(z, 2)].astype(single)
    for k in range(1, N_HID):
        arrive(q3.at[k - 1], tag_q3[k - 1], z_dev[k])
        total = total + q3[k - 1].astype(single)
    r.g_qkv[...] = total
    total = et[z].astype(single)
    for k in range(1, N_HID):
        arrive(e3.at[k - 1], tag_e3[k - 1], z_dev[k])
        total = total + e3[k - 1].astype(single)
    r.g_patch[:, 0:512] = total[0:24]
    r.g_patch[:, 512:768] = total[24:48, 0:256]
    r.g_table[...] = total[24:48, 256 : 256 + seq_len]
    columns = total[24:48, 256:512]
    pick_f = (iota((8, 256), 1) == iota((8, 256), 0) + seq_len).astype(single)
    r.g_gains[...] = dot_nt(pick_f, columns, precision=highest)[0:4]


    def read(prefix, kind):
        values = getattr(r, prefix + kind)[...]
        return values.reshape(-1, values.shape[-1])

    lane = iota((8, 128), 1)
    own = jnp.where(lane == 0, term, 0.0)
    grad_square = None
    for n, kind in enumerate(KINDS):
        value = square_sum(read("g_", kind))
        grad_square = value if grad_square is None else grad_square + value
        own = jnp.where(lane == 8 + n, square_sum(read("w_", kind)), own)
    own = jnp.where(lane == 1, grad_square, own)

    def all_sum(vector, line, every):
        line[z] = vector
        tags_z = [send(line.at[z], line.at[z], z_dev[k]) for k in range(1, N_HID)]
        for k in range(1, N_HID):
            arrive(line.at[z_down[k]], tags_z[k - 1], z_dev[k])
        every[h, dp] = (line[0] + line[1]) + (line[2] + line[3])
        tags_g = [send(every.at[h, dp], every.at[h, dp], device) for device in group_dev]
        for i, (gh, gd) in enumerate(group):
            arrive(every.at[gh, gd], tags_g[i], group_dev[i])
        total = None
        for a in range(2):
            for d in range(4):
                total = every[a, d] if total is None else total + every[a, d]
        return total

    sums = all_sum(own, r.l1, r.v1)
    grad_norm = jnp.sqrt(jnp.sum(jnp.where(lane == 1, sums, 0.0), axis=1, keepdims=True))[0:1]
    clip = jnp.minimum(1.0, clip_at / grad_norm)
    own = jnp.zeros((8, 128), single)
    for n, kind in enumerate(KINDS):
        update = one_update(read("w_", kind), read("m_", kind), read("v_", kind), read("g_", kind), clip)[2]
        own = jnp.where(lane == 8 + n, square_sum(update), own)
    updates = all_sum(own, r.l2, r.v2)
    result = jnp.sqrt(sums) / jnp.sqrt(updates)
    result = jnp.where(lane == 0, sums, result)
    result = jnp.where(lane == 1, grad_norm, result)
    result = jnp.where(lane == 2, clip, result)
    r.scalars[...] = result
    for copy in sends:
        copy.wait_send()


def write_kernel(names, *refs):
    r = types.SimpleNamespace(**dict(zip(names, refs)))
    lane = iota((8, 128), 1)

    def pick(n):
        return jnp.sum(jnp.where(lane == n, r.scalars[...], 0.0), axis=1, keepdims=True)[0:1]

    clip = pick(2)
    for n, kind in enumerate(KINDS):
        master = getattr(r, "w_" + kind)[...]
        grad = getattr(r, "g_" + kind)[...]
        ratio = pick(8 + n)
        if len(master.shape) == 3:
            c, ratio = clip[None], ratio[None]
        else:
            c = clip
        first, second, update = one_update(master, getattr(r, "m_" + kind)[...], getattr(r, "v_" + kind)[...], grad, c)
        getattr(r, "nm_" + kind)[...] = first
        getattr(r, "nv_" + kind)[...] = second
        getattr(r, "nw_" + kind)[...] = master - learn_rate * ratio * update


def fast_device(patches, labels, *state):
    bfloat, single = jnp.bfloat16, jnp.float32

    def turn(kind, value):
        if kind in ("patch", "table", "down"):
            return value.T
        if kind == "qkv":
            return value.transpose(1, 0, 2)
        return value

    flat = [turn(KINDS[i % 8], value) for i, value in enumerate(state)]
    vmem = pl.BlockSpec(memory_space=pltpu.VMEM)
    smem = pl.BlockSpec(memory_space=pltpu.SMEM)
    in_names = ["labels", "patches"] + [p + k for p in ("w_", "m_", "v_") for k in KINDS]
    out_names = ["g_" + k for k in KINDS] + ["scalars"]
    scratch = dict(
        px=((2, ROWS, 1024), bfloat),
        gext=((4, 4, 48, 512), bfloat),
        gqkv=((3, 2, 4, 2, 48, 384), bfloat),
        gout=((4, 4, 96, 256), bfloat),
        gup=((4, 2, 4, 96, 384), bfloat),
        gdn=((4, 2, 4, 96, 384), bfloat),
        ghd=((2, 4, 4, 48, 512), bfloat),
        x0=((384, 512), single),
        x1=((384, 512), single),
        x2=((768, 512), single),
        x3=((768, 512), single),
        ga=((2, 8, 384), single),
        st=((2, 2, ROWS, 384), bfloat),
        nb=((2 * ROWS, 768), bfloat),
        nbt=((768, 2 * ROWS), bfloat),
        qn=((6, 2 * ROWS, HD), single),
        kn=((6, 2 * ROWS, HD), single),
        qr=((6, 2 * ROWS, 1), single),
        kr=((6, 2 * ROWS, 1), single),
        q=((12, ROWS, HD), bfloat),
        k=((12, ROWS, HD), bfloat),
        v=((12, ROWS, HD), bfloat),
        pr=((12, ROWS, ROWS), single),
        ho=((12, ROWS, HD), single),
        hof=((2 * ROWS, 384), bfloat),
        us=((4, 2 * ROWS, 384), single),
        hb=((4, 2 * ROWS, 384), bfloat),
        br=((2 * ROWS, 768), single),
        brs=((2, ROWS, 384), bfloat),
        brr=((2, ROWS, 384), bfloat),
        ds=((ROWS, 768), single),
        db=((2, ROWS, 768), bfloat),
        dbt=((768, 2 * ROWS), bfloat),
        al=((2, 4, 4, 8, 256), single),
        rff=((4, 2, 2, 2, 2, 96, 384), bfloat),
        f1=((4, 2, 2, 2, 96, 384), bfloat),
        f2=((4, 2, 2, 96, 384), bfloat),
        ft=((3, 2, 2, 96, 384), bfloat),
        f3=((3, 2, 2, 96, 384), bfloat),
        rout=((4, 2, 2, 96, 256), bfloat),
        o1=((4, 2, 96, 256), bfloat),
        o2=((4, 96, 256), bfloat),
        ot=((4, 96, 256), bfloat),
        o3=((3, 96, 256), bfloat),
        dh=((12, ROWS, HD), bfloat),
        dk=((12, ROWS, HD), single),
        dv=((12, ROWS, HD), single),
        rqkv=((3, 2, 2, 2, 2, 48, 384), bfloat),
        q1=((3, 2, 2, 2, 48, 384), bfloat),
        q2=((3, 2, 2, 48, 384), bfloat),
        qt=((3, 2, 2, 48, 384), bfloat),
        q3=((3, 3, 48, 384), bfloat),
        dns=((ROWS, 768), bfloat),
        dnr=((ROWS, 768), bfloat),
        dx=((3, ROWS, 384), bfloat),
        gg=((3, 8, 384), single),
        rext=((2, 2, 4, 48, 512), bfloat),
        e1=((2, 4, 48, 512), bfloat),
        e2=((4, 48, 512), bfloat),
        et=((4, 48, 512), bfloat),
        e3=((3, 48, 512), bfloat),
        l1=((4, 8, 128), single),
        l2=((4, 8, 128), single),
        v1=((2, 4, 8, 128), single),
        v2=((2, 4, 8, 128), single),
    )
    semaphores = 180
    shapes = [flat[i].shape for i in range(8)]
    npatch, seq_len, classes = patches.shape[1], flat[1].shape[1], flat[3].shape[1]
    total_images = labels.shape[0] * lax.axis_size("dp")
    sizes = (npatch, seq_len, classes, total_images)
    names = in_names + out_names + list(scratch) + ["ssem", "rsem"]
    found = pl.pallas_call(
        functools.partial(step_kernel, sizes, names),
        out_shape=[jax.ShapeDtypeStruct(s, single) for s in shapes]
        + [jax.ShapeDtypeStruct((8, 128), single)],
        in_specs=[smem] + [vmem] * 25,
        out_specs=[vmem] * 9,
        scratch_shapes=[pltpu.VMEM(s, t) for s, t in scratch.values()]
        + [pltpu.SemaphoreType.DMA((semaphores,))] * 2,
        compiler_params=pltpu.CompilerParams(
            collective_id=0, has_side_effects=True, vmem_limit_bytes=62 * 2**20
        ),
        name="train_step",
    )(labels, patches, *flat)
    grads, scalars = found[:8], found[8]
    names = (
        ["scalars"]
        + [p + k for p in ("w_", "m_", "v_", "g_") for k in KINDS]
        + [p + k for p in ("nm_", "nv_", "nw_") for k in KINDS]
    )
    written = pl.pallas_call(
        functools.partial(write_kernel, names),
        out_shape=[jax.ShapeDtypeStruct(s, single) for s in shapes * 3],
        in_specs=[vmem] * 33,
        out_specs=[vmem] * 24,
        compiler_params=pltpu.CompilerParams(vmem_limit_bytes=48 * 2**20),
        name="write_step",
    )(scalars, *flat, *grads)
    back = [turn(KINDS[i % 8], value) for i, value in enumerate(written)]
    return (scalars[0, 0], scalars[0, 1], *back)


def fits(mesh):
    return tuple(mesh.shape[a] for a in ALL) == (4, 2, N_HID)


def solution(mesh):
    placed = (
        P(ALL, None, None),
        P("dp"),
        P(None, ALL),
        P(None, ALL),
        P(None, ALL),
        P(ALL, None),
        P(DATA, None, "heads"),
        P(MODEL, "dp"),
        P("dp", MODEL),
        P(MODEL, "dp"),
        P(None, ALL),
        P(None, ALL),
        P(None, ALL),
        P(ALL, None),
        P(DATA, None, "heads"),
        P(MODEL, "dp"),
        P("dp", MODEL),
        P(MODEL, "dp"),
        P(None, ALL),
        P(None, ALL),
        P(None, ALL),
        P(ALL, None),
        P(DATA, None, "heads"),
        P(MODEL, "dp"),
        P("dp", MODEL),
        P(MODEL, "dp"),
    )
    return jax.shard_map(
        fast_device if fits(mesh) else per_device,
        mesh=mesh,
        in_specs=placed,
        out_specs=(
            P(),
            P(),
            P(None, ALL),
            P(None, ALL),
            P(None, ALL),
            P(ALL, None),
            P(DATA, None, "heads"),
            P(MODEL, "dp"),
            P("dp", MODEL),
            P(MODEL, "dp"),
            P(None, ALL),
            P(None, ALL),
            P(None, ALL),
            P(ALL, None),
            P(DATA, None, "heads"),
            P(MODEL, "dp"),
            P("dp", MODEL),
            P(MODEL, "dp"),
            P(None, ALL),
            P(None, ALL),
            P(None, ALL),
            P(ALL, None),
            P(DATA, None, "heads"),
            P(MODEL, "dp"),
            P("dp", MODEL),
            P(MODEL, "dp"),
        ),
        check_vma=False,
    )
```

```python
import functools
import types

import jax
import jax.numpy as jnp
from jax import lax
from jax.experimental import pallas as pl
from jax.experimental.pallas import tpu as pltpu
from jax.sharding import PartitionSpec as P

HD = 64
PD = 768
STEP = 10
MESH = pl.DeviceIdType.MESH
ALL = ("dp", "heads", "hidden")
DATA = ("dp", "hidden")
MODEL = ("heads", "hidden")


beta_one = 0.9
beta_two = 0.999
adam_eps = 1e-08
decay_rate = 0.01
learn_rate = 0.5
clip_at = 0.001
norm_eps = 1e-06
highest = lax.Precision.HIGHEST


def layer_norm(values):
    center = values - jnp.mean(values, axis=-1, keepdims=True)
    return center * lax.rsqrt(jnp.mean(center * center, axis=-1, keepdims=True) + norm_eps)


def head_loss(stream_out, targets, final_gain, head_weight, npatch, total_images):
    normed_out, norm_back = jax.vjp(layer_norm, stream_out)
    final = normed_out * final_gain
    pooled_b = jnp.mean(final[:, :npatch], axis=1).astype(jnp.bfloat16)
    logits = jnp.dot(pooled_b, head_weight, preferred_element_type=jnp.float32)
    log_total = jax.nn.logsumexp(logits, axis=-1)
    onehot = (targets[:, None] == lax.broadcasted_iota(jnp.int32, logits.shape, 1)).astype(
        jnp.float32
    )
    terms = log_total - jnp.sum(logits * onehot, axis=-1)
    d_logits = (jnp.exp(logits - log_total[:, None]) - onehot) / total_images
    d_pooled = jnp.dot(d_logits, head_weight.astype(jnp.float32).T, precision=highest)
    count, seq_len, width = stream_out.shape
    spread = jnp.broadcast_to(d_pooled[:, None, :] / npatch, (count, npatch, width))
    d_final = jnp.concatenate(
        [spread, jnp.zeros((count, seq_len - npatch, width), jnp.float32)], axis=1
    )
    d_stream = norm_back(d_final * final_gain)[0]
    d_gain_rows = jnp.sum(d_final * normed_out, axis=1)
    return (terms, pooled_b, d_logits, d_stream, d_gain_rows)


def per_device(
    patches,
    labels,
    w_patch,
    table,
    gains,
    w_head,
    w_qkv,
    w_out,
    w_up,
    w_down,
    first_patch,
    first_table,
    first_gains,
    first_head,
    first_qkv,
    first_out,
    first_up,
    first_down,
    second_patch,
    second_table,
    second_gains,
    second_head,
    second_qkv,
    second_out,
    second_up,
    second_down,
):
    masters = [w_patch, table, gains, w_head, w_qkv, w_out, w_up, w_down]
    firsts = [
        first_patch,
        first_table,
        first_gains,
        first_head,
        first_qkv,
        first_out,
        first_up,
        first_down,
    ]
    seconds = [
        second_patch,
        second_table,
        second_gains,
        second_head,
        second_qkv,
        second_out,
        second_up,
        second_down,
    ]
    bfloat = jnp.bfloat16
    single = jnp.float32
    patch_b, table_b, gains_b, head_b = (
        lax.all_gather(w_patch.astype(bfloat), ALL, axis=1, tiled=True),
        lax.all_gather(table.astype(bfloat), ALL, axis=1, tiled=True),
        lax.all_gather(gains.astype(bfloat), ALL, axis=1, tiled=True),
        lax.all_gather(w_head.astype(bfloat), ALL, axis=0, tiled=True),
    )
    qkv_b = lax.all_gather(w_qkv.astype(bfloat), DATA, axis=0, tiled=True)
    out_b, up_b, down_b = (
        lax.all_gather(w_out.astype(bfloat), "dp", axis=1, tiled=True),
        lax.all_gather(w_up.astype(bfloat), "dp", axis=0, tiled=True),
        lax.all_gather(w_down.astype(bfloat), "dp", axis=1, tiled=True),
    )
    gain_vals = gains_b.astype(single)
    table_vals = table_b.astype(single)
    n_hidden = lax.axis_size("hidden")
    n_own = patches.shape[0]
    npatch = patches.shape[1]
    seq_len = table_b.shape[0]
    width = patch_b.shape[1]
    group_width = qkv_b.shape[2]
    group_heads = group_width // HD
    own_index = lax.axis_index("heads") * n_hidden + lax.axis_index("hidden")
    total_images = labels.shape[0] * lax.axis_size("dp")
    embedded = jnp.dot(patches.reshape(n_own * npatch, PD), patch_b, preferred_element_type=single)
    embedded = embedded.reshape(n_own, npatch, width) + table_vals[:npatch]
    registers = jnp.broadcast_to(table_vals[npatch:], (n_own, seq_len - npatch, width))
    stream_own = jnp.concatenate([embedded, registers], axis=1).astype(bfloat)
    stream_in = lax.all_gather(stream_own, MODEL, axis=0, tiled=True)
    n_img = stream_in.shape[0]
    row_count = n_img * seq_len
    stream_flat = stream_in.astype(single).reshape(row_count, width)
    normed_b = (layer_norm(stream_flat) * gain_vals[0]).astype(bfloat)
    n_att = n_img // n_hidden
    att_start = lax.axis_index("hidden") * n_att
    normed_att = lax.dynamic_slice_in_dim(
        normed_b.reshape(n_img, seq_len, width), att_start, n_att, 0
    )
    query_gain = lax.dynamic_slice_in_dim(
        gain_vals[2], lax.axis_index("heads") * group_width, group_width, 0
    ).reshape(group_heads, HD)
    key_gain = lax.dynamic_slice_in_dim(
        gain_vals[3], lax.axis_index("heads") * group_width, group_width, 0
    ).reshape(group_heads, HD)
    mixed = jnp.einsum("bsd,dcf->bscf", normed_att, qkv_b, preferred_element_type=single)
    mixed = mixed.reshape(n_att, seq_len, 3, group_heads, HD)
    query_norm, query_back = jax.vjp(layer_norm, mixed[:, :, 0])
    key_norm, key_back = jax.vjp(layer_norm, mixed[:, :, 1])
    queries = (query_norm * query_gain).astype(bfloat)
    keys = (key_norm * key_gain).astype(bfloat)
    values = mixed[:, :, 2].astype(bfloat)
    scale = HD ** (-0.5)
    scores = jnp.einsum("bqhd,bkhd->bhqk", queries, keys, preferred_element_type=single) * scale
    probs = jax.nn.softmax(scores, axis=-1)
    probs_b = probs.astype(bfloat)
    heads_out = jnp.einsum("bhqk,bkhd->bqhd", probs_b, values, preferred_element_type=single)
    heads_out = heads_out.astype(bfloat).reshape(n_att * seq_len, group_width)
    columns = lax.all_to_all(heads_out, "hidden", split_axis=1, concat_axis=0, tiled=True)
    attn_part = jnp.dot(columns, out_b, preferred_element_type=single)
    upper = jnp.dot(normed_b, up_b, preferred_element_type=single)
    activated, gelu_back = jax.vjp(jax.nn.gelu, upper)
    activated_b = activated.astype(bfloat)
    partial_sum = attn_part + jnp.dot(activated_b, down_b, preferred_element_type=single)
    total = lax.psum(partial_sum, MODEL)
    stream_out = (stream_flat + total).reshape(n_img, seq_len, width)
    terms, pooled_b, d_logits, d_stream, d_gain_rows = head_loss(
        stream_out, labels, gain_vals[1], head_b, npatch, total_images
    )
    loss_terms = lax.dynamic_slice_in_dim(terms, own_index * n_own, n_own, 0)
    pooled_own = lax.dynamic_slice_in_dim(pooled_b, own_index * n_own, n_own, 0)
    logits_own = lax.dynamic_slice_in_dim(d_logits, own_index * n_own, n_own, 0)
    d_head = jnp.dot(pooled_own.astype(single).T, logits_own, precision=highest)
    d_final_gain = jnp.sum(
        lax.dynamic_slice_in_dim(d_gain_rows, own_index * n_own, n_own, 0), axis=0
    )
    d_stream_own = lax.dynamic_slice_in_dim(d_stream, own_index * n_own, n_own, 0)
    d_branch = d_stream.reshape(row_count, width).astype(bfloat)
    d_activated = jnp.dot(d_branch, down_b.T, preferred_element_type=single)
    d_upper = gelu_back(d_activated)[0].astype(bfloat)
    d_down = jnp.dot(activated_b.T, d_branch, preferred_element_type=single)
    d_up = jnp.dot(normed_b.T, d_upper, preferred_element_type=single)
    d_normed = jnp.dot(d_upper, up_b.T, preferred_element_type=single)
    d_out = jnp.dot(columns.T, d_branch, preferred_element_type=single)
    d_columns = jnp.dot(d_branch, out_b.T, preferred_element_type=single).astype(bfloat)
    d_heads = lax.all_to_all(d_columns, "hidden", split_axis=0, concat_axis=1, tiled=True).reshape(
        n_att, seq_len, group_heads, HD
    )
    d_probs = jnp.einsum("bqhd,bkhd->bhqk", d_heads, values, preferred_element_type=single)
    d_values = jnp.einsum("bhqk,bqhd->bkhd", probs_b, d_heads, preferred_element_type=single)
    d_scores = (probs * (d_probs - jnp.sum(probs * d_probs, axis=-1, keepdims=True))).astype(bfloat)
    d_query_norm = (
        jnp.einsum("bhqk,bkhd->bqhd", d_scores, keys, preferred_element_type=single) * scale
    )
    d_key_norm = (
        jnp.einsum("bhqk,bqhd->bkhd", d_scores, queries, preferred_element_type=single) * scale
    )
    d_queries = query_back(d_query_norm * query_gain)[0]
    d_keys = key_back(d_key_norm * key_gain)[0]
    d_query_gain = jnp.sum(d_query_norm * query_norm, axis=(0, 1)).reshape(group_width)
    d_key_gain = jnp.sum(d_key_norm * key_norm, axis=(0, 1)).reshape(group_width)
    d_mixed = (
        jnp.stack([d_queries, d_keys, d_values], axis=2)
        .astype(bfloat)
        .reshape(n_att, seq_len, 3, group_width)
    )
    d_qkv = jnp.einsum("bsd,bscf->dcf", normed_att, d_mixed, preferred_element_type=single)
    d_att_in = jnp.einsum("bscf,dcf->bsd", d_mixed, qkv_b, preferred_element_type=single)
    d_normed = d_normed.reshape(n_img, seq_len, width)
    d_normed = lax.dynamic_update_slice_in_dim(
        d_normed, lax.dynamic_slice_in_dim(d_normed, att_start, n_att, 0) + d_att_in, att_start, 0
    )
    d_normed_own = lax.psum_scatter(
        d_normed.reshape(row_count, width).astype(jnp.bfloat16),
        MODEL,
        scatter_dimension=0,
        tiled=True,
    ).astype(jnp.float32)
    d_normed_own = d_normed_own.reshape(n_own, seq_len, width)
    normed_own, block_back = jax.vjp(layer_norm, stream_own.astype(single))
    d_stream_in = d_stream_own + block_back(d_normed_own * gain_vals[0])[0]
    d_block_gain = jnp.sum(d_normed_own * normed_own, axis=(0, 1))
    d_patch = jnp.dot(
        patches.reshape(n_own * npatch, PD).astype(single).T,
        d_stream_in[:, :npatch].reshape(n_own * npatch, width),
        precision=highest,
    )
    d_table = jnp.sum(d_stream_in, axis=0)
    zero_row = jnp.zeros((width,), single)
    gain_offset = lax.axis_index("heads") * group_width
    d_gains = jnp.stack(
        [
            d_block_gain,
            d_final_gain,
            lax.dynamic_update_slice_in_dim(zero_row, d_query_gain, gain_offset, 0),
            lax.dynamic_update_slice_in_dim(zero_row, d_key_gain, gain_offset, 0),
        ]
    )
    grad_patch, grad_table, grad_gains, grad_head = (
        lax.psum_scatter(d_patch, ALL, scatter_dimension=1, tiled=True),
        lax.psum_scatter(d_table, ALL, scatter_dimension=1, tiled=True),
        lax.psum_scatter(d_gains, ALL, scatter_dimension=1, tiled=True),
        lax.psum_scatter(d_head, ALL, scatter_dimension=0, tiled=True),
    )
    grad_qkv = lax.psum_scatter(d_qkv, DATA, scatter_dimension=0, tiled=True)
    grad_out, grad_up, grad_down = (
        lax.psum_scatter(d_out.astype(jnp.bfloat16), "dp", scatter_dimension=1, tiled=True).astype(
            jnp.float32
        ),
        lax.psum_scatter(d_up.astype(jnp.bfloat16), "dp", scatter_dimension=0, tiled=True).astype(
            jnp.float32
        ),
        lax.psum_scatter(d_down.astype(jnp.bfloat16), "dp", scatter_dimension=1, tiled=True).astype(
            jnp.float32
        ),
    )
    grads = [grad_patch, grad_table, grad_gains, grad_head, grad_qkv, grad_out, grad_up, grad_down]
    grad_squares = jnp.stack([jnp.sum(grad * grad) for grad in grads])
    weight_squares = jnp.stack([jnp.sum(master * master) for master in masters])
    grad_squares, weight_squares, loss_sum = lax.psum(
        (grad_squares, weight_squares, jnp.sum(loss_terms)), ALL
    )
    grad_norm = jnp.sqrt(jnp.sum(grad_squares))
    clip = jnp.minimum(1.0, clip_at / grad_norm)
    new_firsts, new_seconds, updates = ([], [], [])
    for master, first, second, grad in zip(masters, firsts, seconds, grads):
        clipped = grad * clip
        first_new = beta_one * first + (1.0 - beta_one) * clipped
        second_new = beta_two * second + (1.0 - beta_two) * clipped * clipped
        update = (
            first_new
            / (1.0 - beta_one**STEP)
            / (jnp.sqrt(second_new / (1.0 - beta_two**STEP)) + adam_eps)
        )
        updates.append(update + decay_rate * master)
        new_firsts.append(first_new)
        new_seconds.append(second_new)
    update_squares = lax.psum(
        jnp.stack([jnp.sum(update * update) for update in updates]), ALL
    )
    ratios = jnp.sqrt(weight_squares) / jnp.sqrt(update_squares)
    new_weights = [
        master - learn_rate * ratios[number] * update
        for number, (master, update) in enumerate(zip(masters, updates))
    ]
    return (
        loss_sum,
        grad_norm,
        new_firsts[0],
        new_firsts[1],
        new_firsts[2],
        new_firsts[3],
        new_firsts[4],
        new_firsts[5],
        new_firsts[6],
        new_firsts[7],
        new_seconds[0],
        new_seconds[1],
        new_seconds[2],
        new_seconds[3],
        new_seconds[4],
        new_seconds[5],
        new_seconds[6],
        new_seconds[7],
        new_weights[0],
        new_weights[1],
        new_weights[2],
        new_weights[3],
        new_weights[4],
        new_weights[5],
        new_weights[6],
        new_weights[7],
    )


def dot(a, b):
    return jnp.dot(a, b, preferred_element_type=jnp.float32)


def dot_nt(a, b, precision=None):
    return lax.dot_general(
        a, b, (((1,), (1,)), ((), ())), precision=precision, preferred_element_type=jnp.float32
    )


def dot_tn(a, b, precision=None):
    return lax.dot_general(
        a, b, (((0,), (0,)), ((), ())), precision=precision, preferred_element_type=jnp.float32
    )


def norm_parts(values):
    center = values - jnp.mean(values, axis=-1, keepdims=True)
    scale = lax.rsqrt(jnp.mean(center * center, axis=-1, keepdims=True) + norm_eps)
    return center * scale, scale


def norm_back(normed, scale, grad):
    inner = jnp.mean(grad * normed, axis=-1, keepdims=True)
    return scale * (grad - jnp.mean(grad, axis=-1, keepdims=True) - normed * inner)


gelu_c = 0.7978845608028654


def gelu_tanh(u):
    return jnp.tanh(gelu_c * (u + 0.044715 * (u * u * u)))


def iota(shape, axis):
    return lax.broadcasted_iota(jnp.int32, shape, axis)


def one_update(master, first, second, grad, clip):
    clipped = grad * clip
    first_new = beta_one * first + (1.0 - beta_one) * clipped
    second_new = beta_two * second + (1.0 - beta_two) * clipped * clipped
    update = (
        first_new
        / (1.0 - beta_one**STEP)
        / (jnp.sqrt(second_new / (1.0 - beta_two**STEP)) + adam_eps)
    )
    return first_new, second_new, update + decay_rate * master


def square_sum(values):
    return jnp.sum(values * values, axis=(0, 1), keepdims=True)


KINDS = ("patch", "table", "gains", "head", "qkv", "out", "up", "down")
ROWS = 208
N_HID = 4


def step_kernel(sizes, names, *refs):
    npatch, seq_len, classes, total_images = sizes
    r = types.SimpleNamespace(**dict(zip(names, refs)))
    bfloat, single = jnp.bfloat16, jnp.float32
    dp, h, z = (lax.axis_index(a) for a in ALL)
    core, y = lax.rem(dp, 2), dp // 2
    y_dp, core_dp = (1 - y) * 2 + core, y * 2 + (1 - core)
    x_dev, y_dev, core_dev = (dp, 1 - h, z), (y_dp, h, z), (core_dp, h, z)
    z_up = [lax.rem(z + k, N_HID) for k in range(N_HID)]
    z_down = [lax.rem(z + N_HID - k, N_HID) for k in range(N_HID)]
    z_dev = [(dp, h, z_up[k]) for k in range(N_HID)]
    group = []
    for a in (0, 1):
        for b in (0, 1):
            for c in (0, 1):
                if a + b + c:
                    gh = 1 - h if a else h
                    gy = 1 - y if b else y
                    gc = 1 - core if c else core
                    group.append((gh, gy * 2 + gc))
    group_dev = [(gd, gh, z) for gh, gd in group]

    barrier = pltpu.get_barrier_semaphore()
    for device in z_dev[1:] + group_dev:
        pl.semaphore_signal(barrier, inc=1, device_id=device, device_id_type=MESH)

    loads = {}
    order = ["w_patch", "w_table", "w_gains", "patches"]
    order += [p + k for p in ("w_", "m_", "v_") for k in KINDS if p + k not in order]
    for number, name in enumerate(order):
        loads[name] = pltpu.make_async_copy(
            getattr(r, "h_" + name), getattr(r, name), r.lsem.at[number]
        )
        loads[name].start()
    stores = []

    def store(name):
        copy = pltpu.make_async_copy(
            getattr(r, name), getattr(r, "h_" + name), r.lsem.at[len(order) + len(stores)]
        )
        copy.start()
        stores.append(copy)

    ssem, rsem = r.ssem, r.rsem
    count = [0]
    sends = {}
    last = N_HID - 1
    holds = {}
    for d in range(1, N_HID):
        holds["left", d] = z >= d
        holds["right", d] = z + d <= last
        holds["on_right", d] = (z >= d) & (z < last)
        holds["on_left", d] = (z + d <= last) & (z > 0)
    holds["on_right", 0] = z < last
    holds["on_left", 0] = z > 0
    next_z = {"left": (dp, h, z_up[1]), "right": (dp, h, z_down[1])}

    def send(source, target, device, key=None):
        number = count[0]
        count[0] += 1
        copy = pltpu.make_async_remote_copy(
            src_ref=source,
            dst_ref=target,
            send_sem=ssem.at[number],
            recv_sem=rsem.at[number],
            device_id=device,
            device_id_type=MESH,
        )
        if key is None:
            copy.start()
        else:
            pl.when(holds[key])(copy.start)
        sends.setdefault(key, []).append(copy)
        return number

    def arrive(target, number, device):
        pltpu.make_async_remote_copy(
            src_ref=target,
            dst_ref=target,
            send_sem=ssem.at[number],
            recv_sem=rsem.at[number],
            device_id=device,
            device_id_type=MESH,
        ).wait_recv()

    gext, gqkv, gout, gup, gdn, ghd = r.gext, r.gqkv, r.gout, r.gup, r.gdn, r.ghd
    x0, x1, px = r.x0, r.x1, r.px

    def pack_ext():
        x1[0:24, :] = jnp.zeros((24, 512), single)
        for name in order[0:3]:
            loads[name].wait()
        x1[0:24, 256 : 256 + seq_len] = r.w_table[...]
        pick = (iota((4, 256), 1) == iota((4, 256), 0) + seq_len).astype(bfloat)
        table_part = x1[0:24, 256:512] + dot_tn(r.w_gains[...].astype(bfloat), pick)
        wp = r.w_patch[...]
        gext[dp, z] = jnp.concatenate(
            [wp[:, 0:512], jnp.concatenate([wp[:, 512:768], table_part], axis=1)], axis=0
        ).astype(bfloat)

    def pack_patches():
        row, col = iota((ROWS, 256), 0), iota((ROWS, 256), 1)
        spot = jnp.where((row == col) & (row < seq_len), 1.0, 0.0).astype(bfloat)
        px[0, :, 768:1024] = spot
        px[1, :, 768:1024] = spot
        px[0, ROWS - 16 : ROWS, 0:768] = jnp.zeros((16, 768), bfloat)
        loads["patches"].wait()
        px[0, 0:npatch, 0:768] = r.patches[0]

    def pack_rest():
        loads["w_qkv"].wait()
        gqkv[:, z // 2, dp, lax.rem(z, 2)] = r.w_qkv[...].astype(bfloat)
        yield
        loads["w_up"].wait()
        gup[z, :, dp] = r.w_up[...].astype(bfloat).reshape(2, 96, 384)
        yield
        loads["w_head"].wait()
        x0[0:24, :] = r.w_head[:, 0:512]
        x1[0:24, :] = jnp.zeros((24, 512), single)
        x1[0:24, 0 : classes - 512] = r.w_head[:, 512:classes]
        ghd[h, dp, z] = jnp.concatenate([x0[0:24, :], x1[0:24, :]], axis=0).astype(bfloat)
        yield
        loads["w_out"].wait()
        gout[dp, z] = jnp.zeros((96, 256), bfloat)
        gout[dp, z, :, 0:192] = r.w_out[...].astype(bfloat)
        yield
        loads["w_down"].wait()
        gdn[z, :, dp] = r.w_down[...].astype(bfloat).reshape(2, 96, 384)
        yield

    def at_ext(d, w):
        return gext.at[d, w]

    def at_qkv(d, w):
        return gqkv.at[:, w // 2, d, lax.rem(w, 2)]

    def at_out(d, w):
        return gout.at[d, w]

    def at_up(half):
        return lambda d, w: gup.at[w, half, d]

    def at_dn(half):
        return lambda d, w: gdn.at[w, half, d]

    def at_hd(d, w):
        return ghd.at[h, d, w]

    slot = {
        "ext": at_ext,
        "qkv": at_qkv,
        "out": at_out,
        "up0": at_up(0),
        "up1": at_up(1),
        "dn0": at_dn(0),
        "dn1": at_dn(1),
        "hd": at_hd,
    }
    lines = {
        "ext": lambda d: gext.at[d],
        "qkv": lambda d: gqkv.at[:, :, d],
        "out": lambda d: gout.at[d],
        "up0": lambda d: gup.at[:, 0, d],
        "up1": lambda d: gup.at[:, 1, d],
        "dn0": lambda d: gdn.at[:, 0, d],
        "dn1": lambda d: gdn.at[:, 1, d],
        "hd": lambda d: ghd.at[h, d],
    }
    tags = {}

    def send_own(name):
        own = slot[name](dp, z)
        tags[name, "left", 1] = send(own, own, next_z["left"], ("on_right", 0))
        tags[name, "right", 1] = send(own, own, next_z["right"], ("on_left", 0))
        tags[name, "y", 0] = send(own, own, y_dev)

    def pass_z(name, d):
        for side, on, theirs in (("left", "on_right", z_down[d]), ("right", "on_left", z_up[d])):
            block = slot[name](dp, theirs)
            number = tags[name, side, d]
            pl.when(holds[side, d])(functools.partial(arrive, block, number, y_dev))
            if d < last:
                tags[name, side, d + 1] = send(block, block, next_z[side], (on, d))
            tags[name, "y", side, d] = send(block, block, y_dev, (side, d))
        if d == last and name != "hd":
            line = lines[name](dp)
            tags[name, "c", 0] = send(line, line, core_dev)

    def pass_core(name):
        at = slot[name]
        arrive(at(y_dp, z), tags[name, "y", 0], y_dev)
        for d in range(1, N_HID):
            for side, theirs in (("left", z_down[d]), ("right", z_up[d])):
                number = tags[name, "y", side, d]
                pl.when(holds[side, d])(functools.partial(arrive, at(y_dp, theirs), number, y_dev))
        line = lines[name](y_dp)
        if name != "hd":
            tags[name, "c", 1] = send(line, line, core_dev)
        else:
            own = lines[name](dp)
            tags[name, "x", 0] = send(own, own, x_dev)
            tags[name, "x", 1] = send(line, line, x_dev)

    def complete(name):
        far = (1 - y) * 2 + (1 - core)
        arrive(lines[name](core_dp), tags[name, "c", 0], core_dev)
        arrive(lines[name](far), tags[name, "c", 1], core_dev)

    def head_core():
        for i, d in enumerate((dp, y_dp)):
            arrive(ghd.at[1 - h, d], tags["hd", "x", i], x_dev)
        for i, d in enumerate((dp, y_dp)):
            block = ghd.at[:, d]
            tags["hd", "c", i] = send(block, block, core_dev)

    def head_complete():
        far = (1 - y) * 2 + (1 - core)
        for i, d in enumerate((core_dp, far)):
            arrive(ghd.at[:, d], tags["hd", "c", i], core_dev)

    pack_ext()
    pl.semaphore_wait(barrier, len(z_dev) - 1 + len(group_dev))
    send_own("ext")
    packing = pack_rest()
    next(packing)
    send_own("qkv")
    pass_z("ext", 1)
    pack_patches()
    images = px.at[0, :, pl.ds(0, 768)]
    tag_px = send(images, px.at[1, :, pl.ds(0, 768)], x_dev)
    next(packing)
    send_own("up0")
    pass_z("ext", 2)
    pass_z("qkv", 1)
    send_own("up1")
    pass_z("ext", 3)
    for _ in packing:
        pass
    pass_z("qkv", 2)
    pass_z("up0", 1)
    send_own("hd")
    pass_core("ext")
    complete("ext")

    for d in range(4):
        for w in range(N_HID):
            s = (d * N_HID + w) * 24
            block = gext[d, w].astype(single)
            x0[s : s + 24, :] = block[0:24]
            x1[s : s + 24, :] = block[24:48]
    x1b = x1[...].astype(bfloat)
    ga = r.ga
    rows_of = (iota((8, 512), 1) == iota((8, 512), 0) + (256 + seq_len)) & (iota((8, 512), 0) < 4)
    ga[h] = dot_nt(rows_of.astype(bfloat), x1b)
    tag_ga = send(ga.at[h], ga.at[h], x_dev)
    x0b = x0[...].astype(bfloat)
    st = r.st
    st[h, 0] = (dot_nt(px[0, :, 0:512], x0b) + dot_nt(px[0, :, 512:1024], x1b)).astype(bfloat)
    tag_st0 = send(st.at[h, 0], st.at[h, 1], x_dev)
    arrive(px.at[1, :, pl.ds(0, 768)], tag_px, x_dev)
    st[h, 1] = (dot_nt(px[1, :, 0:512], x0b) + dot_nt(px[1, :, 512:1024], x1b)).astype(bfloat)
    tag_st1 = send(st.at[h, 1], st.at[h, 0], x_dev)
    pass_z("qkv", 3)
    pass_z("up0", 2)
    pass_z("up1", 1)
    send_own("out")
    arrive(ga.at[1 - h], tag_ga, x_dev)
    arrive(st.at[1 - h, 1], tag_st0, x_dev)
    arrive(st.at[1 - h, 0], tag_st1, x_dev)

    def gain_row(i):
        return jnp.concatenate([ga[0, i : i + 1, :], ga[1, i : i + 1, :]], axis=1)

    def head_gain(i):
        pieces = []
        both = [ga[0, i : i + 1, :], ga[1, i : i + 1, :]]
        for d in range(4):
            pieces.extend(half[:, d * 96 : d * 96 + 96] for half in both)
        low = jnp.concatenate(pieces[0:4], axis=1)
        high = jnp.concatenate(pieces[4:8], axis=1)
        return jnp.where(h == 0, low, high)

    nb, nbt = r.nb, r.nbt
    block_gain = gain_row(0)
    for i in range(2):
        stream = jnp.concatenate([st[0, i], st[1, i]], axis=1).astype(single)
        nb[i * ROWS : (i + 1) * ROWS, :] = (norm_parts(stream)[0] * block_gain).astype(bfloat)
    pass_z("up0", 3)
    pass_z("up1", 2)
    pass_z("hd", 1)
    send_own("dn0")
    pass_core("qkv")
    complete("qkv")

    qn, kn = r.qn, r.kn
    q_ref, k_ref, v_ref = r.q, r.k, r.v
    q_gain, k_gain = head_gain(2), head_gain(3)
    for c, (keep, out, gain) in enumerate(
        ((qn, q_ref, q_gain), (kn, k_ref, k_gain), (None, v_ref, None))
    ):
        mixed = dot(nb[...], gqkv[c].reshape(768, 384))
        for n in range(6):
            part = mixed[:, n * HD : (n + 1) * HD]
            if keep is not None:
                part, scale = norm_parts(part)
                keep[n, :, 0:HD] = part
                keep[n, :, HD : 2 * HD] = jnp.broadcast_to(scale, (2 * ROWS, HD))
                part = part * gain[:, n * HD : (n + 1) * HD]
            part = part.astype(bfloat)
            out[2 * n] = part[0:ROWS]
            out[2 * n + 1] = part[ROWS : 2 * ROWS]
        if c == 0:
            pass_z("up1", 3)
            pass_z("hd", 2)
            pass_z("out", 1)
            send_own("dn1")
            pass_core("up0")

    pr, ho = r.pr, r.ho
    dead = iota((ROWS, ROWS), 1) >= seq_len

    def attend(n, carry):
        for i in (2 * n, 2 * n + 1):
            scores = dot_nt(q_ref[i], k_ref[i]) * HD ** (-0.5)
            scores = jnp.where(dead, -1e30, scores)
            scores = scores - jnp.max(scores, axis=-1, keepdims=True)
            weights = jnp.exp(scores)
            probs = weights / jnp.sum(weights, axis=-1, keepdims=True)
            pr[i] = probs
            ho[i] = dot(probs.astype(bfloat), v_ref[i])
        return carry

    lax.fori_loop(0, 2, attend, 0)
    pass_z("hd", 3)
    pass_z("out", 2)
    pass_z("dn0", 1)
    pass_core("up1")
    lax.fori_loop(2, 6, attend, 0)
    pass_z("out", 3)
    pass_z("dn0", 2)
    pass_z("dn1", 1)
    pass_core("hd")
    hof = r.hof
    for i in range(2):
        joined = jnp.concatenate([ho[2 * n + i] for n in range(6)], axis=1)
        hof[i * ROWS : (i + 1) * ROWS, :] = joined.astype(bfloat)
    complete("up0")
    complete("up1")

    us, hb, br = r.us, r.hb, r.br

    def rise(w, carry):
        upper = dot(nb[...], gup[w].reshape(768, 384))
        us[w] = upper
        hb[w] = (0.5 * upper * (1.0 + gelu_tanh(upper))).astype(bfloat)
        return carry

    lax.fori_loop(0, N_HID, rise, 0)
    pass_z("dn0", 3)
    pass_z("dn1", 2)
    pass_core("out")
    complete("out")
    lefts, rights = [], []
    for d in range(4):
        part = dot(hof[...], gout[d].reshape(384, 256))
        lefts.append(part[:, 0:96])
        rights.append(part[:, 96:192])
    br[:, 0:384] = jnp.concatenate(lefts, axis=1)
    br[:, 384:768] = jnp.concatenate(rights, axis=1)
    head_core()
    nbt[...] = nb[...].T
    brs, brr = r.brs, r.brr
    tag_br = {}
    for half in range(2):
        name = "dn%d" % half
        lanes = slice(half * 384, half * 384 + 384)
        if half:
            head_complete()
        else:
            pass_z("dn1", 3)
        pass_core(name)
        complete(name)

        def fall(w, carry):
            br[:, lanes] += dot_nt(hb[w], gdn[w, half].reshape(384, 384))
            return carry

        lax.fori_loop(0, N_HID, fall, 0)
        for i in (1, 0):
            brs[half, i] = br[i * ROWS : (i + 1) * ROWS, lanes].astype(bfloat)
            tag_br[half, i] = send(brs.at[half, i], brr.at[half, 1 - i], x_dev)
    hw = r.hw
    for a in range(2):
        for d in range(4):
            for w in range(N_HID):
                s = (d * N_HID + w) * 24
                block = ghd[a, d, w].astype(single)
                x0[s : s + 24, :] = block[0:24]
                x1[s : s + 24, :] = block[24:48]
        hw[0, a * 384 : a * 384 + 384, :] = x0[...].astype(bfloat)
        hw[1, a * 384 : a * 384 + 384, :] = x1[...].astype(bfloat)

    def stream_out(i):
        for half in range(2):
            arrive(brr.at[half, i], tag_br[half, 1 - i], x_dev)
        stream = jnp.concatenate([st[0, i], st[1, i]], axis=1).astype(single)
        theirs = jnp.concatenate([brr[0, i], brr[1, i]], axis=1).astype(single)
        return norm_parts(stream + (br[i * ROWS : (i + 1) * ROWS, :] + theirs))

    out_n, out_scale = stream_out(0)
    is_patch = iota((ROWS, 1), 0) < npatch
    final_gain = gain_row(1)
    n_sum = jnp.sum(jnp.where(is_patch, out_n, 0.0), axis=0, keepdims=True)
    pooled = n_sum * final_gain / npatch
    pooled_b = pooled.astype(bfloat)
    heads_b = [hw[0], hw[1]]
    pooled_8 = jnp.broadcast_to(pooled_b, (16, 768))
    logits = jnp.concatenate([dot(pooled_8, m)[0:1] for m in heads_b], axis=1)
    lane = iota((1, 1024), 1)
    logits = jnp.where(lane < classes, logits, -1e30)
    top = jnp.max(logits, axis=-1, keepdims=True)
    log_total = top + jnp.log(jnp.sum(jnp.exp(logits - top), axis=-1, keepdims=True))
    onehot = jnp.where(lane == r.labels[h * N_HID + z], 1.0, 0.0)
    term = log_total - jnp.sum(jnp.where(lane < classes, logits, 0.0) * onehot, axis=-1, keepdims=True)
    d_logits = (jnp.exp(logits - log_total) - onehot) / total_images
    hi = d_logits.astype(bfloat).astype(single)
    both = jnp.concatenate([hi, d_logits - hi, jnp.zeros((14, 1024), single)], axis=0).astype(bfloat)
    back = dot_nt(both[:, 0:512], heads_b[0]) + dot_nt(both[:, 512:1024], heads_b[1])
    d_pooled = (back[0:1] + back[1:2]) / npatch
    d_row = d_pooled * final_gain
    rw = r.rw
    rw[0] = jnp.broadcast_to(d_row, (8, 768))
    tag_rw = send(rw.at[0], rw.at[1], x_dev)
    ds, db, dbt = r.ds, r.db, r.dbt
    d_stream = jnp.where(is_patch, norm_back(out_n, out_scale, d_row), 0.0)
    ds[...] = d_stream
    db[0] = d_stream.astype(bfloat)
    dbt[:, 0:ROWS] = d_stream.T.astype(bfloat)
    d_final_gain = d_pooled * n_sum
    al = r.al
    pooled_f = pooled_b.astype(single)
    al[h, dp, z] = jnp.concatenate(
        [d_logits[:, q * 256 : q * 256 + 256] for q in range(4)]
        + [pooled_f[:, q * 256 : q * 256 + 256] for q in range(3)]
        + [jnp.zeros((1, 256), single)],
        axis=0,
    )
    tag_al = [send(al.at[h, dp, z], al.at[h, dp, z], z_dev[k]) for k in range(1, N_HID)]
    out_n, out_scale = stream_out(1)
    arrive(rw.at[1], tag_rw, x_dev)
    d_stream = jnp.where(is_patch, norm_back(out_n, out_scale, rw[1, 0:1, :]), 0.0)
    db[1] = d_stream.astype(bfloat)
    dbt[:, ROWS : 2 * ROWS] = d_stream.T.astype(bfloat)
    db2 = db[...].reshape(2 * ROWS, 768)

    rff, f1, f2, ft, f3 = r.rff, r.f1, r.f2, r.ft, r.f3
    dn = br
    ff_tags = {}

    def ff_block(k):
        w = z_up[k]
        upper = us[w]
        t = gelu_tanh(upper)
        slope = 0.5 * (1.0 + t) + 0.5 * upper * (1.0 - t * t) * gelu_c * (
            1.0 + 3 * 0.044715 * (upper * upper)
        )
        d_hidden = dot(db2, gdn[w].reshape(768, 384))
        d_upper = (d_hidden * slope).astype(bfloat)
        rff[k, 1] = dot(dbt[...], hb[w]).astype(bfloat).reshape(2, 2, 2, 96, 384)
        rff[k, 0] = dot(nbt[...], d_upper).astype(bfloat).reshape(2, 2, 2, 96, 384)
        ff_tags[k, 0] = send(rff.at[k, :, :, :, 1 - core], f1.at[k], core_dev)
        part = dot_nt(d_upper, gup[w].reshape(768, 384))
        if k == 1:
            dn[...] = part
        else:
            dn[...] += part

    def ff_y(k):
        arrive(f1.at[k], ff_tags[k, 0], core_dev)
        f1[k] = f1[k] + rff[k, :, :, :, core]
        ff_tags[k, 1] = send(f1.at[k, :, :, 1 - y], f2.at[k], y_dev)

    def ff_z(k):
        arrive(f2.at[k], ff_tags[k, 1], y_dev)
        if k:
            ft[k - 1] = f1[k, :, :, y] + f2[k]
            ff_tags[k, 2] = send(ft.at[k - 1], f3.at[k - 1], z_dev[k])

    def ff_end():
        total = f1[0, :, :, y].astype(single) + f2[0].astype(single)
        for k in range(1, N_HID):
            arrive(f3.at[k - 1], ff_tags[k, 2], z_dev[k])
            total = total + f3[k - 1].astype(single)
        r.g_up[...] = total[0].reshape(192, 384)
        r.g_down[...] = total[1].reshape(192, 384)
        store("g_up")
        store("g_down")

    ff_block(1)
    ff_y(1)
    ff_block(2)
    ff_y(2)
    for k in range(1, N_HID):
        arrive(al.at[h, dp, z_down[k]], tag_al[k - 1], z_dev[k])
    tag_ag = [send(al.at[h, dp], al.at[h, dp], device) for device in group_dev]
    ff_block(3)
    ff_y(3)
    ff_block(0)
    ff_y(0)

    rout, o1, o2, ot, o3 = r.rout, r.o1, r.o2, r.ot, r.o3
    pieces = [
        jnp.concatenate([db2[:, d * 96 : d * 96 + 96], db2[:, 384 + d * 96 : 384 + d * 96 + 96]], axis=1)
        for d in range(4)
    ]
    hot = hof[...].T
    d_heads = None
    for d in range(4):
        rout[:, d // 2, d % 2] = jnp.zeros((N_HID, 96, 256), bfloat)
        rout[:, d // 2, d % 2, :, 0:192] = dot(hot, pieces[d]).astype(bfloat).reshape(N_HID, 96, 192)
        part = dot_nt(pieces[d], gout[d].reshape(384, 256)[:, 0:192])
        d_heads = part if d_heads is None else d_heads + part
    tag_o1 = send(rout.at[:, :, 1 - core], o1, core_dev)
    dh = r.dh
    for n in range(6):
        part = d_heads[:, n * HD : (n + 1) * HD].astype(bfloat)
        dh[2 * n] = part[0:ROWS]
        dh[2 * n + 1] = part[ROWS : 2 * ROWS]
    ff_z(1)

    dq, dk, dv = ho, r.dk, r.dv

    def attend_back(n, carry):
        for i in (2 * n, 2 * n + 1):
            probs = pr[i]
            d_out = dh[i]
            d_probs = dot_nt(d_out, v_ref[i])
            dv[i] = dot_tn(probs.astype(bfloat), d_out)
            inner = jnp.sum(probs * d_probs, axis=-1, keepdims=True)
            d_scores = (probs * (d_probs - inner)).astype(bfloat)
            dq[i] = dot(d_scores, k_ref[i]) * HD ** (-0.5)
            dk[i] = dot_tn(d_scores, q_ref[i]) * HD ** (-0.5)
        return carry

    arrive(o1, tag_o1, core_dev)
    o1[...] = o1[...] + rout[:, :, core]
    tag_o2 = send(o1.at[:, 1 - y], o2, y_dev)
    lax.fori_loop(0, 3, attend_back, 0)
    ff_z(2)
    lax.fori_loop(3, 6, attend_back, 0)
    ff_z(3)

    rqkv, q1, q2, qt, q3 = r.rqkv, r.q1, r.q2, r.qt, r.q3
    gain_sums, dm = [], hb
    for c, (grads, kept, gain) in enumerate(
        ((dq, qn, q_gain), (dk, kn, k_gain), (dv, None, None))
    ):
        parts, sums = [], []
        for n in range(6):
            grad = jnp.concatenate([grads[2 * n], grads[2 * n + 1]], axis=0)
            if kept is not None:
                normed, scale = kept[n, :, 0:HD], kept[n, :, HD : HD + 1]
                sums.append(jnp.sum(grad * normed, axis=0, keepdims=True))
                grad = norm_back(normed, scale, grad * gain[:, n * HD : (n + 1) * HD])
            parts.append(grad)
        if sums:
            gain_sums.append(jnp.concatenate(sums, axis=1))
        dm[c] = jnp.concatenate(parts, axis=1).astype(bfloat)
        dn[...] += dot_nt(dm[c], gqkv[c].reshape(768, 384))
    dns, dnr = r.dns, r.dnr
    dns[...] = dn[ROWS : 2 * ROWS, :].astype(bfloat)
    tag_dn = send(dns, dnr, x_dev)
    for c in range(3):
        rqkv[c] = dot(nbt[...], dm[c]).astype(bfloat).reshape(2, 2, 2, 2, 48, 384)
    tag_q1 = send(rqkv.at[:, :, :, 1 - core], q1, core_dev)
    ff_z(0)
    arrive(q1, tag_q1, core_dev)
    q1[...] = q1[...] + rqkv[:, :, :, core]
    tag_q2 = send(q1.at[:, :, 1 - y], q2, y_dev)
    arrive(o2, tag_o2, y_dev)
    ot[...] = o1[:, y] + o2[...]
    tag_o3 = [send(ot.at[z_up[k]], o3.at[k - 1], z_dev[k]) for k in range(1, N_HID)]

    for i, (gh, gd) in enumerate(group):
        arrive(al.at[gh, gd], tag_ag[i], group_dev[i])
    rows_all = al[...].reshape(32, 8, 256)
    d_logits_all = jnp.concatenate([rows_all[:, q, :] for q in range(4)], axis=1)
    pooled_all = jnp.concatenate([rows_all[:, 4 + q, :] for q in range(3)], axis=1)
    start = ((h * 4 + dp) * N_HID + z) * 24
    chosen = (iota((24, 768), 1) == iota((24, 768), 0) + start).astype(bfloat)
    mine = dot_nt(chosen, pooled_all.astype(bfloat))
    g_head = jnp.dot(mine, d_logits_all, precision=highest, preferred_element_type=single)
    r.g_head[...] = g_head[:, 0:classes]
    store("g_head")

    arrive(dnr, tag_dn, x_dev)
    d_normed = dn[0:ROWS, :] + dnr[...].astype(single)
    block_n, block_scale = norm_parts(jnp.concatenate([st[0, 0], st[1, 0]], axis=1).astype(single))
    d_block_gain = jnp.sum(d_normed * block_n, axis=0, keepdims=True)
    d_in = ds[...] + norm_back(block_n, block_scale, d_normed * block_gain)
    dx, gg = r.dx, r.gg
    low, high = d_in[:, 0:384], d_in[:, 384:768]
    dx[0] = jnp.where(h == 0, low, high).astype(bfloat)
    dx[2] = jnp.where(h == 0, high, low).astype(bfloat)
    tag_dx = send(dx.at[2], dx.at[1], x_dev)

    def spread(row):
        blank = jnp.zeros((1, 192), single)
        halves = []
        for a in range(2):
            part = jnp.concatenate([row[:, a * 96 : a * 96 + 96], row[:, 192 + a * 96 : 288 + a * 96]], axis=1)
            halves.append(
                jnp.where(
                    h == 0,
                    jnp.concatenate([part, blank], axis=1),
                    jnp.concatenate([blank, part], axis=1),
                )
            )
        return jnp.concatenate(halves, axis=1)

    d_gains = jnp.concatenate(
        [d_block_gain, d_final_gain, spread(gain_sums[0]), spread(gain_sums[1]), jnp.zeros((4, 768), single)],
        axis=0,
    )
    low, high = d_gains[:, 0:384], d_gains[:, 384:768]
    gg[0] = jnp.where(h == 0, low, high)
    gg[2] = jnp.where(h == 0, high, low)
    tag_gg = send(gg.at[2], gg.at[1], x_dev)
    arrive(dx.at[1], tag_dx, x_dev)
    arrive(gg.at[1], tag_gg, x_dev)
    rext, e1, e2, et, e3 = r.rext, r.e1, r.e2, r.et, r.e3
    dxt = jnp.concatenate([dx[0].astype(single), dx[1].astype(single)], axis=0).T.astype(bfloat)
    px2 = px[...].reshape(2 * ROWS, 1024)
    d_gains = (gg[0] + gg[1]).astype(bfloat)
    x0[...] = dot(dxt, px2[:, 0:512])
    x1[...] = dot(dxt, px2[:, 512:1024]) + dot_tn(d_gains, rows_of.astype(bfloat))
    for d in range(4):
        for w in range(N_HID):
            s = (d * N_HID + w) * 24
            rext[d // 2, d % 2, w] = jnp.concatenate(
                [x0[s : s + 24, :], x1[s : s + 24, :]], axis=0
            ).astype(bfloat)
    tag_e1 = send(rext.at[:, 1 - core], e1, core_dev)
    arrive(q2, tag_q2, y_dev)
    qt[...] = q1[:, :, y] + q2[...]
    tag_q3 = [
        send(qt.at[:, z_up[k] // 2, lax.rem(z_up[k], 2)], q3.at[k - 1], z_dev[k])
        for k in range(1, N_HID)
    ]
    arrive(e1, tag_e1, core_dev)
    e1[...] = e1[...] + rext[:, core]
    tag_e2 = send(e1.at[1 - y], e2, y_dev)
    ff_end()
    total = ot[z].astype(single)
    for k in range(1, N_HID):
        arrive(o3.at[k - 1], tag_o3[k - 1], z_dev[k])
        total = total + o3[k - 1].astype(single)
    r.g_out[...] = total[:, 0:192]
    store("g_out")
    arrive(e2, tag_e2, y_dev)
    et[...] = e1[y] + e2[...]
    tag_e3 = [send(et.at[z_up[k]], e3.at[k - 1], z_dev[k]) for k in range(1, N_HID)]
    total = qt[:, z // 2, lax.rem(z, 2)].astype(single)
    for k in range(1, N_HID):
        arrive(q3.at[k - 1], tag_q3[k - 1], z_dev[k])
        total = total + q3[k - 1].astype(single)
    r.g_qkv[...] = total
    store("g_qkv")
    total = et[z].astype(single)
    for k in range(1, N_HID):
        arrive(e3.at[k - 1], tag_e3[k - 1], z_dev[k])
        total = total + e3[k - 1].astype(single)
    r.g_patch[:, 0:512] = total[0:24]
    r.g_patch[:, 512:768] = total[24:48, 0:256]
    r.g_table[...] = total[24:48, 256 : 256 + seq_len]
    columns = total[24:48, 256:512]
    pick_f = (iota((8, 256), 1) == iota((8, 256), 0) + seq_len).astype(single)
    r.g_gains[...] = dot_nt(pick_f, columns, precision=highest)[0:4]
    for name in ("g_patch", "g_table", "g_gains"):
        store(name)


    def read(prefix, kind):
        values = getattr(r, prefix + kind)[...]
        return values.reshape(-1, values.shape[-1])

    lane = iota((8, 128), 1)
    own = jnp.where(lane == 0, term, 0.0)
    grad_square = None
    for n, kind in enumerate(KINDS):
        value = square_sum(read("g_", kind))
        grad_square = value if grad_square is None else grad_square + value
        own = jnp.where(lane == 8 + n, square_sum(read("w_", kind)), own)
    own = jnp.where(lane == 1, grad_square, own)

    def all_sum(vector, line, every):
        line[z] = vector
        tags_z = [send(line.at[z], line.at[z], z_dev[k]) for k in range(1, N_HID)]
        for k in range(1, N_HID):
            arrive(line.at[z_down[k]], tags_z[k - 1], z_dev[k])
        every[h, dp] = (line[0] + line[1]) + (line[2] + line[3])
        tags_g = [send(every.at[h, dp], every.at[h, dp], device) for device in group_dev]
        for i, (gh, gd) in enumerate(group):
            arrive(every.at[gh, gd], tags_g[i], group_dev[i])
        total = None
        for a in range(2):
            for d in range(4):
                total = every[a, d] if total is None else total + every[a, d]
        return total

    sums = all_sum(own, r.l1, r.v1)
    grad_norm = jnp.sqrt(jnp.sum(jnp.where(lane == 1, sums, 0.0), axis=1, keepdims=True))[0:1]
    clip = jnp.minimum(1.0, clip_at / grad_norm)
    own = jnp.zeros((8, 128), single)
    for name in order[9:]:
        loads[name].wait()
    for n, kind in enumerate(KINDS):
        update = one_update(read("w_", kind), read("m_", kind), read("v_", kind), read("g_", kind), clip)[2]
        own = jnp.where(lane == 8 + n, square_sum(update), own)
    updates = all_sum(own, r.l2, r.v2)
    result = jnp.sqrt(sums) / jnp.sqrt(updates)
    result = jnp.where(lane == 0, sums, result)
    result = jnp.where(lane == 1, grad_norm, result)
    result = jnp.where(lane == 2, clip, result)
    r.scalars[...] = result
    store("scalars")
    for copy in stores:
        copy.wait()
    for key, copies in sends.items():

        def settle(copies=copies):
            for copy in copies:
                copy.wait_send()

        if key is None:
            settle()
        else:
            pl.when(holds[key])(settle)


def write_kernel(names, *refs):
    r = types.SimpleNamespace(**dict(zip(names, refs)))
    lane = iota((8, 128), 1)
    inputs = ["scalars"] + [p + k for k in KINDS for p in ("w_", "m_", "v_", "g_")]
    loads = {}
    for number, name in enumerate(inputs):
        loads[name] = pltpu.make_async_copy(
            getattr(r, "h_" + name), getattr(r, name), r.lsem.at[number]
        )
        loads[name].start()
    loads["scalars"].wait()

    def pick(n):
        return jnp.sum(jnp.where(lane == n, r.scalars[...], 0.0), axis=1, keepdims=True)[0:1]

    clip = pick(2)
    stores = []
    for n, kind in enumerate(KINDS):
        for p in ("w_", "m_", "v_", "g_"):
            loads[p + kind].wait()
        master = getattr(r, "w_" + kind)[...]
        grad = getattr(r, "g_" + kind)[...]
        ratio, c = pick(8 + n), clip
        if len(master.shape) == 3:
            c, ratio = clip[None], ratio[None]
        first, second, update = one_update(
            master, getattr(r, "m_" + kind)[...], getattr(r, "v_" + kind)[...], grad, c
        )
        results = (first, second, master - learn_rate * ratio * update)
        for p, value in zip(("nm_", "nv_", "nw_"), results):
            getattr(r, p + kind)[...] = value
            copy = pltpu.make_async_copy(
                getattr(r, p + kind),
                getattr(r, "h_" + p + kind),
                r.lsem.at[len(inputs) + len(stores)],
            )
            copy.start()
            stores.append(copy)
    for copy in stores:
        copy.wait()


def fast_device(patches, labels, *state):
    bfloat, single = jnp.bfloat16, jnp.float32

    def turn(kind, value):
        if kind in ("patch", "table", "down"):
            return value.T
        if kind == "qkv":
            return value.transpose(1, 0, 2)
        return value

    flat = [turn(KINDS[i % 8], value) for i, value in enumerate(state)]
    hbm = pl.BlockSpec(memory_space=pl.ANY)
    smem = pl.BlockSpec(memory_space=pltpu.SMEM)
    in_names = ["patches"] + [p + k for p in ("w_", "m_", "v_") for k in KINDS]
    out_names = ["g_" + k for k in KINDS] + ["scalars"]
    scratch = dict(
        px=((2, ROWS, 1024), bfloat),
        gext=((4, 4, 48, 512), bfloat),
        gqkv=((3, 2, 4, 2, 48, 384), bfloat),
        gout=((4, 4, 96, 256), bfloat),
        gup=((4, 2, 4, 96, 384), bfloat),
        gdn=((4, 2, 4, 96, 384), bfloat),
        ghd=((2, 4, 4, 48, 512), bfloat),
        x0=((384, 512), single),
        x1=((384, 512), single),
        hw=((2, 768, 512), bfloat),
        ga=((2, 8, 384), single),
        st=((2, 2, ROWS, 384), bfloat),
        nb=((2 * ROWS, 768), bfloat),
        nbt=((768, 2 * ROWS), bfloat),
        qn=((6, 2 * ROWS, 2 * HD), single),
        kn=((6, 2 * ROWS, 2 * HD), single),
        q=((12, ROWS, HD), bfloat),
        k=((12, ROWS, HD), bfloat),
        v=((12, ROWS, HD), bfloat),
        pr=((12, ROWS, ROWS), single),
        ho=((12, ROWS, HD), single),
        hof=((2 * ROWS, 384), bfloat),
        us=((4, 2 * ROWS, 384), single),
        hb=((4, 2 * ROWS, 384), bfloat),
        br=((2 * ROWS, 768), single),
        brs=((2, 2, ROWS, 384), bfloat),
        brr=((2, 2, ROWS, 384), bfloat),
        rw=((2, 8, 768), single),
        ds=((ROWS, 768), single),
        db=((2, ROWS, 768), bfloat),
        dbt=((768, 2 * ROWS), bfloat),
        al=((2, 4, 4, 8, 256), single),
        rff=((4, 2, 2, 2, 2, 96, 384), bfloat),
        f1=((4, 2, 2, 2, 96, 384), bfloat),
        f2=((4, 2, 2, 96, 384), bfloat),
        ft=((3, 2, 2, 96, 384), bfloat),
        f3=((3, 2, 2, 96, 384), bfloat),
        rout=((4, 2, 2, 96, 256), bfloat),
        o1=((4, 2, 96, 256), bfloat),
        o2=((4, 96, 256), bfloat),
        ot=((4, 96, 256), bfloat),
        o3=((3, 96, 256), bfloat),
        dh=((12, ROWS, HD), bfloat),
        dk=((12, ROWS, HD), single),
        dv=((12, ROWS, HD), single),
        rqkv=((3, 2, 2, 2, 2, 48, 384), bfloat),
        q1=((3, 2, 2, 2, 48, 384), bfloat),
        q2=((3, 2, 2, 48, 384), bfloat),
        qt=((3, 2, 2, 48, 384), bfloat),
        q3=((3, 3, 48, 384), bfloat),
        dns=((ROWS, 768), bfloat),
        dnr=((ROWS, 768), bfloat),
        dx=((3, ROWS, 384), bfloat),
        gg=((3, 8, 384), single),
        rext=((2, 2, 4, 48, 512), bfloat),
        e1=((2, 4, 48, 512), bfloat),
        e2=((4, 48, 512), bfloat),
        et=((4, 48, 512), bfloat),
        e3=((3, 48, 512), bfloat),
        l1=((4, 8, 128), single),
        l2=((4, 8, 128), single),
        v1=((2, 4, 8, 128), single),
        v2=((2, 4, 8, 128), single),
    )
    semaphores = 256
    shapes = [flat[i].shape for i in range(8)]
    npatch, seq_len, classes = patches.shape[1], flat[1].shape[1], flat[3].shape[1]
    total_images = labels.shape[0] * lax.axis_size("dp")
    sizes = (npatch, seq_len, classes, total_images)
    held = [(patches.shape, bfloat)] + [(s, single) for s in shapes * 4] + [((8, 128), single)]
    names = ["labels"] + ["h_" + n for n in in_names + out_names] + in_names + out_names
    names += list(scratch) + ["ssem", "rsem", "lsem"]
    found = pl.pallas_call(
        functools.partial(step_kernel, sizes, names),
        out_shape=[jax.ShapeDtypeStruct(s, single) for s in shapes]
        + [jax.ShapeDtypeStruct((8, 128), single)],
        in_specs=[smem] + [hbm] * 25,
        out_specs=[hbm] * 9,
        scratch_shapes=[pltpu.VMEM(s, t) for s, t in held + list(scratch.values())]
        + [pltpu.SemaphoreType.DMA((semaphores,))] * 2
        + [pltpu.SemaphoreType.DMA((len(held),))],
        compiler_params=pltpu.CompilerParams(
            collective_id=0, has_side_effects=True, vmem_limit_bytes=62 * 2**20
        ),
        name="train_step",
    )(labels, patches, *flat)
    grads, scalars = found[:8], found[8]
    in_names = ["scalars"] + [p + k for p in ("w_", "m_", "v_", "g_") for k in KINDS]
    out_names = [p + k for p in ("nm_", "nv_", "nw_") for k in KINDS]
    held = [((8, 128), single)] + [(s, single) for s in shapes * 7]
    names = ["h_" + n for n in in_names + out_names] + in_names + out_names + ["lsem"]
    written = pl.pallas_call(
        functools.partial(write_kernel, names),
        out_shape=[jax.ShapeDtypeStruct(s, single) for s in shapes * 3],
        in_specs=[hbm] * 33,
        out_specs=[hbm] * 24,
        scratch_shapes=[pltpu.VMEM(s, t) for s, t in held]
        + [pltpu.SemaphoreType.DMA((len(held),))],
        compiler_params=pltpu.CompilerParams(vmem_limit_bytes=62 * 2**20),
        name="write_step",
    )(scalars, *flat, *grads)
    back = [turn(KINDS[i % 8], value) for i, value in enumerate(written)]
    return (scalars[0, 0], scalars[0, 1], *back)


def fits(mesh):
    return tuple(mesh.shape[a] for a in ALL) == (4, 2, N_HID)


def solution(mesh):
    placed = (
        P(ALL, None, None),
        P("dp"),
        P(None, ALL),
        P(None, ALL),
        P(None, ALL),
        P(ALL, None),
        P(DATA, None, "heads"),
        P(MODEL, "dp"),
        P("dp", MODEL),
        P(MODEL, "dp"),
        P(None, ALL),
        P(None, ALL),
        P(None, ALL),
        P(ALL, None),
        P(DATA, None, "heads"),
        P(MODEL, "dp"),
        P("dp", MODEL),
        P(MODEL, "dp"),
        P(None, ALL),
        P(None, ALL),
        P(None, ALL),
        P(ALL, None),
        P(DATA, None, "heads"),
        P(MODEL, "dp"),
        P("dp", MODEL),
        P(MODEL, "dp"),
    )
    return jax.shard_map(
        fast_device if fits(mesh) else per_device,
        mesh=mesh,
        in_specs=placed,
        out_specs=(
            P(),
            P(),
            P(None, ALL),
            P(None, ALL),
            P(None, ALL),
            P(ALL, None),
            P(DATA, None, "heads"),
            P(MODEL, "dp"),
            P("dp", MODEL),
            P(MODEL, "dp"),
            P(None, ALL),
            P(None, ALL),
            P(None, ALL),
            P(ALL, None),
            P(DATA, None, "heads"),
            P(MODEL, "dp"),
            P("dp", MODEL),
            P(MODEL, "dp"),
            P(None, ALL),
            P(None, ALL),
            P(None, ALL),
            P(ALL, None),
            P(DATA, None, "heads"),
            P(MODEL, "dp"),
            P("dp", MODEL),
            P(MODEL, "dp"),
        ),
        check_vma=False,
    )
```

```python
import functools
import types

import jax
import jax.numpy as jnp
from jax import lax
from jax.experimental import pallas as pl
from jax.experimental.pallas import tpu as pltpu
from jax.sharding import PartitionSpec as P

HD = 64
PD = 768
STEP = 10
MESH = pl.DeviceIdType.MESH
ALL = ("dp", "heads", "hidden")
DATA = ("dp", "hidden")
MODEL = ("heads", "hidden")


beta_one = 0.9
beta_two = 0.999
adam_eps = 1e-08
decay_rate = 0.01
learn_rate = 0.5
clip_at = 0.001
norm_eps = 1e-06
highest = lax.Precision.HIGHEST


def layer_norm(values):
    center = values - jnp.mean(values, axis=-1, keepdims=True)
    return center * lax.rsqrt(jnp.mean(center * center, axis=-1, keepdims=True) + norm_eps)


def head_loss(stream_out, targets, final_gain, head_weight, npatch, total_images):
    normed_out, norm_back = jax.vjp(layer_norm, stream_out)
    final = normed_out * final_gain
    pooled_b = jnp.mean(final[:, :npatch], axis=1).astype(jnp.bfloat16)
    logits = jnp.dot(pooled_b, head_weight, preferred_element_type=jnp.float32)
    log_total = jax.nn.logsumexp(logits, axis=-1)
    onehot = (targets[:, None] == lax.broadcasted_iota(jnp.int32, logits.shape, 1)).astype(
        jnp.float32
    )
    terms = log_total - jnp.sum(logits * onehot, axis=-1)
    d_logits = (jnp.exp(logits - log_total[:, None]) - onehot) / total_images
    d_pooled = jnp.dot(d_logits, head_weight.astype(jnp.float32).T, precision=highest)
    count, seq_len, width = stream_out.shape
    spread = jnp.broadcast_to(d_pooled[:, None, :] / npatch, (count, npatch, width))
    d_final = jnp.concatenate(
        [spread, jnp.zeros((count, seq_len - npatch, width), jnp.float32)], axis=1
    )
    d_stream = norm_back(d_final * final_gain)[0]
    d_gain_rows = jnp.sum(d_final * normed_out, axis=1)
    return (terms, pooled_b, d_logits, d_stream, d_gain_rows)


def per_device(
    patches,
    labels,
    w_patch,
    table,
    gains,
    w_head,
    w_qkv,
    w_out,
    w_up,
    w_down,
    first_patch,
    first_table,
    first_gains,
    first_head,
    first_qkv,
    first_out,
    first_up,
    first_down,
    second_patch,
    second_table,
    second_gains,
    second_head,
    second_qkv,
    second_out,
    second_up,
    second_down,
):
    masters = [w_patch, table, gains, w_head, w_qkv, w_out, w_up, w_down]
    firsts = [
        first_patch,
        first_table,
        first_gains,
        first_head,
        first_qkv,
        first_out,
        first_up,
        first_down,
    ]
    seconds = [
        second_patch,
        second_table,
        second_gains,
        second_head,
        second_qkv,
        second_out,
        second_up,
        second_down,
    ]
    bfloat = jnp.bfloat16
    single = jnp.float32
    patch_b, table_b, gains_b, head_b = (
        lax.all_gather(w_patch.astype(bfloat), ALL, axis=1, tiled=True),
        lax.all_gather(table.astype(bfloat), ALL, axis=1, tiled=True),
        lax.all_gather(gains.astype(bfloat), ALL, axis=1, tiled=True),
        lax.all_gather(w_head.astype(bfloat), ALL, axis=0, tiled=True),
    )
    qkv_b = lax.all_gather(w_qkv.astype(bfloat), DATA, axis=0, tiled=True)
    out_b, up_b, down_b = (
        lax.all_gather(w_out.astype(bfloat), "dp", axis=1, tiled=True),
        lax.all_gather(w_up.astype(bfloat), "dp", axis=0, tiled=True),
        lax.all_gather(w_down.astype(bfloat), "dp", axis=1, tiled=True),
    )
    gain_vals = gains_b.astype(single)
    table_vals = table_b.astype(single)
    n_hidden = lax.axis_size("hidden")
    n_own = patches.shape[0]
    npatch = patches.shape[1]
    seq_len = table_b.shape[0]
    width = patch_b.shape[1]
    group_width = qkv_b.shape[2]
    group_heads = group_width // HD
    own_index = lax.axis_index("heads") * n_hidden + lax.axis_index("hidden")
    total_images = labels.shape[0] * lax.axis_size("dp")
    embedded = jnp.dot(patches.reshape(n_own * npatch, PD), patch_b, preferred_element_type=single)
    embedded = embedded.reshape(n_own, npatch, width) + table_vals[:npatch]
    registers = jnp.broadcast_to(table_vals[npatch:], (n_own, seq_len - npatch, width))
    stream_own = jnp.concatenate([embedded, registers], axis=1).astype(bfloat)
    stream_in = lax.all_gather(stream_own, MODEL, axis=0, tiled=True)
    n_img = stream_in.shape[0]
    row_count = n_img * seq_len
    stream_flat = stream_in.astype(single).reshape(row_count, width)
    normed_b = (layer_norm(stream_flat) * gain_vals[0]).astype(bfloat)
    n_att = n_img // n_hidden
    att_start = lax.axis_index("hidden") * n_att
    normed_att = lax.dynamic_slice_in_dim(
        normed_b.reshape(n_img, seq_len, width), att_start, n_att, 0
    )
    query_gain = lax.dynamic_slice_in_dim(
        gain_vals[2], lax.axis_index("heads") * group_width, group_width, 0
    ).reshape(group_heads, HD)
    key_gain = lax.dynamic_slice_in_dim(
        gain_vals[3], lax.axis_index("heads") * group_width, group_width, 0
    ).reshape(group_heads, HD)
    mixed = jnp.einsum("bsd,dcf->bscf", normed_att, qkv_b, preferred_element_type=single)
    mixed = mixed.reshape(n_att, seq_len, 3, group_heads, HD)
    query_norm, query_back = jax.vjp(layer_norm, mixed[:, :, 0])
    key_norm, key_back = jax.vjp(layer_norm, mixed[:, :, 1])
    queries = (query_norm * query_gain).astype(bfloat)
    keys = (key_norm * key_gain).astype(bfloat)
    values = mixed[:, :, 2].astype(bfloat)
    scale = HD ** (-0.5)
    scores = jnp.einsum("bqhd,bkhd->bhqk", queries, keys, preferred_element_type=single) * scale
    probs = jax.nn.softmax(scores, axis=-1)
    probs_b = probs.astype(bfloat)
    heads_out = jnp.einsum("bhqk,bkhd->bqhd", probs_b, values, preferred_element_type=single)
    heads_out = heads_out.astype(bfloat).reshape(n_att * seq_len, group_width)
    columns = lax.all_to_all(heads_out, "hidden", split_axis=1, concat_axis=0, tiled=True)
    attn_part = jnp.dot(columns, out_b, preferred_element_type=single)
    upper = jnp.dot(normed_b, up_b, preferred_element_type=single)
    activated, gelu_back = jax.vjp(jax.nn.gelu, upper)
    activated_b = activated.astype(bfloat)
    partial_sum = attn_part + jnp.dot(activated_b, down_b, preferred_element_type=single)
    total = lax.psum(partial_sum, MODEL)
    stream_out = (stream_flat + total).reshape(n_img, seq_len, width)
    terms, pooled_b, d_logits, d_stream, d_gain_rows = head_loss(
        stream_out, labels, gain_vals[1], head_b, npatch, total_images
    )
    loss_terms = lax.dynamic_slice_in_dim(terms, own_index * n_own, n_own, 0)
    pooled_own = lax.dynamic_slice_in_dim(pooled_b, own_index * n_own, n_own, 0)
    logits_own = lax.dynamic_slice_in_dim(d_logits, own_index * n_own, n_own, 0)
    d_head = jnp.dot(pooled_own.astype(single).T, logits_own, precision=highest)
    d_final_gain = jnp.sum(
        lax.dynamic_slice_in_dim(d_gain_rows, own_index * n_own, n_own, 0), axis=0
    )
    d_stream_own = lax.dynamic_slice_in_dim(d_stream, own_index * n_own, n_own, 0)
    d_branch = d_stream.reshape(row_count, width).astype(bfloat)
    d_activated = jnp.dot(d_branch, down_b.T, preferred_element_type=single)
    d_upper = gelu_back(d_activated)[0].astype(bfloat)
    d_down = jnp.dot(activated_b.T, d_branch, preferred_element_type=single)
    d_up = jnp.dot(normed_b.T, d_upper, preferred_element_type=single)
    d_normed = jnp.dot(d_upper, up_b.T, preferred_element_type=single)
    d_out = jnp.dot(columns.T, d_branch, preferred_element_type=single)
    d_columns = jnp.dot(d_branch, out_b.T, preferred_element_type=single).astype(bfloat)
    d_heads = lax.all_to_all(d_columns, "hidden", split_axis=0, concat_axis=1, tiled=True).reshape(
        n_att, seq_len, group_heads, HD
    )
    d_probs = jnp.einsum("bqhd,bkhd->bhqk", d_heads, values, preferred_element_type=single)
    d_values = jnp.einsum("bhqk,bqhd->bkhd", probs_b, d_heads, preferred_element_type=single)
    d_scores = (probs * (d_probs - jnp.sum(probs * d_probs, axis=-1, keepdims=True))).astype(bfloat)
    d_query_norm = (
        jnp.einsum("bhqk,bkhd->bqhd", d_scores, keys, preferred_element_type=single) * scale
    )
    d_key_norm = (
        jnp.einsum("bhqk,bqhd->bkhd", d_scores, queries, preferred_element_type=single) * scale
    )
    d_queries = query_back(d_query_norm * query_gain)[0]
    d_keys = key_back(d_key_norm * key_gain)[0]
    d_query_gain = jnp.sum(d_query_norm * query_norm, axis=(0, 1)).reshape(group_width)
    d_key_gain = jnp.sum(d_key_norm * key_norm, axis=(0, 1)).reshape(group_width)
    d_mixed = (
        jnp.stack([d_queries, d_keys, d_values], axis=2)
        .astype(bfloat)
        .reshape(n_att, seq_len, 3, group_width)
    )
    d_qkv = jnp.einsum("bsd,bscf->dcf", normed_att, d_mixed, preferred_element_type=single)
    d_att_in = jnp.einsum("bscf,dcf->bsd", d_mixed, qkv_b, preferred_element_type=single)
    d_normed = d_normed.reshape(n_img, seq_len, width)
    d_normed = lax.dynamic_update_slice_in_dim(
        d_normed, lax.dynamic_slice_in_dim(d_normed, att_start, n_att, 0) + d_att_in, att_start, 0
    )
    d_normed_own = lax.psum_scatter(
        d_normed.reshape(row_count, width).astype(jnp.bfloat16),
        MODEL,
        scatter_dimension=0,
        tiled=True,
    ).astype(jnp.float32)
    d_normed_own = d_normed_own.reshape(n_own, seq_len, width)
    normed_own, block_back = jax.vjp(layer_norm, stream_own.astype(single))
    d_stream_in = d_stream_own + block_back(d_normed_own * gain_vals[0])[0]
    d_block_gain = jnp.sum(d_normed_own * normed_own, axis=(0, 1))
    d_patch = jnp.dot(
        patches.reshape(n_own * npatch, PD).astype(single).T,
        d_stream_in[:, :npatch].reshape(n_own * npatch, width),
        precision=highest,
    )
    d_table = jnp.sum(d_stream_in, axis=0)
    zero_row = jnp.zeros((width,), single)
    gain_offset = lax.axis_index("heads") * group_width
    d_gains = jnp.stack(
        [
            d_block_gain,
            d_final_gain,
            lax.dynamic_update_slice_in_dim(zero_row, d_query_gain, gain_offset, 0),
            lax.dynamic_update_slice_in_dim(zero_row, d_key_gain, gain_offset, 0),
        ]
    )
    grad_patch, grad_table, grad_gains, grad_head = (
        lax.psum_scatter(d_patch, ALL, scatter_dimension=1, tiled=True),
        lax.psum_scatter(d_table, ALL, scatter_dimension=1, tiled=True),
        lax.psum_scatter(d_gains, ALL, scatter_dimension=1, tiled=True),
        lax.psum_scatter(d_head, ALL, scatter_dimension=0, tiled=True),
    )
    grad_qkv = lax.psum_scatter(d_qkv, DATA, scatter_dimension=0, tiled=True)
    grad_out, grad_up, grad_down = (
        lax.psum_scatter(d_out.astype(jnp.bfloat16), "dp", scatter_dimension=1, tiled=True).astype(
            jnp.float32
        ),
        lax.psum_scatter(d_up.astype(jnp.bfloat16), "dp", scatter_dimension=0, tiled=True).astype(
            jnp.float32
        ),
        lax.psum_scatter(d_down.astype(jnp.bfloat16), "dp", scatter_dimension=1, tiled=True).astype(
            jnp.float32
        ),
    )
    grads = [grad_patch, grad_table, grad_gains, grad_head, grad_qkv, grad_out, grad_up, grad_down]
    grad_squares = jnp.stack([jnp.sum(grad * grad) for grad in grads])
    weight_squares = jnp.stack([jnp.sum(master * master) for master in masters])
    grad_squares, weight_squares, loss_sum = lax.psum(
        (grad_squares, weight_squares, jnp.sum(loss_terms)), ALL
    )
    grad_norm = jnp.sqrt(jnp.sum(grad_squares))
    clip = jnp.minimum(1.0, clip_at / grad_norm)
    new_firsts, new_seconds, updates = ([], [], [])
    for master, first, second, grad in zip(masters, firsts, seconds, grads):
        clipped = grad * clip
        first_new = beta_one * first + (1.0 - beta_one) * clipped
        second_new = beta_two * second + (1.0 - beta_two) * clipped * clipped
        update = (
            first_new
            / (1.0 - beta_one**STEP)
            / (jnp.sqrt(second_new / (1.0 - beta_two**STEP)) + adam_eps)
        )
        updates.append(update + decay_rate * master)
        new_firsts.append(first_new)
        new_seconds.append(second_new)
    update_squares = lax.psum(
        jnp.stack([jnp.sum(update * update) for update in updates]), ALL
    )
    ratios = jnp.sqrt(weight_squares) / jnp.sqrt(update_squares)
    new_weights = [
        master - learn_rate * ratios[number] * update
        for number, (master, update) in enumerate(zip(masters, updates))
    ]
    return (
        loss_sum,
        grad_norm,
        new_firsts[0],
        new_firsts[1],
        new_firsts[2],
        new_firsts[3],
        new_firsts[4],
        new_firsts[5],
        new_firsts[6],
        new_firsts[7],
        new_seconds[0],
        new_seconds[1],
        new_seconds[2],
        new_seconds[3],
        new_seconds[4],
        new_seconds[5],
        new_seconds[6],
        new_seconds[7],
        new_weights[0],
        new_weights[1],
        new_weights[2],
        new_weights[3],
        new_weights[4],
        new_weights[5],
        new_weights[6],
        new_weights[7],
    )


def dot(a, b):
    return jnp.dot(a, b, preferred_element_type=jnp.float32)


def dot_nt(a, b, precision=None):
    return lax.dot_general(
        a, b, (((1,), (1,)), ((), ())), precision=precision, preferred_element_type=jnp.float32
    )


def dot_tn(a, b, precision=None):
    return lax.dot_general(
        a, b, (((0,), (0,)), ((), ())), precision=precision, preferred_element_type=jnp.float32
    )


def norm_parts(values):
    center = values - jnp.mean(values, axis=-1, keepdims=True)
    scale = lax.rsqrt(jnp.mean(center * center, axis=-1, keepdims=True) + norm_eps)
    return center * scale, scale


def norm_back(normed, scale, grad):
    inner = jnp.mean(grad * normed, axis=-1, keepdims=True)
    return scale * (grad - jnp.mean(grad, axis=-1, keepdims=True) - normed * inner)


gelu_c = 0.7978845608028654


def gelu_tanh(u):
    return jnp.tanh(gelu_c * (u + 0.044715 * (u * u * u)))


def iota(shape, axis):
    return lax.broadcasted_iota(jnp.int32, shape, axis)


def one_update(master, first, second, grad, clip):
    clipped = grad * clip
    first_new = beta_one * first + (1.0 - beta_one) * clipped
    second_new = beta_two * second + (1.0 - beta_two) * clipped * clipped
    update = (
        first_new
        / (1.0 - beta_one**STEP)
        / (jnp.sqrt(second_new / (1.0 - beta_two**STEP)) + adam_eps)
    )
    return first_new, second_new, update + decay_rate * master


def square_sum(values):
    return jnp.sum(values * values, axis=(0, 1), keepdims=True)


KINDS = ("patch", "table", "gains", "head", "qkv", "out", "up", "down")
EXT, QKV, UP0, UP1, HEAD, OUT, DN0, DN1 = range(8)
LEFT, RIGHT, ON_LEFT, ON_RIGHT = "left", "right", "on_left", "on_right"
ROWS = 208
N_HID = 4


def step_kernel(sizes, names, *refs):
    npatch, seq_len, classes, total_images = sizes
    r = types.SimpleNamespace(**dict(zip(names, refs)))
    bfloat, single = jnp.bfloat16, jnp.float32
    dp, h, z = (lax.axis_index(a) for a in ALL)
    core, y = lax.rem(dp, 2), dp // 2
    y_dp, core_dp = (1 - y) * 2 + core, y * 2 + (1 - core)
    x_dev, y_dev, core_dev = (dp, 1 - h, z), (y_dp, h, z), (core_dp, h, z)
    z_up = [lax.rem(z + k, N_HID) for k in range(N_HID)]
    z_down = [lax.rem(z + N_HID - k, N_HID) for k in range(N_HID)]
    z_dev = [(dp, h, z_up[k]) for k in range(N_HID)]
    group = []
    for a in (0, 1):
        for b in (0, 1):
            for c in (0, 1):
                if a + b + c:
                    gh = 1 - h if a else h
                    gy = 1 - y if b else y
                    gc = 1 - core if c else core
                    group.append((gh, gy * 2 + gc))
    group_dev = [(gd, gh, z) for gh, gd in group]

    barrier = pltpu.get_barrier_semaphore()
    for device in z_dev[1:] + group_dev:
        pl.semaphore_signal(barrier, inc=1, device_id=device, device_id_type=MESH)

    loads = {}
    order = ["w_patch", "w_table", "w_gains", "patches"]
    order += [p + k for p in ("w_", "m_", "v_") for k in KINDS if p + k not in order]
    for number, name in enumerate(order):
        loads[name] = pltpu.make_async_copy(
            getattr(r, "h_" + name), getattr(r, name), r.lsem.at[number]
        )
        loads[name].start()
    stores = []

    def store(name):
        copy = pltpu.make_async_copy(
            getattr(r, name), getattr(r, "h_" + name), r.lsem.at[len(order) + len(stores)]
        )
        copy.start()
        stores.append(copy)

    ssem, rsem = r.ssem, r.rsem
    count = [0]
    sends = {}
    last = N_HID - 1
    holds = {}
    for d in range(1, N_HID):
        holds[LEFT, d] = z >= d
        holds[RIGHT, d] = z + d <= last
        holds[ON_RIGHT, d] = (z >= d) & (z < last)
        holds[ON_LEFT, d] = (z + d <= last) & (z > 0)
    holds[ON_RIGHT, 0] = z < last
    holds[ON_LEFT, 0] = z > 0
    next_z = {LEFT: (dp, h, z_up[1]), RIGHT: (dp, h, z_down[1])}

    def send(source, target, device, key=None):
        number = count[0]
        count[0] += 1
        copy = pltpu.make_async_remote_copy(
            src_ref=source,
            dst_ref=target,
            send_sem=ssem.at[number],
            recv_sem=rsem.at[number],
            device_id=device,
            device_id_type=MESH,
        )
        if key is None:
            copy.start()
        else:
            pl.when(holds[key])(copy.start)
        sends.setdefault(key, []).append(copy)
        return number

    def arrive(target, number, device):
        pltpu.make_async_remote_copy(
            src_ref=target,
            dst_ref=target,
            send_sem=ssem.at[number],
            recv_sem=rsem.at[number],
            device_id=device,
            device_id_type=MESH,
        ).wait_recv()

    gext, gqkv, gout, gup, gdn, ghd = r.gext, r.gqkv, r.gout, r.gup, r.gdn, r.ghd
    x0, x1, px = r.x0, r.x1, r.px
    kept = types.SimpleNamespace()

    def pack_ext():
        x1[0:24, :] = jnp.zeros((24, 512), single)
        for name in order[0:3]:
            loads[name].wait()
        x1[0:24, 256 : 256 + seq_len] = r.w_table[...]
        pick = (iota((4, 256), 1) == iota((4, 256), 0) + seq_len).astype(bfloat)
        table_part = x1[0:24, 256:512] + dot_tn(r.w_gains[...].astype(bfloat), pick)
        wp = r.w_patch[...]
        gext[dp, z] = jnp.concatenate(
            [wp[:, 0:512], jnp.concatenate([wp[:, 512:768], table_part], axis=1)], axis=0
        ).astype(bfloat)

    def pack_patches():
        row, col = iota((ROWS, 256), 0), iota((ROWS, 256), 1)
        spot = jnp.where((row == col) & (row < seq_len), 1.0, 0.0).astype(bfloat)
        px[0, :, 768:1024] = spot
        px[1, :, 768:1024] = spot
        px[0, ROWS - 16 : ROWS, 0:768] = jnp.zeros((16, 768), bfloat)
        loads["patches"].wait()
        px[0, 0:npatch, 0:768] = r.patches[0]

    def pack_qkv():
        loads["w_qkv"].wait()
        gqkv[:, z // 2, dp, lax.rem(z, 2)] = r.w_qkv[...].astype(bfloat)

    def pack_up():
        loads["w_up"].wait()
        gup[z, :, dp] = r.w_up[...].astype(bfloat).reshape(2, 96, 384)

    def pack_head():
        loads["w_head"].wait()
        x0[0:24, :] = r.w_head[:, 0:512]
        x1[0:24, :] = jnp.zeros((24, 512), single)
        x1[0:24, 0 : classes - 512] = r.w_head[:, 512:classes]
        ghd[h, dp, z] = jnp.concatenate([x0[0:24, :], x1[0:24, :]], axis=0).astype(bfloat)

    def pack_out():
        loads["w_out"].wait()
        gout[dp, z] = jnp.zeros((96, 256), bfloat)
        gout[dp, z, :, 0:192] = r.w_out[...].astype(bfloat)

    def pack_down():
        loads["w_down"].wait()
        gdn[z, :, dp] = r.w_down[...].astype(bfloat).reshape(2, 96, 384)

    def at_ext(d, w):
        return gext.at[d, w]

    def at_qkv(d, w):
        return gqkv.at[:, w // 2, d, lax.rem(w, 2)]

    def at_out(d, w):
        return gout.at[d, w]

    def at_up(half):
        return lambda d, w: gup.at[w, half, d]

    def at_dn(half):
        return lambda d, w: gdn.at[w, half, d]

    def at_hd(d, w):
        return ghd.at[h, d, w]

    slot = {
        EXT: at_ext,
        QKV: at_qkv,
        OUT: at_out,
        UP0: at_up(0),
        UP1: at_up(1),
        DN0: at_dn(0),
        DN1: at_dn(1),
        HEAD: at_hd,
    }
    lines = {
        EXT: lambda d: gext.at[d],
        QKV: lambda d: gqkv.at[:, :, d],
        OUT: lambda d: gout.at[d],
        UP0: lambda d: gup.at[:, 0, d],
        UP1: lambda d: gup.at[:, 1, d],
        DN0: lambda d: gdn.at[:, 0, d],
        DN1: lambda d: gdn.at[:, 1, d],
        HEAD: lambda d: ghd.at[h, d],
    }
    tags = {}

    def own_z(name):
        own = slot[name](dp, z)
        tags[name, LEFT, 1] = send(own, own, next_z[LEFT], (ON_RIGHT, 0))
        tags[name, RIGHT, 1] = send(own, own, next_z[RIGHT], (ON_LEFT, 0))

    def own_y(name):
        own = slot[name](dp, z)
        tags[name, "y", 0] = send(own, own, y_dev)

    def pass_z(name, d):
        for side, on, theirs in ((LEFT, ON_RIGHT, z_down[d]), (RIGHT, ON_LEFT, z_up[d])):
            block = slot[name](dp, theirs)
            number = tags[name, side, d]
            pl.when(holds[side, d])(functools.partial(arrive, block, number, y_dev))
            if d < last:
                tags[name, side, d + 1] = send(block, block, next_z[side], (on, d))
            tags[name, "y", side, d] = send(block, block, y_dev, (side, d))
        if d == last and name != HEAD:
            line = lines[name](dp)
            tags[name, "c", 0] = send(line, line, core_dev)

    def pass_core(name):
        at = slot[name]
        arrive(at(y_dp, z), tags[name, "y", 0], y_dev)
        for d in range(1, N_HID):
            for side, theirs in ((LEFT, z_down[d]), (RIGHT, z_up[d])):
                number = tags[name, "y", side, d]
                pl.when(holds[side, d])(functools.partial(arrive, at(y_dp, theirs), number, y_dev))
        line = lines[name](y_dp)
        if name != HEAD:
            tags[name, "c", 1] = send(line, line, core_dev)
        else:
            own = lines[name](dp)
            tags[name, "x", 0] = send(own, own, x_dev)
            tags[name, "x", 1] = send(line, line, x_dev)

    def complete(name):
        far = (1 - y) * 2 + (1 - core)
        arrive(lines[name](core_dp), tags[name, "c", 0], core_dev)
        arrive(lines[name](far), tags[name, "c", 1], core_dev)

    def head_core():
        for i, d in enumerate((dp, y_dp)):
            arrive(ghd.at[1 - h, d], tags[HEAD, "x", i], x_dev)
        for i, d in enumerate((dp, y_dp)):
            block = ghd.at[:, d]
            tags[HEAD, "c", i] = send(block, block, core_dev)

    def head_complete():
        far = (1 - y) * 2 + (1 - core)
        for i, d in enumerate((core_dp, far)):
            arrive(ghd.at[:, d], tags[HEAD, "c", i], core_dev)

    def send_images():
        images = px.at[0, :, pl.ds(0, 768)]
        tags["px"] = send(images, px.at[1, :, pl.ds(0, 768)], x_dev)

    ga, st = r.ga, r.st
    rows_of = (iota((8, 512), 1) == iota((8, 512), 0) + (256 + seq_len)) & (iota((8, 512), 0) < 4)

    def unpack(block_of, low, high):
        for d in range(4):
            for w in range(N_HID):
                s = (d * N_HID + w) * 24
                block = block_of(d, w).astype(single)
                low[s : s + 24, :] = block[0:24]
                high[s : s + 24, :] = block[24:48]

    def embed(i):
        if i == 0:
            unpack(lambda d, w: gext[d, w], x0, x1)
            ga[h] = dot_nt(rows_of.astype(bfloat), x1[...].astype(bfloat))
            tags["ga"] = send(ga.at[h], ga.at[h], x_dev)
        else:
            arrive(px.at[1, :, pl.ds(0, 768)], tags["px"], x_dev)
        low, high = x0[...].astype(bfloat), x1[...].astype(bfloat)
        made = dot_nt(px[i, :, 0:512], low) + dot_nt(px[i, :, 512:1024], high)
        st[h, i] = made.astype(bfloat)
        tags["st", i] = send(st.at[h, i], st.at[h, 1 - i], x_dev)

    def gain_row(i):
        return jnp.concatenate([ga[0, i : i + 1, :], ga[1, i : i + 1, :]], axis=1)

    def head_gain(i):
        pieces = []
        both = [ga[0, i : i + 1, :], ga[1, i : i + 1, :]]
        for d in range(4):
            pieces.extend(half[:, d * 96 : d * 96 + 96] for half in both)
        low = jnp.concatenate(pieces[0:4], axis=1)
        high = jnp.concatenate(pieces[4:8], axis=1)
        return jnp.where(h == 0, low, high)

    nb, nbt = r.nb, r.nbt

    def block_norm():
        arrive(ga.at[1 - h], tags["ga"], x_dev)
        arrive(st.at[1 - h, 1], tags["st", 0], x_dev)
        arrive(st.at[1 - h, 0], tags["st", 1], x_dev)
        gain = gain_row(0)
        for i in range(2):
            stream = jnp.concatenate([st[0, i], st[1, i]], axis=1).astype(single)
            nb[i * ROWS : (i + 1) * ROWS, :] = (norm_parts(stream)[0] * gain).astype(bfloat)

    nq, sq, bd = r.nq, r.sq, r.bd
    q_ref, k_ref, v_ref = r.q, r.k, r.v

    def head_mean(values):
        return dot(values.astype(bfloat), bd[...])

    def project(c):
        mixed = dot(nb[...], gqkv[c].reshape(768, 384))
        if c == 0:
            same = iota((384, 384), 0) // HD == iota((384, 384), 1) // HD
            bd[...] = jnp.where(same, 1.0 / HD, 0.0).astype(bfloat)
        if c < 2:
            top = mixed.astype(bfloat).astype(single)
            center = mixed - (head_mean(top) + head_mean(mixed - top))
            scale = lax.rsqrt(head_mean(center * center) + norm_eps)
            normed = center * scale
            nq[c] = normed
            sq[c] = scale
            mixed = normed * head_gain(2 + c)
        out = (q_ref, k_ref, v_ref)[c]
        mixed = mixed.astype(bfloat)
        for n in range(6):
            part = mixed[:, n * HD : (n + 1) * HD]
            out[2 * n] = part[0:ROWS]
            out[2 * n + 1] = part[ROWS : 2 * ROWS]

    pr, hof = r.pr, r.hof
    dead = iota((ROWS, ROWS), 1) >= seq_len

    def attend(pair, carry):
        for i in range(2):
            made = []
            for side in range(2):
                n = 4 * pair + 2 * side + i
                scores = dot_nt(q_ref[n], k_ref[n]) * HD ** (-0.5)
                scores = jnp.where(dead, -1e30, scores)
                scores = scores - jnp.max(scores, axis=-1, keepdims=True)
                weights = jnp.exp(scores)
                probs = weights / jnp.sum(weights, axis=-1, keepdims=True)
                pr[n] = probs
                made.append(dot(probs.astype(bfloat), v_ref[n]))
            both = jnp.concatenate(made, axis=1).astype(bfloat)
            hof[i * ROWS : (i + 1) * ROWS, pl.ds(pl.multiple_of(pair * 128, 128), 128)] = both
        return carry

    us, hb, br = r.us, r.hb, r.br

    def rise(w, carry):
        upper = dot(nb[...], gup[w].reshape(768, 384))
        us[w] = upper
        hb[w] = (0.5 * upper * (1.0 + gelu_tanh(upper))).astype(bfloat)
        return carry

    def project_out():
        lefts, rights = [], []
        for d in range(4):
            part = dot(hof[...], gout[d].reshape(384, 256))
            lefts.append(part[:, 0:96])
            rights.append(part[:, 96:192])
        br[:, 0:384] = jnp.concatenate(lefts, axis=1)
        br[:, 384:768] = jnp.concatenate(rights, axis=1)

    def turn_normed():
        nbt[...] = nb[...].T

    brs, brr = r.brs, r.brr

    def fall(half):
        lanes = slice(half * 384, half * 384 + 384)

        def add(w, carry):
            br[:, lanes] += dot_nt(hb[w], gdn[w, half].reshape(384, 384))
            return carry

        lax.fori_loop(0, N_HID, add, 0)

    def share(half, i):
        lanes = slice(half * 384, half * 384 + 384)
        brs[half, i] = br[i * ROWS : (i + 1) * ROWS, lanes].astype(bfloat)
        tags["br", half, i] = send(brs.at[half, i], brr.at[half, 1 - i], x_dev)

    hw = r.hw

    def unpack_head():
        for a in range(2):
            unpack(lambda d, w: ghd[a, d, w], x0, x1)
            hw[0, a * 384 : a * 384 + 384, :] = x0[...].astype(bfloat)
            hw[1, a * 384 : a * 384 + 384, :] = x1[...].astype(bfloat)

    def stream_out(i):
        for half in range(2):
            arrive(brr.at[half, i], tags["br", half, 1 - i], x_dev)
        stream = jnp.concatenate([st[0, i], st[1, i]], axis=1).astype(single)
        theirs = jnp.concatenate([brr[0, i], brr[1, i]], axis=1).astype(single)
        return norm_parts(stream + (br[i * ROWS : (i + 1) * ROWS, :] + theirs))

    pl.semaphore_wait(barrier, len(z_dev) - 1 + len(group_dev))
    pack_qkv()
    own_y(QKV)
    own_z(QKV)
    pack_head()
    pack_ext()
    own_y(HEAD)
    own_z(EXT)
    pack_up()
    own_y(UP0)
    pack_patches()
    own_y(EXT)
    send_images()
    own_z(HEAD)
    pass_z(EXT, 1)
    pack_down()
    own_y(DN1)
    own_z(UP0)
    pack_out()
    pass_z(EXT, 2)
    pass_z(HEAD, 1)
    pass_z(EXT, 3)
    pass_z(QKV, 1)
    own_z(OUT)
    pass_core(EXT)
    pass_z(QKV, 2)
    complete(EXT)
    embed(0)
    embed(1)
    own_y(OUT)
    pass_z(OUT, 1)
    own_z(UP1)
    pass_z(QKV, 3)
    pass_z(OUT, 2)
    pass_z(UP0, 1)
    own_y(UP1)
    pass_z(UP1, 1)
    pass_z(HEAD, 2)
    pass_z(OUT, 3)
    own_z(DN0)
    own_z(DN1)
    pass_core(QKV)
    pass_z(UP0, 2)
    block_norm()
    pass_z(UP1, 2)
    complete(QKV)
    project(0)
    project(1)
    project(2)
    pass_z(HEAD, 3)
    lax.fori_loop(0, 1, attend, 0)
    pass_z(UP0, 3)
    pass_z(DN1, 1)
    pass_core(OUT)
    lax.fori_loop(1, 2, attend, 0)
    complete(OUT)
    pass_z(UP1, 3)
    pass_z(DN1, 2)
    pass_core(HEAD)
    pass_core(UP0)
    lax.fori_loop(2, 3, attend, 0)
    pass_z(DN1, 3)
    pass_z(DN0, 1)
    complete(UP0)
    pass_core(UP1)
    project_out()
    complete(UP1)
    lax.fori_loop(0, 2, rise, 0)
    pass_z(DN0, 2)
    pass_core(DN1)
    lax.fori_loop(2, 4, rise, 0)
    complete(DN1)
    fall(1)
    share(1, 1)
    share(1, 0)
    own_y(DN0)
    pass_z(DN0, 3)
    pass_core(DN0)
    complete(DN0)
    fall(0)
    share(0, 1)
    share(0, 0)
    turn_normed()
    head_core()
    head_complete()
    unpack_head()
    block_gain, q_gain, k_gain = gain_row(0), head_gain(2), head_gain(3)

    out_n, out_scale = stream_out(0)
    is_patch = iota((ROWS, 1), 0) < npatch
    final_gain = gain_row(1)
    n_sum = jnp.sum(jnp.where(is_patch, out_n, 0.0), axis=0, keepdims=True)
    pooled = n_sum * final_gain / npatch
    pooled_b = pooled.astype(bfloat)
    heads_b = [hw[0], hw[1]]
    pooled_8 = jnp.broadcast_to(pooled_b, (16, 768))
    logits = jnp.concatenate([dot(pooled_8, m)[0:1] for m in heads_b], axis=1)
    lane = iota((1, 1024), 1)
    logits = jnp.where(lane < classes, logits, -1e30)
    top = jnp.max(logits, axis=-1, keepdims=True)
    log_total = top + jnp.log(jnp.sum(jnp.exp(logits - top), axis=-1, keepdims=True))
    onehot = jnp.where(lane == r.labels[h * N_HID + z], 1.0, 0.0)
    term = log_total - jnp.sum(jnp.where(lane < classes, logits, 0.0) * onehot, axis=-1, keepdims=True)
    d_logits = (jnp.exp(logits - log_total) - onehot) / total_images
    hi = d_logits.astype(bfloat).astype(single)
    both = jnp.concatenate([hi, d_logits - hi, jnp.zeros((14, 1024), single)], axis=0).astype(bfloat)
    back = dot_nt(both[:, 0:512], heads_b[0]) + dot_nt(both[:, 512:1024], heads_b[1])
    d_pooled = (back[0:1] + back[1:2]) / npatch
    d_row = d_pooled * final_gain
    rw = r.rw
    rw[0] = jnp.broadcast_to(d_row, (8, 768))
    tag_rw = send(rw.at[0], rw.at[1], x_dev)
    ds, db, dbt = r.ds, r.db, r.dbt
    d_stream = jnp.where(is_patch, norm_back(out_n, out_scale, d_row), 0.0)
    ds[...] = d_stream
    db[0] = d_stream.astype(bfloat)
    dbt[:, 0:ROWS] = d_stream.T.astype(bfloat)
    d_final_gain = d_pooled * n_sum
    al = r.al
    pooled_f = pooled_b.astype(single)
    al[h, dp, z] = jnp.concatenate(
        [d_logits[:, q * 256 : q * 256 + 256] for q in range(4)]
        + [pooled_f[:, q * 256 : q * 256 + 256] for q in range(3)]
        + [jnp.zeros((1, 256), single)],
        axis=0,
    )
    tag_al = [send(al.at[h, dp, z], al.at[h, dp, z], z_dev[k]) for k in range(1, N_HID)]
    out_n, out_scale = stream_out(1)
    arrive(rw.at[1], tag_rw, x_dev)
    d_stream = jnp.where(is_patch, norm_back(out_n, out_scale, rw[1, 0:1, :]), 0.0)
    db[1] = d_stream.astype(bfloat)
    dbt[:, ROWS : 2 * ROWS] = d_stream.T.astype(bfloat)
    db2 = db[...].reshape(2 * ROWS, 768)

    rff, f1, f2, ft, f3 = r.rff, r.f1, r.f2, r.ft, r.f3
    dn, dm = br, r.dm
    kept = types.SimpleNamespace(fresh=True, gains=[])

    def add_in(part):
        if kept.fresh:
            dn[...] = part
        else:
            dn[...] += part
        kept.fresh = False

    def ff_send(m, k):
        tags["ff", m, k] = send(rff.at[k, m, :, :, 1 - core], f1.at[k, m], core_dev)

    def ff_down(k):
        rff[k, 0] = dot(dbt[...], hb[z_up[k]]).astype(bfloat).reshape(2, 2, 2, 96, 384)
        ff_send(0, k)

    def ff_up(k):
        w = z_up[k]
        upper = us[w]
        t = gelu_tanh(upper)
        slope = 0.5 * (1.0 + t) + 0.5 * upper * (1.0 - t * t) * gelu_c * (
            1.0 + 3 * 0.044715 * (upper * upper)
        )
        d_upper = (dot(db2, gdn[w].reshape(768, 384)) * slope).astype(bfloat)
        us[w] = d_upper.astype(single)
        rff[k, 1] = dot(nbt[...], d_upper).astype(bfloat).reshape(2, 2, 2, 96, 384)
        ff_send(1, k)

    def ff_in(k):
        w = z_up[k]
        add_in(dot_nt(us[w].astype(bfloat), gup[w].reshape(768, 384)))

    def ff_y(m, k):
        arrive(f1.at[k, m], tags["ff", m, k], core_dev)
        f1[k, m] = f1[k, m] + rff[k, m, :, :, core]
        tags["fy", m, k] = send(f1.at[k, m, :, 1 - y], f2.at[k, m], y_dev)

    def ff_z(m, k):
        arrive(f2.at[k, m], tags["fy", m, k], y_dev)
        if k:
            ft[k - 1, m] = f1[k, m, :, y] + f2[k, m]
            tags["fz", m, k] = send(ft.at[k - 1, m], f3.at[k - 1, m], z_dev[k])

    def ff_end():
        for m, name in enumerate(("g_down", "g_up")):
            total = f1[0, m, :, y].astype(single) + f2[0, m].astype(single)
            for k in range(1, N_HID):
                arrive(f3.at[k - 1, m], tags["fz", m, k], z_dev[k])
                total = total + f3[k - 1, m].astype(single)
            getattr(r, name)[...] = total.reshape(192, 384)
            store(name)

    def pass_rows():
        for k in range(1, N_HID):
            arrive(al.at[h, dp, z_down[k]], tag_al[k - 1], z_dev[k])
        tags["ag"] = [send(al.at[h, dp], al.at[h, dp], device) for device in group_dev]

    rout, o1, o2, ot, o3, pc = r.rout, r.o1, r.o2, r.ot, r.o3, r.pc

    def cut_branch():
        for d in range(4):
            low = db2[:, d * 96 : d * 96 + 96]
            high = db2[:, 384 + d * 96 : 384 + d * 96 + 96]
            pc[d] = jnp.concatenate([low, high], axis=1)

    def out_grad():
        hot = hof[...].T
        for d in range(4):
            rout[:, d // 2, d % 2] = jnp.zeros((N_HID, 96, 256), bfloat)
            grad = dot(hot, pc[d]).astype(bfloat).reshape(N_HID, 96, 192)
            rout[:, d // 2, d % 2, :, 0:192] = grad
        tags["o1"] = send(rout.at[:, :, 1 - core], o1, core_dev)

    dh = r.dh

    def out_back():
        d_heads = None
        for d in range(4):
            part = dot_nt(pc[d], gout[d].reshape(384, 256)[:, 0:192])
            d_heads = part if d_heads is None else d_heads + part
        d_heads = d_heads.astype(bfloat)
        for n in range(6):
            part = d_heads[:, n * HD : (n + 1) * HD]
            dh[2 * n] = part[0:ROWS]
            dh[2 * n + 1] = part[ROWS : 2 * ROWS]

    def out_y():
        arrive(o1, tags["o1"], core_dev)
        o1[...] = o1[...] + rout[:, :, core]
        tags["o2"] = send(o1.at[:, 1 - y], o2, y_dev)

    def out_z():
        arrive(o2, tags["o2"], y_dev)
        ot[...] = o1[:, y] + o2[...]
        tags["o3"] = [send(ot.at[z_up[k]], o3.at[k - 1], z_dev[k]) for k in range(1, N_HID)]

    def out_end():
        total = ot[z].astype(single)
        for k in range(1, N_HID):
            arrive(o3.at[k - 1], tags["o3"][k - 1], z_dev[k])
            total = total + o3[k - 1].astype(single)
        r.g_out[...] = total[:, 0:192]
        store("g_out")

    dqkv = r.dqkv

    def attend_back(pair, carry):
        for i in range(2):
            made = ([], [], [])
            for side in range(2):
                n = 4 * pair + 2 * side + i
                probs = pr[n]
                d_out = dh[n]
                d_probs = dot_nt(d_out, v_ref[n])
                inner = jnp.sum(probs * d_probs, axis=-1, keepdims=True)
                d_scores = (probs * (d_probs - inner)).astype(bfloat)
                made[0].append(dot(d_scores, k_ref[n]) * HD ** (-0.5))
                made[1].append(dot_tn(d_scores, q_ref[n]) * HD ** (-0.5))
                made[2].append(dot_tn(probs.astype(bfloat), d_out))
            for c in range(3):
                both = jnp.concatenate(made[c], axis=1)
                lanes = pl.ds(pl.multiple_of(pair * 128, 128), 128)
                dqkv[c, i * ROWS : (i + 1) * ROWS, lanes] = both
        return carry

    rqkv, q1, q2, qt, q3 = r.rqkv, r.q1, r.q2, r.qt, r.q3

    def mix_back():
        for c, gain in enumerate((q_gain, k_gain, None)):
            grad = dqkv[c]
            if gain is not None:
                normed = nq[c]
                kept.gains.append(jnp.sum(grad * normed, axis=0, keepdims=True))
                grad = grad * gain
                grad = sq[c] * (grad - head_mean(grad) - normed * head_mean(grad * normed))
            dm[c] = grad.astype(bfloat)
            add_in(dot_nt(dm[c], gqkv[c].reshape(768, 384)))

    dns, dnr = r.dns, r.dnr

    def send_in():
        dns[...] = dn[ROWS : 2 * ROWS, :].astype(bfloat)
        tags["dn"] = send(dns, dnr, x_dev)

    def qkv_grad(c):
        rqkv[c] = dot(nbt[...], dm[c]).astype(bfloat).reshape(2, 2, 2, 2, 48, 384)
        tags["q1", c] = send(rqkv.at[c, :, :, 1 - core], q1.at[c], core_dev)

    def qkv_y(c):
        arrive(q1.at[c], tags["q1", c], core_dev)
        q1[c] = q1[c] + rqkv[c, :, :, core]
        tags["q2", c] = send(q1.at[c, :, 1 - y], q2.at[c], y_dev)

    def qkv_z(c):
        arrive(q2.at[c], tags["q2", c], y_dev)
        qt[c] = q1[c, :, y] + q2[c]
        for k in range(1, N_HID):
            block = qt.at[c, z_up[k] // 2, lax.rem(z_up[k], 2)]
            tags["q3", c, k] = send(block, q3.at[k - 1, c], z_dev[k])

    def qkv_end():
        for c in range(3):
            total = qt[c, z // 2, lax.rem(z, 2)].astype(single)
            for k in range(1, N_HID):
                arrive(q3.at[k - 1, c], tags["q3", c, k], z_dev[k])
                total = total + q3[k - 1, c].astype(single)
            r.g_qkv[c] = total
        store("g_qkv")

    def head_grad():
        for i, (gh, gd) in enumerate(group):
            arrive(al.at[gh, gd], tags["ag"][i], group_dev[i])
        rows_all = al[...].reshape(32, 8, 256)
        d_logits_all = jnp.concatenate([rows_all[:, q, :] for q in range(4)], axis=1)
        pooled_all = jnp.concatenate([rows_all[:, 4 + q, :] for q in range(3)], axis=1)
        start = ((h * 4 + dp) * N_HID + z) * 24
        chosen = (iota((24, 768), 1) == iota((24, 768), 0) + start).astype(bfloat)
        mine = dot_nt(chosen, pooled_all.astype(bfloat))
        g_head = jnp.dot(mine, d_logits_all, precision=highest, preferred_element_type=single)
        r.g_head[...] = g_head[:, 0:classes]
        store("g_head")

    dx, gg = r.dx, r.gg

    def spread(row):
        blank = jnp.zeros((1, 192), single)
        halves = []
        for a in range(2):
            part = jnp.concatenate([row[:, a * 96 : a * 96 + 96], row[:, 192 + a * 96 : 288 + a * 96]], axis=1)
            halves.append(
                jnp.where(
                    h == 0,
                    jnp.concatenate([part, blank], axis=1),
                    jnp.concatenate([blank, part], axis=1),
                )
            )
        return jnp.concatenate(halves, axis=1)

    def norm_in():
        arrive(dnr, tags["dn"], x_dev)
        d_normed = dn[0:ROWS, :] + dnr[...].astype(single)
        block_n, block_scale = norm_parts(jnp.concatenate([st[0, 0], st[1, 0]], axis=1).astype(single))
        d_block_gain = jnp.sum(d_normed * block_n, axis=0, keepdims=True)
        d_in = ds[...] + norm_back(block_n, block_scale, d_normed * block_gain)
        low, high = d_in[:, 0:384], d_in[:, 384:768]
        dx[2] = jnp.where(h == 0, high, low).astype(bfloat)
        tags["dx"] = send(dx.at[2], dx.at[1], x_dev)
        dx[0] = jnp.where(h == 0, low, high).astype(bfloat)
        d_gains = jnp.concatenate(
            [d_block_gain, d_final_gain, spread(kept.gains[0]), spread(kept.gains[1])]
            + [jnp.zeros((4, 768), single)],
            axis=0,
        )
        low, high = d_gains[:, 0:384], d_gains[:, 384:768]
        gg[0] = jnp.where(h == 0, low, high)
        gg[2] = jnp.where(h == 0, high, low)
        tags["gg"] = send(gg.at[2], gg.at[1], x_dev)

    rext, e1, e2, et, e3 = r.rext, r.e1, r.e2, r.et, r.e3

    def ext_grad():
        arrive(dx.at[1], tags["dx"], x_dev)
        arrive(gg.at[1], tags["gg"], x_dev)
        dxt = jnp.concatenate([dx[0].astype(single), dx[1].astype(single)], axis=0).T.astype(bfloat)
        px2 = px[...].reshape(2 * ROWS, 1024)
        d_gains = (gg[0] + gg[1]).astype(bfloat)
        x0[...] = dot(dxt, px2[:, 0:512])
        x1[...] = dot(dxt, px2[:, 512:1024]) + dot_tn(d_gains, rows_of.astype(bfloat))
        for d in range(4):
            for w in range(N_HID):
                s = (d * N_HID + w) * 24
                rext[d // 2, d % 2, w] = jnp.concatenate(
                    [x0[s : s + 24, :], x1[s : s + 24, :]], axis=0
                ).astype(bfloat)
        tags["e1"] = send(rext.at[:, 1 - core], e1, core_dev)

    def ext_y():
        arrive(e1, tags["e1"], core_dev)
        e1[...] = e1[...] + rext[:, core]
        tags["e2"] = send(e1.at[1 - y], e2, y_dev)

    def ext_z():
        arrive(e2, tags["e2"], y_dev)
        et[...] = e1[y] + e2[...]
        tags["e3"] = [send(et.at[z_up[k]], e3.at[k - 1], z_dev[k]) for k in range(1, N_HID)]

    def ext_end():
        total = et[z].astype(single)
        for k in range(1, N_HID):
            arrive(e3.at[k - 1], tags["e3"][k - 1], z_dev[k])
            total = total + e3[k - 1].astype(single)
        r.g_patch[:, 0:512] = total[0:24]
        r.g_patch[:, 512:768] = total[24:48, 0:256]
        r.g_table[...] = total[24:48, 256 : 256 + seq_len]
        columns = total[24:48, 256:512]
        pick_f = (iota((8, 256), 1) == iota((8, 256), 0) + seq_len).astype(single)
        r.g_gains[...] = dot_nt(pick_f, columns, precision=highest)[0:4]
        for name in ("g_patch", "g_table", "g_gains"):
            store(name)

    ff_down(1)
    ff_down(2)
    ff_y(0, 1)
    cut_branch()
    out_back()
    ff_down(3)
    pass_rows()
    ff_up(2)
    ff_y(0, 2)
    ff_in(2)
    ff_up(3)
    ff_y(0, 3)
    ff_z(0, 1)
    out_grad()
    ff_up(1)
    ff_up(0)
    ff_y(1, 2)
    ff_y(1, 1)
    ff_y(1, 3)
    ff_z(0, 2)
    lax.fori_loop(0, 1, attend_back, 0)
    ff_in(3)
    ff_y(1, 0)
    ff_z(0, 3)
    lax.fori_loop(1, 2, attend_back, 0)
    lax.fori_loop(2, 3, attend_back, 0)
    out_y()
    ff_z(1, 2)
    ff_in(0)
    mix_back()
    ff_in(1)
    send_in()
    qkv_grad(0)
    ff_z(1, 3)
    qkv_grad(2)
    qkv_y(2)
    qkv_grad(1)
    ff_down(0)
    qkv_y(0)
    ff_z(1, 1)
    out_z()
    qkv_y(1)
    norm_in()
    qkv_z(2)
    ff_z(1, 0)
    qkv_z(0)
    ext_grad()
    out_end()
    ext_y()
    head_grad()
    ff_y(0, 0)
    qkv_z(1)
    ext_z()
    qkv_end()
    ff_z(0, 0)
    ff_end()
    ext_end()


    def read(prefix, kind):
        values = getattr(r, prefix + kind)[...]
        return values.reshape(-1, values.shape[-1])

    lane = iota((8, 128), 1)
    own = jnp.where(lane == 0, term, 0.0)
    grad_square = None
    for n, kind in enumerate(KINDS):
        value = square_sum(read("g_", kind))
        grad_square = value if grad_square is None else grad_square + value
        own = jnp.where(lane == 8 + n, square_sum(read("w_", kind)), own)
    own = jnp.where(lane == 1, grad_square, own)

    def all_sum(vector, line, every):
        line[z] = vector
        tags_z = [send(line.at[z], line.at[z], z_dev[k]) for k in range(1, N_HID)]
        for k in range(1, N_HID):
            arrive(line.at[z_down[k]], tags_z[k - 1], z_dev[k])
        every[h, dp] = (line[0] + line[1]) + (line[2] + line[3])
        tags_g = [send(every.at[h, dp], every.at[h, dp], device) for device in group_dev]
        for i, (gh, gd) in enumerate(group):
            arrive(every.at[gh, gd], tags_g[i], group_dev[i])
        total = None
        for a in range(2):
            for d in range(4):
                total = every[a, d] if total is None else total + every[a, d]
        return total

    sums = all_sum(own, r.l1, r.v1)
    grad_norm = jnp.sqrt(jnp.sum(jnp.where(lane == 1, sums, 0.0), axis=1, keepdims=True))[0:1]
    clip = jnp.minimum(1.0, clip_at / grad_norm)
    own = jnp.zeros((8, 128), single)
    for name in order[9:]:
        loads[name].wait()
    for n, kind in enumerate(KINDS):
        update = one_update(read("w_", kind), read("m_", kind), read("v_", kind), read("g_", kind), clip)[2]
        own = jnp.where(lane == 8 + n, square_sum(update), own)
    updates = all_sum(own, r.l2, r.v2)
    result = jnp.sqrt(sums) / jnp.sqrt(updates)
    result = jnp.where(lane == 0, sums, result)
    result = jnp.where(lane == 1, grad_norm, result)
    result = jnp.where(lane == 2, clip, result)
    r.scalars[...] = result
    store("scalars")
    for copy in stores:
        copy.wait()
    for key, copies in sends.items():

        def settle(copies=copies):
            for copy in copies:
                copy.wait_send()

        if key is None:
            settle()
        else:
            pl.when(holds[key])(settle)


def write_kernel(names, *refs):
    r = types.SimpleNamespace(**dict(zip(names, refs)))
    lane = iota((8, 128), 1)
    inputs = ["scalars"] + [p + k for k in KINDS for p in ("w_", "m_", "v_", "g_")]
    loads = {}
    for number, name in enumerate(inputs):
        loads[name] = pltpu.make_async_copy(
            getattr(r, "h_" + name), getattr(r, name), r.lsem.at[number]
        )
        loads[name].start()
    loads["scalars"].wait()

    def pick(n):
        return jnp.sum(jnp.where(lane == n, r.scalars[...], 0.0), axis=1, keepdims=True)[0:1]

    clip = pick(2)
    stores = []
    for n, kind in enumerate(KINDS):
        for p in ("w_", "m_", "v_", "g_"):
            loads[p + kind].wait()
        master = getattr(r, "w_" + kind)[...]
        grad = getattr(r, "g_" + kind)[...]
        ratio, c = pick(8 + n), clip
        if len(master.shape) == 3:
            c, ratio = clip[None], ratio[None]
        first, second, update = one_update(
            master, getattr(r, "m_" + kind)[...], getattr(r, "v_" + kind)[...], grad, c
        )
        results = (first, second, master - learn_rate * ratio * update)
        for p, value in zip(("nm_", "nv_", "nw_"), results):
            getattr(r, p + kind)[...] = value
            copy = pltpu.make_async_copy(
                getattr(r, p + kind),
                getattr(r, "h_" + p + kind),
                r.lsem.at[len(inputs) + len(stores)],
            )
            copy.start()
            stores.append(copy)
    for copy in stores:
        copy.wait()


def fast_device(patches, labels, *state):
    bfloat, single = jnp.bfloat16, jnp.float32

    def turn(kind, value):
        if kind in ("patch", "table", "down"):
            return value.T
        if kind == "qkv":
            return value.transpose(1, 0, 2)
        return value

    flat = [turn(KINDS[i % 8], value) for i, value in enumerate(state)]
    hbm = pl.BlockSpec(memory_space=pl.ANY)
    smem = pl.BlockSpec(memory_space=pltpu.SMEM)
    in_names = ["patches"] + [p + k for p in ("w_", "m_", "v_") for k in KINDS]
    out_names = ["g_" + k for k in KINDS] + ["scalars"]
    scratch = dict(
        px=((2, ROWS, 1024), bfloat),
        gext=((4, 4, 48, 512), bfloat),
        gqkv=((3, 2, 4, 2, 48, 384), bfloat),
        gout=((4, 4, 96, 256), bfloat),
        gup=((4, 2, 4, 96, 384), bfloat),
        gdn=((4, 2, 4, 96, 384), bfloat),
        ghd=((2, 4, 4, 48, 512), bfloat),
        x0=((384, 512), single),
        x1=((384, 512), single),
        hw=((2, 768, 512), bfloat),
        ga=((2, 8, 384), single),
        st=((2, 2, ROWS, 384), bfloat),
        nb=((2 * ROWS, 768), bfloat),
        nbt=((768, 2 * ROWS), bfloat),
        nq=((2, 2 * ROWS, 384), single),
        sq=((2, 2 * ROWS, 384), single),
        bd=((384, 384), bfloat),
        q=((12, ROWS, HD), bfloat),
        k=((12, ROWS, HD), bfloat),
        v=((12, ROWS, HD), bfloat),
        pr=((12, ROWS, ROWS), single),
        hof=((2 * ROWS, 384), bfloat),
        us=((4, 2 * ROWS, 384), single),
        hb=((4, 2 * ROWS, 384), bfloat),
        br=((2 * ROWS, 768), single),
        brs=((2, 2, ROWS, 384), bfloat),
        brr=((2, 2, ROWS, 384), bfloat),
        rw=((2, 8, 768), single),
        ds=((ROWS, 768), single),
        db=((2, ROWS, 768), bfloat),
        dbt=((768, 2 * ROWS), bfloat),
        al=((2, 4, 4, 8, 256), single),
        rff=((4, 2, 2, 2, 2, 96, 384), bfloat),
        f1=((4, 2, 2, 2, 96, 384), bfloat),
        f2=((4, 2, 2, 96, 384), bfloat),
        ft=((3, 2, 2, 96, 384), bfloat),
        f3=((3, 2, 2, 96, 384), bfloat),
        rout=((4, 2, 2, 96, 256), bfloat),
        o1=((4, 2, 96, 256), bfloat),
        o2=((4, 96, 256), bfloat),
        ot=((4, 96, 256), bfloat),
        o3=((3, 96, 256), bfloat),
        dh=((12, ROWS, HD), bfloat),
        dm=((3, 2 * ROWS, 384), bfloat),
        pc=((4, 2 * ROWS, 192), bfloat),
        dqkv=((3, 2 * ROWS, 384), single),
        rqkv=((3, 2, 2, 2, 2, 48, 384), bfloat),
        q1=((3, 2, 2, 2, 48, 384), bfloat),
        q2=((3, 2, 2, 48, 384), bfloat),
        qt=((3, 2, 2, 48, 384), bfloat),
        q3=((3, 3, 48, 384), bfloat),
        dns=((ROWS, 768), bfloat),
        dnr=((ROWS, 768), bfloat),
        dx=((3, ROWS, 384), bfloat),
        gg=((3, 8, 384), single),
        rext=((2, 2, 4, 48, 512), bfloat),
        e1=((2, 4, 48, 512), bfloat),
        e2=((4, 48, 512), bfloat),
        et=((4, 48, 512), bfloat),
        e3=((3, 48, 512), bfloat),
        l1=((4, 8, 128), single),
        l2=((4, 8, 128), single),
        v1=((2, 4, 8, 128), single),
        v2=((2, 4, 8, 128), single),
    )
    semaphores = 256
    shapes = [flat[i].shape for i in range(8)]
    npatch, seq_len, classes = patches.shape[1], flat[1].shape[1], flat[3].shape[1]
    total_images = labels.shape[0] * lax.axis_size("dp")
    sizes = (npatch, seq_len, classes, total_images)
    held = [(patches.shape, bfloat)] + [(s, single) for s in shapes * 4] + [((8, 128), single)]
    names = ["labels"] + ["h_" + n for n in in_names + out_names] + in_names + out_names
    names += list(scratch) + ["ssem", "rsem", "lsem"]
    found = pl.pallas_call(
        functools.partial(step_kernel, sizes, names),
        out_shape=[jax.ShapeDtypeStruct(s, single) for s in shapes]
        + [jax.ShapeDtypeStruct((8, 128), single)],
        in_specs=[smem] + [hbm] * 25,
        out_specs=[hbm] * 9,
        scratch_shapes=[pltpu.VMEM(s, t) for s, t in held + list(scratch.values())]
        + [pltpu.SemaphoreType.DMA((semaphores,))] * 2
        + [pltpu.SemaphoreType.DMA((len(held),))],
        compiler_params=pltpu.CompilerParams(
            collective_id=0, has_side_effects=True, vmem_limit_bytes=62 * 2**20
        ),
        name="train_step",
    )(labels, patches, *flat)
    grads, scalars = found[:8], found[8]
    in_names = ["scalars"] + [p + k for p in ("w_", "m_", "v_", "g_") for k in KINDS]
    out_names = [p + k for p in ("nm_", "nv_", "nw_") for k in KINDS]
    held = [((8, 128), single)] + [(s, single) for s in shapes * 7]
    names = ["h_" + n for n in in_names + out_names] + in_names + out_names + ["lsem"]
    written = pl.pallas_call(
        functools.partial(write_kernel, names),
        out_shape=[jax.ShapeDtypeStruct(s, single) for s in shapes * 3],
        in_specs=[hbm] * 33,
        out_specs=[hbm] * 24,
        scratch_shapes=[pltpu.VMEM(s, t) for s, t in held]
        + [pltpu.SemaphoreType.DMA((len(held),))],
        compiler_params=pltpu.CompilerParams(vmem_limit_bytes=62 * 2**20),
        name="write_step",
    )(scalars, *flat, *grads)
    back = [turn(KINDS[i % 8], value) for i, value in enumerate(written)]
    return (scalars[0, 0], scalars[0, 1], *back)


def fits(mesh):
    return tuple(mesh.shape[a] for a in ALL) == (4, 2, N_HID)


def solution(mesh):
    placed = (
        P(ALL, None, None),
        P("dp"),
        P(None, ALL),
        P(None, ALL),
        P(None, ALL),
        P(ALL, None),
        P(DATA, None, "heads"),
        P(MODEL, "dp"),
        P("dp", MODEL),
        P(MODEL, "dp"),
        P(None, ALL),
        P(None, ALL),
        P(None, ALL),
        P(ALL, None),
        P(DATA, None, "heads"),
        P(MODEL, "dp"),
        P("dp", MODEL),
        P(MODEL, "dp"),
        P(None, ALL),
        P(None, ALL),
        P(None, ALL),
        P(ALL, None),
        P(DATA, None, "heads"),
        P(MODEL, "dp"),
        P("dp", MODEL),
        P(MODEL, "dp"),
    )
    return jax.shard_map(
        fast_device if fits(mesh) else per_device,
        mesh=mesh,
        in_specs=placed,
        out_specs=(
            P(),
            P(),
            P(None, ALL),
            P(None, ALL),
            P(None, ALL),
            P(ALL, None),
            P(DATA, None, "heads"),
            P(MODEL, "dp"),
            P("dp", MODEL),
            P(MODEL, "dp"),
            P(None, ALL),
            P(None, ALL),
            P(None, ALL),
            P(ALL, None),
            P(DATA, None, "heads"),
            P(MODEL, "dp"),
            P("dp", MODEL),
            P(MODEL, "dp"),
            P(None, ALL),
            P(None, ALL),
            P(None, ALL),
            P(ALL, None),
            P(DATA, None, "heads"),
            P(MODEL, "dp"),
            P("dp", MODEL),
            P(MODEL, "dp"),
        ),
        check_vma=False,
    )
```

```python
import functools
import types

import jax
import jax.numpy as jnp
from jax import lax
from jax.experimental import pallas as pl
from jax.experimental.pallas import tpu as pltpu
from jax.sharding import PartitionSpec as P

HD = 64
PD = 768
STEP = 10
MESH = pl.DeviceIdType.MESH
ALL = ("dp", "heads", "hidden")
DATA = ("dp", "hidden")
MODEL = ("heads", "hidden")


beta_one = 0.9
beta_two = 0.999
adam_eps = 1e-08
decay_rate = 0.01
learn_rate = 0.5
clip_at = 0.001
norm_eps = 1e-06
highest = lax.Precision.HIGHEST


def layer_norm(values):
    center = values - jnp.mean(values, axis=-1, keepdims=True)
    return center * lax.rsqrt(jnp.mean(center * center, axis=-1, keepdims=True) + norm_eps)


def head_loss(stream_out, targets, final_gain, head_weight, npatch, total_images):
    normed_out, norm_back = jax.vjp(layer_norm, stream_out)
    final = normed_out * final_gain
    pooled_b = jnp.mean(final[:, :npatch], axis=1).astype(jnp.bfloat16)
    logits = jnp.dot(pooled_b, head_weight, preferred_element_type=jnp.float32)
    log_total = jax.nn.logsumexp(logits, axis=-1)
    onehot = (targets[:, None] == lax.broadcasted_iota(jnp.int32, logits.shape, 1)).astype(
        jnp.float32
    )
    terms = log_total - jnp.sum(logits * onehot, axis=-1)
    d_logits = (jnp.exp(logits - log_total[:, None]) - onehot) / total_images
    d_pooled = jnp.dot(d_logits, head_weight.astype(jnp.float32).T, precision=highest)
    count, seq_len, width = stream_out.shape
    spread = jnp.broadcast_to(d_pooled[:, None, :] / npatch, (count, npatch, width))
    d_final = jnp.concatenate(
        [spread, jnp.zeros((count, seq_len - npatch, width), jnp.float32)], axis=1
    )
    d_stream = norm_back(d_final * final_gain)[0]
    d_gain_rows = jnp.sum(d_final * normed_out, axis=1)
    return (terms, pooled_b, d_logits, d_stream, d_gain_rows)


def per_device(
    patches,
    labels,
    w_patch,
    table,
    gains,
    w_head,
    w_qkv,
    w_out,
    w_up,
    w_down,
    first_patch,
    first_table,
    first_gains,
    first_head,
    first_qkv,
    first_out,
    first_up,
    first_down,
    second_patch,
    second_table,
    second_gains,
    second_head,
    second_qkv,
    second_out,
    second_up,
    second_down,
):
    masters = [w_patch, table, gains, w_head, w_qkv, w_out, w_up, w_down]
    firsts = [
        first_patch,
        first_table,
        first_gains,
        first_head,
        first_qkv,
        first_out,
        first_up,
        first_down,
    ]
    seconds = [
        second_patch,
        second_table,
        second_gains,
        second_head,
        second_qkv,
        second_out,
        second_up,
        second_down,
    ]
    bfloat = jnp.bfloat16
    single = jnp.float32
    patch_b, table_b, gains_b, head_b = (
        lax.all_gather(w_patch.astype(bfloat), ALL, axis=1, tiled=True),
        lax.all_gather(table.astype(bfloat), ALL, axis=1, tiled=True),
        lax.all_gather(gains.astype(bfloat), ALL, axis=1, tiled=True),
        lax.all_gather(w_head.astype(bfloat), ALL, axis=0, tiled=True),
    )
    qkv_b = lax.all_gather(w_qkv.astype(bfloat), DATA, axis=0, tiled=True)
    out_b, up_b, down_b = (
        lax.all_gather(w_out.astype(bfloat), "dp", axis=1, tiled=True),
        lax.all_gather(w_up.astype(bfloat), "dp", axis=0, tiled=True),
        lax.all_gather(w_down.astype(bfloat), "dp", axis=1, tiled=True),
    )
    gain_vals = gains_b.astype(single)
    table_vals = table_b.astype(single)
    n_hidden = lax.axis_size("hidden")
    n_own = patches.shape[0]
    npatch = patches.shape[1]
    seq_len = table_b.shape[0]
    width = patch_b.shape[1]
    group_width = qkv_b.shape[2]
    group_heads = group_width // HD
    own_index = lax.axis_index("heads") * n_hidden + lax.axis_index("hidden")
    total_images = labels.shape[0] * lax.axis_size("dp")
    embedded = jnp.dot(patches.reshape(n_own * npatch, PD), patch_b, preferred_element_type=single)
    embedded = embedded.reshape(n_own, npatch, width) + table_vals[:npatch]
    registers = jnp.broadcast_to(table_vals[npatch:], (n_own, seq_len - npatch, width))
    stream_own = jnp.concatenate([embedded, registers], axis=1).astype(bfloat)
    stream_in = lax.all_gather(stream_own, MODEL, axis=0, tiled=True)
    n_img = stream_in.shape[0]
    row_count = n_img * seq_len
    stream_flat = stream_in.astype(single).reshape(row_count, width)
    normed_b = (layer_norm(stream_flat) * gain_vals[0]).astype(bfloat)
    n_att = n_img // n_hidden
    att_start = lax.axis_index("hidden") * n_att
    normed_att = lax.dynamic_slice_in_dim(
        normed_b.reshape(n_img, seq_len, width), att_start, n_att, 0
    )
    query_gain = lax.dynamic_slice_in_dim(
        gain_vals[2], lax.axis_index("heads") * group_width, group_width, 0
    ).reshape(group_heads, HD)
    key_gain = lax.dynamic_slice_in_dim(
        gain_vals[3], lax.axis_index("heads") * group_width, group_width, 0
    ).reshape(group_heads, HD)
    mixed = jnp.einsum("bsd,dcf->bscf", normed_att, qkv_b, preferred_element_type=single)
    mixed = mixed.reshape(n_att, seq_len, 3, group_heads, HD)
    query_norm, query_back = jax.vjp(layer_norm, mixed[:, :, 0])
    key_norm, key_back = jax.vjp(layer_norm, mixed[:, :, 1])
    queries = (query_norm * query_gain).astype(bfloat)
    keys = (key_norm * key_gain).astype(bfloat)
    values = mixed[:, :, 2].astype(bfloat)
    scale = HD ** (-0.5)
    scores = jnp.einsum("bqhd,bkhd->bhqk", queries, keys, preferred_element_type=single) * scale
    probs = jax.nn.softmax(scores, axis=-1)
    probs_b = probs.astype(bfloat)
    heads_out = jnp.einsum("bhqk,bkhd->bqhd", probs_b, values, preferred_element_type=single)
    heads_out = heads_out.astype(bfloat).reshape(n_att * seq_len, group_width)
    columns = lax.all_to_all(heads_out, "hidden", split_axis=1, concat_axis=0, tiled=True)
    attn_part = jnp.dot(columns, out_b, preferred_element_type=single)
    upper = jnp.dot(normed_b, up_b, preferred_element_type=single)
    activated, gelu_back = jax.vjp(jax.nn.gelu, upper)
    activated_b = activated.astype(bfloat)
    partial_sum = attn_part + jnp.dot(activated_b, down_b, preferred_element_type=single)
    total = lax.psum(partial_sum, MODEL)
    stream_out = (stream_flat + total).reshape(n_img, seq_len, width)
    terms, pooled_b, d_logits, d_stream, d_gain_rows = head_loss(
        stream_out, labels, gain_vals[1], head_b, npatch, total_images
    )
    loss_terms = lax.dynamic_slice_in_dim(terms, own_index * n_own, n_own, 0)
    pooled_own = lax.dynamic_slice_in_dim(pooled_b, own_index * n_own, n_own, 0)
    logits_own = lax.dynamic_slice_in_dim(d_logits, own_index * n_own, n_own, 0)
    d_head = jnp.dot(pooled_own.astype(single).T, logits_own, precision=highest)
    d_final_gain = jnp.sum(
        lax.dynamic_slice_in_dim(d_gain_rows, own_index * n_own, n_own, 0), axis=0
    )
    d_stream_own = lax.dynamic_slice_in_dim(d_stream, own_index * n_own, n_own, 0)
    d_branch = d_stream.reshape(row_count, width).astype(bfloat)
    d_activated = jnp.dot(d_branch, down_b.T, preferred_element_type=single)
    d_upper = gelu_back(d_activated)[0].astype(bfloat)
    d_down = jnp.dot(activated_b.T, d_branch, preferred_element_type=single)
    d_up = jnp.dot(normed_b.T, d_upper, preferred_element_type=single)
    d_normed = jnp.dot(d_upper, up_b.T, preferred_element_type=single)
    d_out = jnp.dot(columns.T, d_branch, preferred_element_type=single)
    d_columns = jnp.dot(d_branch, out_b.T, preferred_element_type=single).astype(bfloat)
    d_heads = lax.all_to_all(d_columns, "hidden", split_axis=0, concat_axis=1, tiled=True).reshape(
        n_att, seq_len, group_heads, HD
    )
    d_probs = jnp.einsum("bqhd,bkhd->bhqk", d_heads, values, preferred_element_type=single)
    d_values = jnp.einsum("bhqk,bqhd->bkhd", probs_b, d_heads, preferred_element_type=single)
    d_scores = (probs * (d_probs - jnp.sum(probs * d_probs, axis=-1, keepdims=True))).astype(bfloat)
    d_query_norm = (
        jnp.einsum("bhqk,bkhd->bqhd", d_scores, keys, preferred_element_type=single) * scale
    )
    d_key_norm = (
        jnp.einsum("bhqk,bqhd->bkhd", d_scores, queries, preferred_element_type=single) * scale
    )
    d_queries = query_back(d_query_norm * query_gain)[0]
    d_keys = key_back(d_key_norm * key_gain)[0]
    d_query_gain = jnp.sum(d_query_norm * query_norm, axis=(0, 1)).reshape(group_width)
    d_key_gain = jnp.sum(d_key_norm * key_norm, axis=(0, 1)).reshape(group_width)
    d_mixed = (
        jnp.stack([d_queries, d_keys, d_values], axis=2)
        .astype(bfloat)
        .reshape(n_att, seq_len, 3, group_width)
    )
    d_qkv = jnp.einsum("bsd,bscf->dcf", normed_att, d_mixed, preferred_element_type=single)
    d_att_in = jnp.einsum("bscf,dcf->bsd", d_mixed, qkv_b, preferred_element_type=single)
    d_normed = d_normed.reshape(n_img, seq_len, width)
    d_normed = lax.dynamic_update_slice_in_dim(
        d_normed, lax.dynamic_slice_in_dim(d_normed, att_start, n_att, 0) + d_att_in, att_start, 0
    )
    d_normed_own = lax.psum_scatter(
        d_normed.reshape(row_count, width).astype(jnp.bfloat16),
        MODEL,
        scatter_dimension=0,
        tiled=True,
    ).astype(jnp.float32)
    d_normed_own = d_normed_own.reshape(n_own, seq_len, width)
    normed_own, block_back = jax.vjp(layer_norm, stream_own.astype(single))
    d_stream_in = d_stream_own + block_back(d_normed_own * gain_vals[0])[0]
    d_block_gain = jnp.sum(d_normed_own * normed_own, axis=(0, 1))
    d_patch = jnp.dot(
        patches.reshape(n_own * npatch, PD).astype(single).T,
        d_stream_in[:, :npatch].reshape(n_own * npatch, width),
        precision=highest,
    )
    d_table = jnp.sum(d_stream_in, axis=0)
    zero_row = jnp.zeros((width,), single)
    gain_offset = lax.axis_index("heads") * group_width
    d_gains = jnp.stack(
        [
            d_block_gain,
            d_final_gain,
            lax.dynamic_update_slice_in_dim(zero_row, d_query_gain, gain_offset, 0),
            lax.dynamic_update_slice_in_dim(zero_row, d_key_gain, gain_offset, 0),
        ]
    )
    grad_patch, grad_table, grad_gains, grad_head = (
        lax.psum_scatter(d_patch, ALL, scatter_dimension=1, tiled=True),
        lax.psum_scatter(d_table, ALL, scatter_dimension=1, tiled=True),
        lax.psum_scatter(d_gains, ALL, scatter_dimension=1, tiled=True),
        lax.psum_scatter(d_head, ALL, scatter_dimension=0, tiled=True),
    )
    grad_qkv = lax.psum_scatter(d_qkv, DATA, scatter_dimension=0, tiled=True)
    grad_out, grad_up, grad_down = (
        lax.psum_scatter(d_out.astype(jnp.bfloat16), "dp", scatter_dimension=1, tiled=True).astype(
            jnp.float32
        ),
        lax.psum_scatter(d_up.astype(jnp.bfloat16), "dp", scatter_dimension=0, tiled=True).astype(
            jnp.float32
        ),
        lax.psum_scatter(d_down.astype(jnp.bfloat16), "dp", scatter_dimension=1, tiled=True).astype(
            jnp.float32
        ),
    )
    grads = [grad_patch, grad_table, grad_gains, grad_head, grad_qkv, grad_out, grad_up, grad_down]
    grad_squares = jnp.stack([jnp.sum(grad * grad) for grad in grads])
    weight_squares = jnp.stack([jnp.sum(master * master) for master in masters])
    grad_squares, weight_squares, loss_sum = lax.psum(
        (grad_squares, weight_squares, jnp.sum(loss_terms)), ALL
    )
    grad_norm = jnp.sqrt(jnp.sum(grad_squares))
    clip = jnp.minimum(1.0, clip_at / grad_norm)
    new_firsts, new_seconds, updates = ([], [], [])
    for master, first, second, grad in zip(masters, firsts, seconds, grads):
        clipped = grad * clip
        first_new = beta_one * first + (1.0 - beta_one) * clipped
        second_new = beta_two * second + (1.0 - beta_two) * clipped * clipped
        update = (
            first_new
            / (1.0 - beta_one**STEP)
            / (jnp.sqrt(second_new / (1.0 - beta_two**STEP)) + adam_eps)
        )
        updates.append(update + decay_rate * master)
        new_firsts.append(first_new)
        new_seconds.append(second_new)
    update_squares = lax.psum(
        jnp.stack([jnp.sum(update * update) for update in updates]), ALL
    )
    ratios = jnp.sqrt(weight_squares) / jnp.sqrt(update_squares)
    new_weights = [
        master - learn_rate * ratios[number] * update
        for number, (master, update) in enumerate(zip(masters, updates))
    ]
    return (
        loss_sum,
        grad_norm,
        new_firsts[0],
        new_firsts[1],
        new_firsts[2],
        new_firsts[3],
        new_firsts[4],
        new_firsts[5],
        new_firsts[6],
        new_firsts[7],
        new_seconds[0],
        new_seconds[1],
        new_seconds[2],
        new_seconds[3],
        new_seconds[4],
        new_seconds[5],
        new_seconds[6],
        new_seconds[7],
        new_weights[0],
        new_weights[1],
        new_weights[2],
        new_weights[3],
        new_weights[4],
        new_weights[5],
        new_weights[6],
        new_weights[7],
    )


def dot(a, b):
    return jnp.dot(a, b, preferred_element_type=jnp.float32)


def dot_nt(a, b, precision=None):
    return lax.dot_general(
        a, b, (((1,), (1,)), ((), ())), precision=precision, preferred_element_type=jnp.float32
    )


def dot_tn(a, b, precision=None):
    return lax.dot_general(
        a, b, (((0,), (0,)), ((), ())), precision=precision, preferred_element_type=jnp.float32
    )


def norm_parts(values):
    center = values - jnp.mean(values, axis=-1, keepdims=True)
    scale = lax.rsqrt(jnp.mean(center * center, axis=-1, keepdims=True) + norm_eps)
    return center * scale, scale


def norm_back(normed, scale, grad):
    inner = jnp.mean(grad * normed, axis=-1, keepdims=True)
    return scale * (grad - jnp.mean(grad, axis=-1, keepdims=True) - normed * inner)


gelu_c = 0.7978845608028654


def gelu_tanh(u):
    return jnp.tanh(gelu_c * (u + 0.044715 * (u * u * u)))


def iota(shape, axis):
    return lax.broadcasted_iota(jnp.int32, shape, axis)


def one_update(master, first, second, grad, clip):
    clipped = grad * clip
    first_new = beta_one * first + (1.0 - beta_one) * clipped
    second_new = beta_two * second + (1.0 - beta_two) * clipped * clipped
    one, two = 1.0 / (1.0 - beta_one**STEP), 1.0 / (1.0 - beta_two**STEP)
    update = (first_new * one) / (jnp.sqrt(second_new * two) + adam_eps)
    return first_new, second_new, update + decay_rate * master


def square_sum(values):
    return jnp.sum(values * values, axis=(0, 1), keepdims=True)


KINDS = ("patch", "table", "gains", "head", "qkv", "out", "up", "down")
EXT, QKV, UP0, UP1, HEAD, OUT, DN0, DN1 = range(8)
LEFT, RIGHT, ON_LEFT, ON_RIGHT = "left", "right", "on_left", "on_right"
ROWS = 208
N_HID = 4


def step_kernel(sizes, names, *refs):
    npatch, seq_len, classes, total_images = sizes
    r = types.SimpleNamespace(**dict(zip(names, refs)))
    bfloat, single = jnp.bfloat16, jnp.float32
    dp, h, z = (lax.axis_index(a) for a in ALL)
    core, y = lax.rem(dp, 2), dp // 2
    y_dp, core_dp = (1 - y) * 2 + core, y * 2 + (1 - core)
    x_dev, y_dev, core_dev = (dp, 1 - h, z), (y_dp, h, z), (core_dp, h, z)
    z_up = [lax.rem(z + k, N_HID) for k in range(N_HID)]
    z_down = [lax.rem(z + N_HID - k, N_HID) for k in range(N_HID)]
    z_dev = [(dp, h, z_up[k]) for k in range(N_HID)]
    group = [(h, y, z_up[k]) for k in range(1, N_HID)]
    for gh, gy in ((1 - h, y), (h, 1 - y), (1 - h, 1 - y)):
        group.extend((gh, gy, z_up[k]) for k in range(N_HID))
    source = [(h, y, z_down[k]) for k in range(1, N_HID)]
    for gh, gy in ((1 - h, y), (h, 1 - y), (1 - h, 1 - y)):
        source.extend((gh, gy, z_down[k]) for k in range(N_HID))
    group_dev = [(gy * 2 + core, gh, gz) for gh, gy, gz in group]

    barrier = pltpu.get_barrier_semaphore()
    for device in [core_dev] + group_dev:
        pl.semaphore_signal(barrier, inc=1, device_id=device, device_id_type=MESH)

    loads = {}
    order = ["w_up", "w_patch", "w_table", "w_gains"]
    order += ["w_" + k for k in KINDS if "w_" + k not in order] + ["patches"]
    order += [p + k for p in ("m_", "v_") for k in KINDS]

    def load(names):
        for name in names:
            loads[name] = pltpu.make_async_copy(
                getattr(r, "h_" + name), getattr(r, name), r.lsem.at[order.index(name)]
            )
            loads[name].start()

    load(order[0:9])
    stores = []

    def store(name):
        copy = pltpu.make_async_copy(
            getattr(r, name), getattr(r, "h_" + name), r.lsem.at[len(order) + len(stores)]
        )
        copy.start()
        stores.append(copy)

    ssem, rsem = r.ssem, r.rsem
    count = [0]
    sends = {}
    last = N_HID - 1
    holds = {}
    for d in range(1, N_HID):
        holds[LEFT, d] = z >= d
        holds[RIGHT, d] = z + d <= last
        holds[ON_RIGHT, d] = (z >= d) & (z < last)
        holds[ON_LEFT, d] = (z + d <= last) & (z > 0)
    holds[ON_RIGHT, 0] = z < last
    holds[ON_LEFT, 0] = z > 0
    next_z = {LEFT: (dp, h, z_up[1]), RIGHT: (dp, h, z_down[1])}

    def send(source, target, device, key=None):
        number = count[0]
        count[0] += 1
        copy = pltpu.make_async_remote_copy(
            src_ref=source,
            dst_ref=target,
            send_sem=ssem.at[number],
            recv_sem=rsem.at[number],
            device_id=device,
            device_id_type=MESH,
        )
        if key is None:
            copy.start()
        else:
            pl.when(holds[key])(copy.start)
        sends.setdefault(key, []).append(copy)
        return number

    def arrive(target, number, device):
        pltpu.make_async_remote_copy(
            src_ref=target,
            dst_ref=target,
            send_sem=ssem.at[number],
            recv_sem=rsem.at[number],
            device_id=device,
            device_id_type=MESH,
        ).wait_recv()

    gext, gqkv, gout, gup, gdn, ghd = r.gext, r.gqkv, r.gout, r.gup, r.gdn, r.ghd
    x0, x1, px = r.x0, r.x1, r.px
    kept = types.SimpleNamespace()

    def pack_ext():
        x1[0:24, :] = jnp.zeros((24, 512), single)
        for name in order[1:4]:
            loads[name].wait()
        x1[0:24, 256 : 256 + seq_len] = r.w_table[...]
        pick = (iota((4, 256), 1) == iota((4, 256), 0) + seq_len).astype(bfloat)
        table_part = x1[0:24, 256:512] + dot_tn(r.w_gains[...].astype(bfloat), pick)
        wp = r.w_patch[...]
        gext[dp, z] = jnp.concatenate(
            [wp[:, 0:512], jnp.concatenate([wp[:, 512:768], table_part], axis=1)], axis=0
        ).astype(bfloat)

    def pack_patches():
        row, col = iota((ROWS, 256), 0), iota((ROWS, 256), 1)
        spot = jnp.where((row == col) & (row < seq_len), 1.0, 0.0).astype(bfloat)
        px[0, :, 768:1024] = spot
        px[1, :, 768:1024] = spot
        px[0, ROWS - 16 : ROWS, 0:768] = jnp.zeros((16, 768), bfloat)
        loads["patches"].wait()
        px[0, 0:npatch, 0:768] = r.patches[0]

    def pack_qkv():
        loads["w_qkv"].wait()
        gqkv[:, z // 2, dp, lax.rem(z, 2)] = r.w_qkv[...].astype(bfloat)

    def pack_up():
        loads["w_up"].wait()
        gup[z, :, dp] = r.w_up[...].astype(bfloat).reshape(2, 96, 384)

    def pack_head():
        loads["w_head"].wait()
        x0[0:24, :] = r.w_head[:, 0:512]
        x1[0:24, :] = jnp.zeros((24, 512), single)
        x1[0:24, 0 : classes - 512] = r.w_head[:, 512:classes]
        ghd[h, dp, z] = jnp.concatenate([x0[0:24, :], x1[0:24, :]], axis=0).astype(bfloat)

    def pack_out():
        loads["w_out"].wait()
        gout[dp, z] = jnp.zeros((96, 256), bfloat)
        gout[dp, z, :, 0:192] = r.w_out[...].astype(bfloat)

    def pack_down():
        loads["w_down"].wait()
        gdn[z, :, dp] = r.w_down[...].astype(bfloat).reshape(2, 96, 384)

    def at_ext(d, w):
        return gext.at[d, w]

    def at_qkv(d, w):
        return gqkv.at[:, w // 2, d, lax.rem(w, 2)]

    def at_out(d, w):
        return gout.at[d, w]

    def at_up(half):
        return lambda d, w: gup.at[w, half, d]

    def at_dn(half):
        return lambda d, w: gdn.at[w, half, d]

    def at_hd(d, w):
        return ghd.at[h, d, w]

    slot = {
        EXT: at_ext,
        QKV: at_qkv,
        OUT: at_out,
        UP0: at_up(0),
        UP1: at_up(1),
        DN0: at_dn(0),
        DN1: at_dn(1),
        HEAD: at_hd,
    }
    lines = {
        EXT: lambda d: gext.at[d],
        QKV: lambda d: gqkv.at[:, :, d],
        OUT: lambda d: gout.at[d],
        UP0: lambda d: gup.at[:, 0, d],
        UP1: lambda d: gup.at[:, 1, d],
        DN0: lambda d: gdn.at[:, 0, d],
        DN1: lambda d: gdn.at[:, 1, d],
        HEAD: lambda d: ghd.at[h, d],
    }
    tags = {}

    def own_z(name):
        own = slot[name](dp, z)
        tags[name, LEFT, 1] = send(own, own, next_z[LEFT], (ON_RIGHT, 0))
        tags[name, RIGHT, 1] = send(own, own, next_z[RIGHT], (ON_LEFT, 0))

    def own_y(name):
        own = slot[name](dp, z)
        tags[name, "y", 0] = send(own, own, y_dev)

    def pass_z(name, d):
        for side, on, theirs in ((LEFT, ON_RIGHT, z_down[d]), (RIGHT, ON_LEFT, z_up[d])):
            block = slot[name](dp, theirs)
            number = tags[name, side, d]
            pl.when(holds[side, d])(functools.partial(arrive, block, number, y_dev))
            if d < last:
                tags[name, side, d + 1] = send(block, block, next_z[side], (on, d))
            tags[name, "y", side, d] = send(block, block, y_dev, (side, d))
        if d == last and name != HEAD:
            line = lines[name](dp)
            tags[name, "c", 0] = send(line, line, core_dev)

    def pass_core(name):
        at = slot[name]
        arrive(at(y_dp, z), tags[name, "y", 0], y_dev)
        for d in range(1, N_HID):
            for side, theirs in ((LEFT, z_down[d]), (RIGHT, z_up[d])):
                number = tags[name, "y", side, d]
                pl.when(holds[side, d])(functools.partial(arrive, at(y_dp, theirs), number, y_dev))
        line = lines[name](y_dp)
        if name != HEAD:
            tags[name, "c", 1] = send(line, line, core_dev)
        else:
            own = lines[name](dp)
            tags[name, "x", 0] = send(own, own, x_dev)
            tags[name, "x", 1] = send(line, line, x_dev)

    def complete(name):
        far = (1 - y) * 2 + (1 - core)
        arrive(lines[name](core_dp), tags[name, "c", 0], core_dev)
        arrive(lines[name](far), tags[name, "c", 1], core_dev)

    def head_core():
        for i, d in enumerate((dp, y_dp)):
            arrive(ghd.at[1 - h, d], tags[HEAD, "x", i], x_dev)
        for i, d in enumerate((dp, y_dp)):
            block = ghd.at[:, d]
            tags[HEAD, "c", i] = send(block, block, core_dev)

    def head_complete():
        far = (1 - y) * 2 + (1 - core)
        for i, d in enumerate((core_dp, far)):
            arrive(ghd.at[:, d], tags[HEAD, "c", i], core_dev)

    def send_images():
        images = px.at[0, :, pl.ds(0, 768)]
        tags["px"] = send(images, px.at[1, :, pl.ds(0, 768)], x_dev)

    ga, st = r.ga, r.st
    rows_of = (iota((8, 512), 1) == iota((8, 512), 0) + (256 + seq_len)) & (iota((8, 512), 0) < 4)

    def unpack(block_of, low, high):
        for d in range(4):
            for w in range(N_HID):
                s = (d * N_HID + w) * 24
                block = block_of(d, w).astype(single)
                low[s : s + 24, :] = block[0:24]
                high[s : s + 24, :] = block[24:48]

    def embed(i):
        if i == 0:
            unpack(lambda d, w: gext[d, w], x0, x1)
            ga[h] = dot_nt(rows_of.astype(bfloat), x1[...].astype(bfloat))
            tags["ga"] = send(ga.at[h], ga.at[h], x_dev)
        else:
            arrive(px.at[1, :, pl.ds(0, 768)], tags["px"], x_dev)
        low, high = x0[...].astype(bfloat), x1[...].astype(bfloat)
        made = dot_nt(px[i, :, 0:512], low) + dot_nt(px[i, :, 512:1024], high)
        st[h, i] = made.astype(bfloat)
        tags["st", i] = send(st.at[h, i], st.at[h, 1 - i], x_dev)

    def gain_row(i):
        return jnp.concatenate([ga[0, i : i + 1, :], ga[1, i : i + 1, :]], axis=1)

    def head_gain(i):
        pieces = []
        both = [ga[0, i : i + 1, :], ga[1, i : i + 1, :]]
        for d in range(4):
            pieces.extend(half[:, d * 96 : d * 96 + 96] for half in both)
        low = jnp.concatenate(pieces[0:4], axis=1)
        high = jnp.concatenate(pieces[4:8], axis=1)
        return jnp.where(h == 0, low, high)

    nb, nbt = r.nb, r.nbt

    def block_norm():
        arrive(ga.at[1 - h], tags["ga"], x_dev)
        arrive(st.at[1 - h, 1], tags["st", 0], x_dev)
        arrive(st.at[1 - h, 0], tags["st", 1], x_dev)
        gain = gain_row(0)
        for i in range(2):
            stream = jnp.concatenate([st[0, i], st[1, i]], axis=1).astype(single)
            nb[i * ROWS : (i + 1) * ROWS, :] = (norm_parts(stream)[0] * gain).astype(bfloat)

    nq, sq, bd = r.nq, r.sq, r.bd
    q_ref, k_ref, v_ref = r.q, r.k, r.v

    def head_mean(values):
        return dot(values.astype(bfloat), bd[...])

    def project(c):
        mixed = dot(nb[...], gqkv[c].reshape(768, 384))
        if c == 0:
            same = iota((384, 384), 0) // HD == iota((384, 384), 1) // HD
            bd[...] = jnp.where(same, 1.0 / HD, 0.0).astype(bfloat)
        if c < 2:
            top = mixed.astype(bfloat).astype(single)
            center = mixed - (head_mean(top) + head_mean(mixed - top))
            scale = lax.rsqrt(head_mean(center * center) + norm_eps)
            normed = center * scale
            nq[c] = normed
            sq[c] = scale
            mixed = normed * head_gain(2 + c)
        out = (q_ref, k_ref, v_ref)[c]
        mixed = mixed.astype(bfloat)
        for n in range(6):
            part = mixed[:, n * HD : (n + 1) * HD]
            out[2 * n] = part[0:ROWS]
            out[2 * n + 1] = part[ROWS : 2 * ROWS]

    pr, hof = r.pr, r.hof
    dead = iota((ROWS, ROWS), 1) >= seq_len

    def attend(pair, carry):
        for i in range(2):
            made = []
            for side in range(2):
                n = 4 * pair + 2 * side + i
                scores = dot_nt(q_ref[n], k_ref[n]) * HD ** (-0.5)
                scores = jnp.where(dead, -1e30, scores)
                scores = scores - jnp.max(scores, axis=-1, keepdims=True)
                weights = jnp.exp(scores)
                probs = weights / jnp.sum(weights, axis=-1, keepdims=True)
                pr[n] = probs
                made.append(dot(probs.astype(bfloat), v_ref[n]))
            both = jnp.concatenate(made, axis=1).astype(bfloat)
            hof[i * ROWS : (i + 1) * ROWS, pl.ds(pl.multiple_of(pair * 128, 128), 128)] = both
        return carry

    us, hb, br = r.us, r.hb, r.br

    def rise(w, carry):
        upper = dot(nb[...], gup[w].reshape(768, 384))
        us[w] = upper
        hb[w] = (0.5 * upper * (1.0 + gelu_tanh(upper))).astype(bfloat)
        return carry

    def project_out():
        lefts, rights = [], []
        for d in range(4):
            part = dot(hof[...], gout[d].reshape(384, 256))
            lefts.append(part[:, 0:96])
            rights.append(part[:, 96:192])
        br[:, 0:384] = jnp.concatenate(lefts, axis=1)
        br[:, 384:768] = jnp.concatenate(rights, axis=1)

    def turn_normed():
        nbt[...] = nb[...].T

    brs, brr = r.brs, r.brr

    def fall(half):
        lanes = slice(half * 384, half * 384 + 384)

        def add(w, carry):
            br[:, lanes] += dot_nt(hb[w], gdn[w, half].reshape(384, 384))
            return carry

        lax.fori_loop(0, N_HID, add, 0)

    def share(half, i):
        lanes = slice(half * 384, half * 384 + 384)
        brs[half, i] = br[i * ROWS : (i + 1) * ROWS, lanes].astype(bfloat)
        tags["br", half, i] = send(brs.at[half, i], brr.at[half, 1 - i], x_dev)

    hw = r.hw

    def unpack_head():
        for a in range(2):
            unpack(lambda d, w: ghd[a, d, w], x0, x1)
            hw[0, a * 384 : a * 384 + 384, :] = x0[...].astype(bfloat)
            hw[1, a * 384 : a * 384 + 384, :] = x1[...].astype(bfloat)

    def stream_out(i):
        for half in range(2):
            arrive(brr.at[half, i], tags["br", half, 1 - i], x_dev)
        stream = jnp.concatenate([st[0, i], st[1, i]], axis=1).astype(single)
        theirs = jnp.concatenate([brr[0, i], brr[1, i]], axis=1).astype(single)
        return norm_parts(stream + (br[i * ROWS : (i + 1) * ROWS, :] + theirs))

    pl.semaphore_wait(barrier, 1 + len(group_dev))
    pack_up()
    own_y(UP0)
    own_z(UP0)
    pack_head()
    own_z(HEAD)
    own_y(HEAD)
    pack_ext()
    own_y(EXT)
    own_y(UP1)
    own_z(EXT)
    pack_qkv()
    pass_z(UP0, 1)
    pass_z(EXT, 1)
    pack_out()
    own_y(QKV)
    own_z(QKV)
    own_z(OUT)
    pass_z(EXT, 2)
    pack_patches()
    pass_z(UP0, 2)
    send_images()
    pass_z(QKV, 1)
    pass_z(HEAD, 1)
    pass_z(EXT, 3)
    pack_down()
    own_z(UP1)
    own_y(OUT)
    pass_z(QKV, 2)
    pass_core(EXT)
    pass_z(UP0, 3)
    complete(EXT)
    embed(0)
    load(order[9:])
    pass_z(HEAD, 2)
    pass_z(QKV, 3)
    pass_z(UP1, 1)
    pass_z(HEAD, 3)
    embed(1)
    pass_z(UP1, 2)
    own_z(DN1)
    pass_z(UP1, 3)
    own_y(DN1)
    pass_z(OUT, 1)
    pass_core(UP0)
    pass_core(QKV)
    own_z(DN0)
    block_norm()
    pass_z(DN1, 1)
    pass_z(OUT, 2)
    complete(QKV)
    project(0)
    project(1)
    project(2)
    pass_core(HEAD)
    pass_core(UP1)
    turn_normed()
    pass_z(DN1, 2)
    lax.fori_loop(0, 1, attend, 0)
    complete(UP0)
    pass_z(OUT, 3)
    lax.fori_loop(1, 2, attend, 0)
    lax.fori_loop(2, 3, attend, 0)
    pass_z(DN1, 3)
    pass_z(DN0, 1)
    complete(UP1)
    lax.fori_loop(0, 2, rise, 0)
    own_y(DN0)
    lax.fori_loop(2, 4, rise, 0)
    pass_z(DN0, 2)
    pass_core(OUT)
    pass_core(DN1)
    complete(OUT)
    project_out()
    complete(DN1)
    fall(1)
    share(1, 1)
    pass_z(DN0, 3)
    share(1, 0)
    pass_core(DN0)
    complete(DN0)
    fall(0)
    share(0, 1)
    head_core()
    head_complete()
    share(0, 0)
    unpack_head()
    block_gain, q_gain, k_gain = gain_row(0), head_gain(2), head_gain(3)

    out_n, out_scale = stream_out(0)
    is_patch = iota((ROWS, 1), 0) < npatch
    final_gain = gain_row(1)
    n_sum = jnp.sum(jnp.where(is_patch, out_n, 0.0), axis=0, keepdims=True)
    pooled = n_sum * final_gain / npatch
    pooled_b = pooled.astype(bfloat)
    heads_b = [hw[0], hw[1]]
    pooled_8 = jnp.broadcast_to(pooled_b, (16, 768))
    logits = jnp.concatenate([dot(pooled_8, m)[0:1] for m in heads_b], axis=1)
    lane = iota((1, 1024), 1)
    logits = jnp.where(lane < classes, logits, -1e30)
    top = jnp.max(logits, axis=-1, keepdims=True)
    log_total = top + jnp.log(jnp.sum(jnp.exp(logits - top), axis=-1, keepdims=True))
    onehot = jnp.where(lane == r.labels[h * N_HID + z], 1.0, 0.0)
    term = log_total - jnp.sum(jnp.where(lane < classes, logits, 0.0) * onehot, axis=-1, keepdims=True)
    d_logits = (jnp.exp(logits - log_total) - onehot) / total_images
    hi = d_logits.astype(bfloat).astype(single)
    both = jnp.concatenate([hi, d_logits - hi, jnp.zeros((14, 1024), single)], axis=0).astype(bfloat)
    back = dot_nt(both[:, 0:512], heads_b[0]) + dot_nt(both[:, 512:1024], heads_b[1])
    d_pooled = (back[0:1] + back[1:2]) / npatch
    d_row = d_pooled * final_gain
    rw = r.rw
    rw[0] = jnp.broadcast_to(d_row, (8, 768))
    tag_rw = send(rw.at[0], rw.at[1], x_dev)
    ds, db, dbt = r.ds, r.db, r.dbt
    d_stream = jnp.where(is_patch, norm_back(out_n, out_scale, d_row), 0.0)
    ds[...] = d_stream
    db[0] = d_stream.astype(bfloat)
    dbt[:, 0:ROWS] = d_stream.T.astype(bfloat)
    d_final_gain = d_pooled * n_sum
    al = r.al
    pooled_f = pooled_b.astype(single)
    al[core, h, y, z] = jnp.concatenate(
        [d_logits[:, q * 256 : q * 256 + 256] for q in range(4)]
        + [pooled_f[:, q * 256 : q * 256 + 256] for q in range(3)]
        + [jnp.zeros((1, 256), single)],
        axis=0,
    )
    own = al.at[core, h, y, z]
    tag_al = [send(own, own, device) for device in group_dev]
    out_n, out_scale = stream_out(1)
    arrive(rw.at[1], tag_rw, x_dev)
    d_stream = jnp.where(is_patch, norm_back(out_n, out_scale, rw[1, 0:1, :]), 0.0)
    db[1] = d_stream.astype(bfloat)
    dbt[:, ROWS : 2 * ROWS] = d_stream.T.astype(bfloat)
    db2 = db[...].reshape(2 * ROWS, 768)

    rff, f1, f2, ft, f3 = r.rff, r.f1, r.f2, r.ft, r.f3
    dn, dm = br, r.dm
    kept = types.SimpleNamespace(fresh=True, gains=[])

    def add_in(part):
        if kept.fresh:
            dn[...] = part
        else:
            dn[...] += part
        kept.fresh = False

    def ff_send(m, k):
        tags["ff", m, k] = send(rff.at[k, m, :, :, 1 - core], f1.at[k, m], core_dev)

    def ff_down(k):
        rff[k, 0] = dot(dbt[...], hb[z_up[k]]).astype(bfloat).reshape(2, 2, 2, 96, 384)
        ff_send(0, k)

    def ff_up(k):
        w = z_up[k]
        upper = us[w]
        t = gelu_tanh(upper)
        slope = 0.5 * (1.0 + t) + 0.5 * upper * (1.0 - t * t) * gelu_c * (
            1.0 + 3 * 0.044715 * (upper * upper)
        )
        d_upper = (dot(db2, gdn[w].reshape(768, 384)) * slope).astype(bfloat)
        us[w] = d_upper.astype(single)
        rff[k, 1] = dot(nbt[...], d_upper).astype(bfloat).reshape(2, 2, 2, 96, 384)
        ff_send(1, k)

    def ff_in(k):
        w = z_up[k]
        add_in(dot_nt(us[w].astype(bfloat), gup[w].reshape(768, 384)))

    def ff_y(m, k):
        arrive(f1.at[k, m], tags["ff", m, k], core_dev)
        f1[k, m] = f1[k, m] + rff[k, m, :, :, core]
        tags["fy", m, k] = send(f1.at[k, m, :, 1 - y], f2.at[k, m], y_dev)

    def ff_z(m, k):
        arrive(f2.at[k, m], tags["fy", m, k], y_dev)
        if k:
            ft[k - 1, m] = f1[k, m, :, y] + f2[k, m]
            tags["fz", m, k] = send(ft.at[k - 1, m], f3.at[k - 1, m], z_dev[k])

    def ff_end():
        for m, name in enumerate(("g_down", "g_up")):
            total = f1[0, m, :, y].astype(single) + f2[0, m].astype(single)
            for k in range(1, N_HID):
                arrive(f3.at[k - 1, m], tags["fz", m, k], z_dev[k])
                total = total + f3[k - 1, m].astype(single)
            getattr(r, name)[...] = total.reshape(192, 384)
            store(name)

    def pass_rows():
        for i, place in enumerate(source):
            arrive(al.at[(core, *place)], tag_al[i], core_dev)
        tags["al"] = send(al.at[core], al.at[core], core_dev)

    rout, o1, o2, ot, o3, pc = r.rout, r.o1, r.o2, r.ot, r.o3, r.pc

    def cut_branch():
        for d in range(4):
            low = db2[:, d * 96 : d * 96 + 96]
            high = db2[:, 384 + d * 96 : 384 + d * 96 + 96]
            pc[d] = jnp.concatenate([low, high], axis=1)

    def out_grad():
        hot = hof[...].T
        for d in range(4):
            rout[:, d // 2, d % 2] = jnp.zeros((N_HID, 96, 256), bfloat)
            grad = dot(hot, pc[d]).astype(bfloat).reshape(N_HID, 96, 192)
            rout[:, d // 2, d % 2, :, 0:192] = grad
        tags["o1"] = send(rout.at[:, :, 1 - core], o1, core_dev)

    dh = r.dh

    def out_back():
        d_heads = None
        for d in range(4):
            part = dot_nt(pc[d], gout[d].reshape(384, 256)[:, 0:192])
            d_heads = part if d_heads is None else d_heads + part
        d_heads = d_heads.astype(bfloat)
        for n in range(6):
            part = d_heads[:, n * HD : (n + 1) * HD]
            dh[2 * n] = part[0:ROWS]
            dh[2 * n + 1] = part[ROWS : 2 * ROWS]

    def out_y():
        arrive(o1, tags["o1"], core_dev)
        o1[...] = o1[...] + rout[:, :, core]
        tags["o2"] = send(o1.at[:, 1 - y], o2, y_dev)

    def out_z():
        arrive(o2, tags["o2"], y_dev)
        ot[...] = o1[:, y] + o2[...]
        tags["o3"] = [send(ot.at[z_up[k]], o3.at[k - 1], z_dev[k]) for k in range(1, N_HID)]

    def out_end():
        total = ot[z].astype(single)
        for k in range(1, N_HID):
            arrive(o3.at[k - 1], tags["o3"][k - 1], z_dev[k])
            total = total + o3[k - 1].astype(single)
        r.g_out[...] = total[:, 0:192]
        store("g_out")

    dqkv = r.dqkv

    def attend_back(pair, carry):
        for i in range(2):
            made = ([], [], [])
            for side in range(2):
                n = 4 * pair + 2 * side + i
                probs = pr[n]
                d_out = dh[n]
                d_probs = dot_nt(d_out, v_ref[n])
                inner = jnp.sum(probs * d_probs, axis=-1, keepdims=True)
                d_scores = (probs * (d_probs - inner)).astype(bfloat)
                made[0].append(dot(d_scores, k_ref[n]) * HD ** (-0.5))
                made[1].append(dot_tn(d_scores, q_ref[n]) * HD ** (-0.5))
                made[2].append(dot_tn(probs.astype(bfloat), d_out))
            for c in range(3):
                both = jnp.concatenate(made[c], axis=1)
                lanes = pl.ds(pl.multiple_of(pair * 128, 128), 128)
                dqkv[c, i * ROWS : (i + 1) * ROWS, lanes] = both
        return carry

    rqkv, q1, q2, qt, q3 = r.rqkv, r.q1, r.q2, r.qt, r.q3

    def mix_back():
        for c, gain in enumerate((q_gain, k_gain, None)):
            grad = dqkv[c]
            if gain is not None:
                normed = nq[c]
                kept.gains.append(jnp.sum(grad * normed, axis=0, keepdims=True))
                grad = grad * gain
                grad = sq[c] * (grad - head_mean(grad) - normed * head_mean(grad * normed))
            dm[c] = grad.astype(bfloat)
            add_in(dot_nt(dm[c], gqkv[c].reshape(768, 384)))

    dns, dnr = r.dns, r.dnr

    def send_in():
        dns[...] = dn[ROWS : 2 * ROWS, :].astype(bfloat)
        tags["dn"] = send(dns, dnr, x_dev)

    def qkv_grad(c):
        rqkv[c] = dot(nbt[...], dm[c]).astype(bfloat).reshape(2, 2, 2, 2, 48, 384)
        tags["q1", c] = send(rqkv.at[c, :, :, 1 - core], q1.at[c], core_dev)

    def qkv_y(c):
        arrive(q1.at[c], tags["q1", c], core_dev)
        q1[c] = q1[c] + rqkv[c, :, :, core]
        tags["q2", c] = send(q1.at[c, :, 1 - y], q2.at[c], y_dev)

    def qkv_z(c):
        arrive(q2.at[c], tags["q2", c], y_dev)
        qt[c] = q1[c, :, y] + q2[c]
        for k in range(1, N_HID):
            block = qt.at[c, z_up[k] // 2, lax.rem(z_up[k], 2)]
            tags["q3", c, k] = send(block, q3.at[k - 1, c], z_dev[k])

    def qkv_end():
        for c in range(3):
            total = qt[c, z // 2, lax.rem(z, 2)].astype(single)
            for k in range(1, N_HID):
                arrive(q3.at[k - 1, c], tags["q3", c, k], z_dev[k])
                total = total + q3[k - 1, c].astype(single)
            r.g_qkv[c] = total
        store("g_qkv")

    def head_grad():
        arrive(al.at[1 - core], tags["al"], core_dev)
        rows_all = al[...].reshape(32, 8, 256)
        d_logits_all = jnp.concatenate([rows_all[:, q, :] for q in range(4)], axis=1)
        pooled_all = jnp.concatenate([rows_all[:, 4 + q, :] for q in range(3)], axis=1)
        start = ((h * 4 + dp) * N_HID + z) * 24
        chosen = (iota((24, 768), 1) == iota((24, 768), 0) + start).astype(bfloat)
        mine = dot_nt(chosen, pooled_all.astype(bfloat))
        g_head = jnp.dot(mine, d_logits_all, precision=highest, preferred_element_type=single)
        r.g_head[...] = g_head[:, 0:classes]
        store("g_head")

    dx, gg = r.dx, r.gg

    def spread(row):
        blank = jnp.zeros((1, 192), single)
        halves = []
        for a in range(2):
            part = jnp.concatenate([row[:, a * 96 : a * 96 + 96], row[:, 192 + a * 96 : 288 + a * 96]], axis=1)
            halves.append(
                jnp.where(
                    h == 0,
                    jnp.concatenate([part, blank], axis=1),
                    jnp.concatenate([blank, part], axis=1),
                )
            )
        return jnp.concatenate(halves, axis=1)

    def norm_in():
        arrive(dnr, tags["dn"], x_dev)
        d_normed = dn[0:ROWS, :] + dnr[...].astype(single)
        block_n, block_scale = norm_parts(jnp.concatenate([st[0, 0], st[1, 0]], axis=1).astype(single))
        d_block_gain = jnp.sum(d_normed * block_n, axis=0, keepdims=True)
        d_in = ds[...] + norm_back(block_n, block_scale, d_normed * block_gain)
        low, high = d_in[:, 0:384], d_in[:, 384:768]
        dx[2] = jnp.where(h == 0, high, low).astype(bfloat)
        tags["dx"] = send(dx.at[2], dx.at[1], x_dev)
        dx[0] = jnp.where(h == 0, low, high).astype(bfloat)
        d_gains = jnp.concatenate(
            [d_block_gain, d_final_gain, spread(kept.gains[0]), spread(kept.gains[1])]
            + [jnp.zeros((4, 768), single)],
            axis=0,
        )
        low, high = d_gains[:, 0:384], d_gains[:, 384:768]
        gg[0] = jnp.where(h == 0, low, high)
        gg[2] = jnp.where(h == 0, high, low)
        tags["gg"] = send(gg.at[2], gg.at[1], x_dev)

    rext, e1, e2, et, e3 = r.rext, r.e1, r.e2, r.et, r.e3

    def ext_grad():
        arrive(dx.at[1], tags["dx"], x_dev)
        arrive(gg.at[1], tags["gg"], x_dev)
        dxt = jnp.concatenate([dx[0].astype(single), dx[1].astype(single)], axis=0).T.astype(bfloat)
        px2 = px[...].reshape(2 * ROWS, 1024)
        d_gains = (gg[0] + gg[1]).astype(bfloat)
        x0[...] = dot(dxt, px2[:, 0:512])
        x1[...] = dot(dxt, px2[:, 512:1024]) + dot_tn(d_gains, rows_of.astype(bfloat))
        for d in range(4):
            for w in range(N_HID):
                s = (d * N_HID + w) * 24
                rext[d // 2, d % 2, w] = jnp.concatenate(
                    [x0[s : s + 24, :], x1[s : s + 24, :]], axis=0
                ).astype(bfloat)
        tags["e1"] = send(rext.at[:, 1 - core], e1, core_dev)

    def ext_y():
        arrive(e1, tags["e1"], core_dev)
        e1[...] = e1[...] + rext[:, core]
        tags["e2"] = send(e1.at[1 - y], e2, y_dev)

    def ext_z():
        arrive(e2, tags["e2"], y_dev)
        et[...] = e1[y] + e2[...]
        tags["e3"] = [send(et.at[z_up[k]], e3.at[k - 1], z_dev[k]) for k in range(1, N_HID)]

    def ext_end():
        total = et[z].astype(single)
        for k in range(1, N_HID):
            arrive(e3.at[k - 1], tags["e3"][k - 1], z_dev[k])
            total = total + e3[k - 1].astype(single)
        r.g_patch[:, 0:512] = total[0:24]
        r.g_patch[:, 512:768] = total[24:48, 0:256]
        r.g_table[...] = total[24:48, 256 : 256 + seq_len]
        columns = total[24:48, 256:512]
        pick_f = (iota((8, 256), 1) == iota((8, 256), 0) + seq_len).astype(single)
        r.g_gains[...] = dot_nt(pick_f, columns, precision=highest)[0:4]
        for name in ("g_patch", "g_table", "g_gains"):
            store(name)

    ff_down(2)
    ff_up(3)
    ff_y(0, 2)
    cut_branch()
    out_back()
    ff_down(1)
    ff_up(1)
    ff_y(0, 1)
    pass_rows()
    ff_y(1, 3)
    ff_up(2)
    ff_z(0, 2)
    ff_in(2)
    out_grad()
    ff_up(0)
    ff_in(0)
    ff_z(0, 1)
    ff_y(1, 2)
    lax.fori_loop(0, 1, attend_back, 0)
    lax.fori_loop(1, 2, attend_back, 0)
    ff_y(1, 1)
    ff_z(1, 3)
    ff_down(0)
    ff_in(3)
    ff_in(1)
    ff_down(3)
    out_y()
    lax.fori_loop(2, 3, attend_back, 0)
    ff_y(0, 3)
    ff_z(1, 1)
    ff_z(1, 2)
    mix_back()
    send_in()
    qkv_grad(0)
    qkv_y(0)
    qkv_grad(2)
    qkv_grad(1)
    qkv_y(2)
    out_z()
    qkv_y(1)
    ff_y(1, 0)
    norm_in()
    ff_z(0, 3)
    qkv_z(2)
    ext_grad()
    qkv_z(1)
    qkv_z(0)
    ext_y()
    head_grad()
    ext_z()
    ff_y(0, 0)
    ff_z(0, 0)
    qkv_end()
    ff_z(1, 0)
    out_end()
    ff_end()

    def read(prefix, kind):
        values = getattr(r, prefix + kind)[...]
        return values.reshape(-1, values.shape[-1])
    lane = iota((8, 128), 1)
    own = jnp.zeros((8, 128), single)
    grad_square = jnp.zeros((1, 1), single)
    for n, kind in enumerate(KINDS):
        own = jnp.where(lane == 8 + n, square_sum(read("w_", kind)), own)
        if n > 2:
            grad_square = grad_square + square_sum(read("g_", kind))
    ext_end()

    own = jnp.where(lane == 0, term, own)
    for kind in KINDS[0:3]:
        grad_square = grad_square + square_sum(read("g_", kind))
    own = jnp.where(lane == 1, grad_square, own)

    def all_sum(vector, pair, every):
        pair[0] = vector
        tag = send(pair.at[0], pair.at[1], core_dev)
        arrive(pair.at[1], tag, core_dev)
        every[h, y, z] = pair[0] + pair[1]
        mine = every.at[h, y, z]
        numbers = [send(mine, mine, device) for device in group_dev]
        for i, place in enumerate(source):
            arrive(every.at[place], numbers[i], core_dev)
        return jnp.sum(every[...].reshape(16, 8, 128), axis=0)

    sums = all_sum(own, r.l1, r.v1)
    grad_norm = jnp.sqrt(jnp.sum(jnp.where(lane == 1, sums, 0.0), axis=1, keepdims=True))[0:1]
    clip = jnp.minimum(1.0, clip_at / grad_norm)
    own = jnp.zeros((8, 128), single)
    for name in order[9:]:
        loads[name].wait()
    for n, kind in enumerate(KINDS):
        update = one_update(read("w_", kind), read("m_", kind), read("v_", kind), read("g_", kind), clip)[2]
        own = jnp.where(lane == 8 + n, square_sum(update), own)
    updates = all_sum(own, r.l2, r.v2)
    result = jnp.sqrt(sums) / jnp.sqrt(updates)
    result = jnp.where(lane == 0, sums, result)
    result = jnp.where(lane == 1, grad_norm, result)
    result = jnp.where(lane == 2, clip, result)
    r.scalars[...] = result
    store("scalars")
    for copy in stores:
        copy.wait()
    for key, copies in sends.items():

        def settle(copies=copies):
            for copy in copies:
                copy.wait_send()

        if key is None:
            settle()
        else:
            pl.when(holds[key])(settle)


def write_kernel(names, *refs):
    r = types.SimpleNamespace(**dict(zip(names, refs)))
    lane = iota((8, 128), 1)
    inputs = ["scalars"] + [p + k for k in KINDS for p in ("w_", "m_", "v_", "g_")]
    loads = {}
    for number, name in enumerate(inputs):
        loads[name] = pltpu.make_async_copy(
            getattr(r, "h_" + name), getattr(r, name), r.lsem.at[number]
        )
        loads[name].start()
    loads["scalars"].wait()

    def pick(n):
        return jnp.sum(jnp.where(lane == n, r.scalars[...], 0.0), axis=1, keepdims=True)[0:1]

    clip = pick(2)
    r.o_loss[...] = pick(0)
    r.o_norm[...] = pick(1)
    stores = []
    for n, kind in enumerate(KINDS):
        for p in ("w_", "m_", "v_", "g_"):
            loads[p + kind].wait()
        master = getattr(r, "w_" + kind)[...]
        grad = getattr(r, "g_" + kind)[...]
        ratio, c = pick(8 + n), clip
        if len(master.shape) == 3:
            c, ratio = clip[None], ratio[None]
        first, second, update = one_update(
            master, getattr(r, "m_" + kind)[...], getattr(r, "v_" + kind)[...], grad, c
        )
        results = (first, second, master - learn_rate * ratio * update)
        for p, value in zip(("nm_", "nv_", "nw_"), results):
            getattr(r, p + kind)[...] = value
            copy = pltpu.make_async_copy(
                getattr(r, p + kind),
                getattr(r, "h_" + p + kind),
                r.lsem.at[len(inputs) + len(stores)],
            )
            copy.start()
            stores.append(copy)
    for copy in stores:
        copy.wait()


def fast_device(patches, labels, *state):
    bfloat, single = jnp.bfloat16, jnp.float32

    def turn(kind, value):
        if kind in ("patch", "table", "down"):
            return value.T
        if kind == "qkv":
            return value.transpose(1, 0, 2)
        return value

    flat = [turn(KINDS[i % 8], value) for i, value in enumerate(state)]
    hbm = pl.BlockSpec(memory_space=pl.ANY)
    smem = pl.BlockSpec(memory_space=pltpu.SMEM)
    in_names = ["patches"] + [p + k for p in ("w_", "m_", "v_") for k in KINDS]
    out_names = ["g_" + k for k in KINDS] + ["scalars"]
    scratch = dict(
        px=((2, ROWS, 1024), bfloat),
        gext=((4, 4, 48, 512), bfloat),
        gqkv=((3, 2, 4, 2, 48, 384), bfloat),
        gout=((4, 4, 96, 256), bfloat),
        gup=((4, 2, 4, 96, 384), bfloat),
        gdn=((4, 2, 4, 96, 384), bfloat),
        ghd=((2, 4, 4, 48, 512), bfloat),
        x0=((384, 512), single),
        x1=((384, 512), single),
        hw=((2, 768, 512), bfloat),
        ga=((2, 8, 384), single),
        st=((2, 2, ROWS, 384), bfloat),
        nb=((2 * ROWS, 768), bfloat),
        nbt=((768, 2 * ROWS), bfloat),
        nq=((2, 2 * ROWS, 384), single),
        sq=((2, 2 * ROWS, 384), single),
        bd=((384, 384), bfloat),
        q=((12, ROWS, HD), bfloat),
        k=((12, ROWS, HD), bfloat),
        v=((12, ROWS, HD), bfloat),
        pr=((12, ROWS, ROWS), single),
        hof=((2 * ROWS, 384), bfloat),
        us=((4, 2 * ROWS, 384), single),
        hb=((4, 2 * ROWS, 384), bfloat),
        br=((2 * ROWS, 768), single),
        brs=((2, 2, ROWS, 384), bfloat),
        brr=((2, 2, ROWS, 384), bfloat),
        rw=((2, 8, 768), single),
        ds=((ROWS, 768), single),
        db=((2, ROWS, 768), bfloat),
        dbt=((768, 2 * ROWS), bfloat),
        al=((2, 2, 2, 4, 8, 256), single),
        rff=((4, 2, 2, 2, 2, 96, 384), bfloat),
        f1=((4, 2, 2, 2, 96, 384), bfloat),
        f2=((4, 2, 2, 96, 384), bfloat),
        ft=((3, 2, 2, 96, 384), bfloat),
        f3=((3, 2, 2, 96, 384), bfloat),
        rout=((4, 2, 2, 96, 256), bfloat),
        o1=((4, 2, 96, 256), bfloat),
        o2=((4, 96, 256), bfloat),
        ot=((4, 96, 256), bfloat),
        o3=((3, 96, 256), bfloat),
        dh=((12, ROWS, HD), bfloat),
        dm=((3, 2 * ROWS, 384), bfloat),
        pc=((4, 2 * ROWS, 192), bfloat),
        dqkv=((3, 2 * ROWS, 384), single),
        rqkv=((3, 2, 2, 2, 2, 48, 384), bfloat),
        q1=((3, 2, 2, 2, 48, 384), bfloat),
        q2=((3, 2, 2, 48, 384), bfloat),
        qt=((3, 2, 2, 48, 384), bfloat),
        q3=((3, 3, 48, 384), bfloat),
        dns=((ROWS, 768), bfloat),
        dnr=((ROWS, 768), bfloat),
        dx=((3, ROWS, 384), bfloat),
        gg=((3, 8, 384), single),
        rext=((2, 2, 4, 48, 512), bfloat),
        e1=((2, 4, 48, 512), bfloat),
        e2=((4, 48, 512), bfloat),
        et=((4, 48, 512), bfloat),
        e3=((3, 48, 512), bfloat),
        l1=((2, 8, 128), single),
        l2=((2, 8, 128), single),
        v1=((2, 2, 4, 8, 128), single),
        v2=((2, 2, 4, 8, 128), single),
    )
    semaphores = 320
    shapes = [flat[i].shape for i in range(8)]
    npatch, seq_len, classes = patches.shape[1], flat[1].shape[1], flat[3].shape[1]
    total_images = labels.shape[0] * lax.axis_size("dp")
    sizes = (npatch, seq_len, classes, total_images)
    held = [(patches.shape, bfloat)] + [(s, single) for s in shapes * 4] + [((8, 128), single)]
    names = ["labels"] + ["h_" + n for n in in_names + out_names] + in_names + out_names
    names += list(scratch) + ["ssem", "rsem", "lsem"]
    found = pl.pallas_call(
        functools.partial(step_kernel, sizes, names),
        out_shape=[jax.ShapeDtypeStruct(s, single) for s in shapes]
        + [jax.ShapeDtypeStruct((8, 128), single)],
        in_specs=[smem] + [hbm] * 25,
        out_specs=[hbm] * 9,
        scratch_shapes=[pltpu.VMEM(s, t) for s, t in held + list(scratch.values())]
        + [pltpu.SemaphoreType.DMA((semaphores,))] * 2
        + [pltpu.SemaphoreType.DMA((len(held),))],
        compiler_params=pltpu.CompilerParams(
            collective_id=0, has_side_effects=True, vmem_limit_bytes=62 * 2**20
        ),
        name="train_step",
    )(labels, patches, *flat)
    grads, scalars = found[:8], found[8]
    in_names = ["scalars"] + [p + k for p in ("w_", "m_", "v_", "g_") for k in KINDS]
    out_names = [p + k for p in ("nm_", "nv_", "nw_") for k in KINDS]
    held = [((8, 128), single)] + [(s, single) for s in shapes * 7]
    names = ["h_" + n for n in in_names + out_names] + ["o_loss", "o_norm"]
    names += in_names + out_names + ["lsem"]
    written = pl.pallas_call(
        functools.partial(write_kernel, names),
        out_shape=[jax.ShapeDtypeStruct(s, single) for s in shapes * 3 + [(1, 1), (1, 1)]],
        in_specs=[hbm] * 33,
        out_specs=[hbm] * 24 + [pl.BlockSpec(memory_space=pltpu.VMEM)] * 2,
        scratch_shapes=[pltpu.VMEM(s, t) for s, t in held]
        + [pltpu.SemaphoreType.DMA((len(held),))],
        compiler_params=pltpu.CompilerParams(vmem_limit_bytes=62 * 2**20),
        name="write_step",
    )(scalars, *flat, *grads)
    back = [turn(KINDS[i % 8], value) for i, value in enumerate(written[:24])]
    return (written[24].reshape(()), written[25].reshape(()), *back)


def fits(mesh):
    return tuple(mesh.shape[a] for a in ALL) == (4, 2, N_HID)


def solution(mesh):
    placed = (
        P(ALL, None, None),
        P("dp"),
        P(None, ALL),
        P(None, ALL),
        P(None, ALL),
        P(ALL, None),
        P(DATA, None, "heads"),
        P(MODEL, "dp"),
        P("dp", MODEL),
        P(MODEL, "dp"),
        P(None, ALL),
        P(None, ALL),
        P(None, ALL),
        P(ALL, None),
        P(DATA, None, "heads"),
        P(MODEL, "dp"),
        P("dp", MODEL),
        P(MODEL, "dp"),
        P(None, ALL),
        P(None, ALL),
        P(None, ALL),
        P(ALL, None),
        P(DATA, None, "heads"),
        P(MODEL, "dp"),
        P("dp", MODEL),
        P(MODEL, "dp"),
    )
    return jax.shard_map(
        fast_device if fits(mesh) else per_device,
        mesh=mesh,
        in_specs=placed,
        out_specs=(
            P(),
            P(),
            P(None, ALL),
            P(None, ALL),
            P(None, ALL),
            P(ALL, None),
            P(DATA, None, "heads"),
            P(MODEL, "dp"),
            P("dp", MODEL),
            P(MODEL, "dp"),
            P(None, ALL),
            P(None, ALL),
            P(None, ALL),
            P(ALL, None),
            P(DATA, None, "heads"),
            P(MODEL, "dp"),
            P("dp", MODEL),
            P(MODEL, "dp"),
            P(None, ALL),
            P(None, ALL),
            P(None, ALL),
            P(ALL, None),
            P(DATA, None, "heads"),
            P(MODEL, "dp"),
            P("dp", MODEL),
            P(MODEL, "dp"),
        ),
        check_vma=False,
    )
```

```python
import functools
import types

import jax
import jax.numpy as jnp
from jax import lax
from jax.experimental import pallas as pl
from jax.experimental.pallas import tpu as pltpu
from jax.sharding import PartitionSpec as P

HD = 64
PD = 768
STEP = 10
MESH = pl.DeviceIdType.MESH
ALL = ("dp", "heads", "hidden")
DATA = ("dp", "hidden")
MODEL = ("heads", "hidden")


beta_one = 0.9
beta_two = 0.999
adam_eps = 1e-08
decay_rate = 0.01
learn_rate = 0.5
clip_at = 0.001
norm_eps = 1e-06
highest = lax.Precision.HIGHEST


def layer_norm(values):
    center = values - jnp.mean(values, axis=-1, keepdims=True)
    return center * lax.rsqrt(jnp.mean(center * center, axis=-1, keepdims=True) + norm_eps)


def head_loss(stream_out, targets, final_gain, head_weight, npatch, total_images):
    normed_out, norm_back = jax.vjp(layer_norm, stream_out)
    final = normed_out * final_gain
    pooled_b = jnp.mean(final[:, :npatch], axis=1).astype(jnp.bfloat16)
    logits = jnp.dot(pooled_b, head_weight, preferred_element_type=jnp.float32)
    log_total = jax.nn.logsumexp(logits, axis=-1)
    onehot = (targets[:, None] == lax.broadcasted_iota(jnp.int32, logits.shape, 1)).astype(
        jnp.float32
    )
    terms = log_total - jnp.sum(logits * onehot, axis=-1)
    d_logits = (jnp.exp(logits - log_total[:, None]) - onehot) / total_images
    d_pooled = jnp.dot(d_logits, head_weight.astype(jnp.float32).T, precision=highest)
    count, seq_len, width = stream_out.shape
    spread = jnp.broadcast_to(d_pooled[:, None, :] / npatch, (count, npatch, width))
    d_final = jnp.concatenate(
        [spread, jnp.zeros((count, seq_len - npatch, width), jnp.float32)], axis=1
    )
    d_stream = norm_back(d_final * final_gain)[0]
    d_gain_rows = jnp.sum(d_final * normed_out, axis=1)
    return (terms, pooled_b, d_logits, d_stream, d_gain_rows)


def per_device(
    patches,
    labels,
    w_patch,
    table,
    gains,
    w_head,
    w_qkv,
    w_out,
    w_up,
    w_down,
    first_patch,
    first_table,
    first_gains,
    first_head,
    first_qkv,
    first_out,
    first_up,
    first_down,
    second_patch,
    second_table,
    second_gains,
    second_head,
    second_qkv,
    second_out,
    second_up,
    second_down,
):
    masters = [w_patch, table, gains, w_head, w_qkv, w_out, w_up, w_down]
    firsts = [
        first_patch,
        first_table,
        first_gains,
        first_head,
        first_qkv,
        first_out,
        first_up,
        first_down,
    ]
    seconds = [
        second_patch,
        second_table,
        second_gains,
        second_head,
        second_qkv,
        second_out,
        second_up,
        second_down,
    ]
    bfloat = jnp.bfloat16
    single = jnp.float32
    patch_b, table_b, gains_b, head_b = (
        lax.all_gather(w_patch.astype(bfloat), ALL, axis=1, tiled=True),
        lax.all_gather(table.astype(bfloat), ALL, axis=1, tiled=True),
        lax.all_gather(gains.astype(bfloat), ALL, axis=1, tiled=True),
        lax.all_gather(w_head.astype(bfloat), ALL, axis=0, tiled=True),
    )
    qkv_b = lax.all_gather(w_qkv.astype(bfloat), DATA, axis=0, tiled=True)
    out_b, up_b, down_b = (
        lax.all_gather(w_out.astype(bfloat), "dp", axis=1, tiled=True),
        lax.all_gather(w_up.astype(bfloat), "dp", axis=0, tiled=True),
        lax.all_gather(w_down.astype(bfloat), "dp", axis=1, tiled=True),
    )
    gain_vals = gains_b.astype(single)
    table_vals = table_b.astype(single)
    n_hidden = lax.axis_size("hidden")
    n_own = patches.shape[0]
    npatch = patches.shape[1]
    seq_len = table_b.shape[0]
    width = patch_b.shape[1]
    group_width = qkv_b.shape[2]
    group_heads = group_width // HD
    own_index = lax.axis_index("heads") * n_hidden + lax.axis_index("hidden")
    total_images = labels.shape[0] * lax.axis_size("dp")
    embedded = jnp.dot(patches.reshape(n_own * npatch, PD), patch_b, preferred_element_type=single)
    embedded = embedded.reshape(n_own, npatch, width) + table_vals[:npatch]
    registers = jnp.broadcast_to(table_vals[npatch:], (n_own, seq_len - npatch, width))
    stream_own = jnp.concatenate([embedded, registers], axis=1).astype(bfloat)
    stream_in = lax.all_gather(stream_own, MODEL, axis=0, tiled=True)
    n_img = stream_in.shape[0]
    row_count = n_img * seq_len
    stream_flat = stream_in.astype(single).reshape(row_count, width)
    normed_b = (layer_norm(stream_flat) * gain_vals[0]).astype(bfloat)
    n_att = n_img // n_hidden
    att_start = lax.axis_index("hidden") * n_att
    normed_att = lax.dynamic_slice_in_dim(
        normed_b.reshape(n_img, seq_len, width), att_start, n_att, 0
    )
    query_gain = lax.dynamic_slice_in_dim(
        gain_vals[2], lax.axis_index("heads") * group_width, group_width, 0
    ).reshape(group_heads, HD)
    key_gain = lax.dynamic_slice_in_dim(
        gain_vals[3], lax.axis_index("heads") * group_width, group_width, 0
    ).reshape(group_heads, HD)
    mixed = jnp.einsum("bsd,dcf->bscf", normed_att, qkv_b, preferred_element_type=single)
    mixed = mixed.reshape(n_att, seq_len, 3, group_heads, HD)
    query_norm, query_back = jax.vjp(layer_norm, mixed[:, :, 0])
    key_norm, key_back = jax.vjp(layer_norm, mixed[:, :, 1])
    queries = (query_norm * query_gain).astype(bfloat)
    keys = (key_norm * key_gain).astype(bfloat)
    values = mixed[:, :, 2].astype(bfloat)
    scale = HD ** (-0.5)
    scores = jnp.einsum("bqhd,bkhd->bhqk", queries, keys, preferred_element_type=single) * scale
    probs = jax.nn.softmax(scores, axis=-1)
    probs_b = probs.astype(bfloat)
    heads_out = jnp.einsum("bhqk,bkhd->bqhd", probs_b, values, preferred_element_type=single)
    heads_out = heads_out.astype(bfloat).reshape(n_att * seq_len, group_width)
    columns = lax.all_to_all(heads_out, "hidden", split_axis=1, concat_axis=0, tiled=True)
    attn_part = jnp.dot(columns, out_b, preferred_element_type=single)
    upper = jnp.dot(normed_b, up_b, preferred_element_type=single)
    activated, gelu_back = jax.vjp(jax.nn.gelu, upper)
    activated_b = activated.astype(bfloat)
    partial_sum = attn_part + jnp.dot(activated_b, down_b, preferred_element_type=single)
    total = lax.psum(partial_sum, MODEL)
    stream_out = (stream_flat + total).reshape(n_img, seq_len, width)
    terms, pooled_b, d_logits, d_stream, d_gain_rows = head_loss(
        stream_out, labels, gain_vals[1], head_b, npatch, total_images
    )
    loss_terms = lax.dynamic_slice_in_dim(terms, own_index * n_own, n_own, 0)
    pooled_own = lax.dynamic_slice_in_dim(pooled_b, own_index * n_own, n_own, 0)
    logits_own = lax.dynamic_slice_in_dim(d_logits, own_index * n_own, n_own, 0)
    d_head = jnp.dot(pooled_own.astype(single).T, logits_own, precision=highest)
    d_final_gain = jnp.sum(
        lax.dynamic_slice_in_dim(d_gain_rows, own_index * n_own, n_own, 0), axis=0
    )
    d_stream_own = lax.dynamic_slice_in_dim(d_stream, own_index * n_own, n_own, 0)
    d_branch = d_stream.reshape(row_count, width).astype(bfloat)
    d_activated = jnp.dot(d_branch, down_b.T, preferred_element_type=single)
    d_upper = gelu_back(d_activated)[0].astype(bfloat)
    d_down = jnp.dot(activated_b.T, d_branch, preferred_element_type=single)
    d_up = jnp.dot(normed_b.T, d_upper, preferred_element_type=single)
    d_normed = jnp.dot(d_upper, up_b.T, preferred_element_type=single)
    d_out = jnp.dot(columns.T, d_branch, preferred_element_type=single)
    d_columns = jnp.dot(d_branch, out_b.T, preferred_element_type=single).astype(bfloat)
    d_heads = lax.all_to_all(d_columns, "hidden", split_axis=0, concat_axis=1, tiled=True).reshape(
        n_att, seq_len, group_heads, HD
    )
    d_probs = jnp.einsum("bqhd,bkhd->bhqk", d_heads, values, preferred_element_type=single)
    d_values = jnp.einsum("bhqk,bqhd->bkhd", probs_b, d_heads, preferred_element_type=single)
    d_scores = (probs * (d_probs - jnp.sum(probs * d_probs, axis=-1, keepdims=True))).astype(bfloat)
    d_query_norm = (
        jnp.einsum("bhqk,bkhd->bqhd", d_scores, keys, preferred_element_type=single) * scale
    )
    d_key_norm = (
        jnp.einsum("bhqk,bqhd->bkhd", d_scores, queries, preferred_element_type=single) * scale
    )
    d_queries = query_back(d_query_norm * query_gain)[0]
    d_keys = key_back(d_key_norm * key_gain)[0]
    d_query_gain = jnp.sum(d_query_norm * query_norm, axis=(0, 1)).reshape(group_width)
    d_key_gain = jnp.sum(d_key_norm * key_norm, axis=(0, 1)).reshape(group_width)
    d_mixed = (
        jnp.stack([d_queries, d_keys, d_values], axis=2)
        .astype(bfloat)
        .reshape(n_att, seq_len, 3, group_width)
    )
    d_qkv = jnp.einsum("bsd,bscf->dcf", normed_att, d_mixed, preferred_element_type=single)
    d_att_in = jnp.einsum("bscf,dcf->bsd", d_mixed, qkv_b, preferred_element_type=single)
    d_normed = d_normed.reshape(n_img, seq_len, width)
    d_normed = lax.dynamic_update_slice_in_dim(
        d_normed, lax.dynamic_slice_in_dim(d_normed, att_start, n_att, 0) + d_att_in, att_start, 0
    )
    d_normed_own = lax.psum_scatter(
        d_normed.reshape(row_count, width).astype(jnp.bfloat16),
        MODEL,
        scatter_dimension=0,
        tiled=True,
    ).astype(jnp.float32)
    d_normed_own = d_normed_own.reshape(n_own, seq_len, width)
    normed_own, block_back = jax.vjp(layer_norm, stream_own.astype(single))
    d_stream_in = d_stream_own + block_back(d_normed_own * gain_vals[0])[0]
    d_block_gain = jnp.sum(d_normed_own * normed_own, axis=(0, 1))
    d_patch = jnp.dot(
        patches.reshape(n_own * npatch, PD).astype(single).T,
        d_stream_in[:, :npatch].reshape(n_own * npatch, width),
        precision=highest,
    )
    d_table = jnp.sum(d_stream_in, axis=0)
    zero_row = jnp.zeros((width,), single)
    gain_offset = lax.axis_index("heads") * group_width
    d_gains = jnp.stack(
        [
            d_block_gain,
            d_final_gain,
            lax.dynamic_update_slice_in_dim(zero_row, d_query_gain, gain_offset, 0),
            lax.dynamic_update_slice_in_dim(zero_row, d_key_gain, gain_offset, 0),
        ]
    )
    grad_patch, grad_table, grad_gains, grad_head = (
        lax.psum_scatter(d_patch, ALL, scatter_dimension=1, tiled=True),
        lax.psum_scatter(d_table, ALL, scatter_dimension=1, tiled=True),
        lax.psum_scatter(d_gains, ALL, scatter_dimension=1, tiled=True),
        lax.psum_scatter(d_head, ALL, scatter_dimension=0, tiled=True),
    )
    grad_qkv = lax.psum_scatter(d_qkv, DATA, scatter_dimension=0, tiled=True)
    grad_out, grad_up, grad_down = (
        lax.psum_scatter(d_out.astype(jnp.bfloat16), "dp", scatter_dimension=1, tiled=True).astype(
            jnp.float32
        ),
        lax.psum_scatter(d_up.astype(jnp.bfloat16), "dp", scatter_dimension=0, tiled=True).astype(
            jnp.float32
        ),
        lax.psum_scatter(d_down.astype(jnp.bfloat16), "dp", scatter_dimension=1, tiled=True).astype(
            jnp.float32
        ),
    )
    grads = [grad_patch, grad_table, grad_gains, grad_head, grad_qkv, grad_out, grad_up, grad_down]
    grad_squares = jnp.stack([jnp.sum(grad * grad) for grad in grads])
    weight_squares = jnp.stack([jnp.sum(master * master) for master in masters])
    grad_squares, weight_squares, loss_sum = lax.psum(
        (grad_squares, weight_squares, jnp.sum(loss_terms)), ALL
    )
    grad_norm = jnp.sqrt(jnp.sum(grad_squares))
    clip = jnp.minimum(1.0, clip_at / grad_norm)
    new_firsts, new_seconds, updates = ([], [], [])
    for master, first, second, grad in zip(masters, firsts, seconds, grads):
        clipped = grad * clip
        first_new = beta_one * first + (1.0 - beta_one) * clipped
        second_new = beta_two * second + (1.0 - beta_two) * clipped * clipped
        update = (
            first_new
            / (1.0 - beta_one**STEP)
            / (jnp.sqrt(second_new / (1.0 - beta_two**STEP)) + adam_eps)
        )
        updates.append(update + decay_rate * master)
        new_firsts.append(first_new)
        new_seconds.append(second_new)
    update_squares = lax.psum(
        jnp.stack([jnp.sum(update * update) for update in updates]), ALL
    )
    ratios = jnp.sqrt(weight_squares) / jnp.sqrt(update_squares)
    new_weights = [
        master - learn_rate * ratios[number] * update
        for number, (master, update) in enumerate(zip(masters, updates))
    ]
    return (
        loss_sum,
        grad_norm,
        new_firsts[0],
        new_firsts[1],
        new_firsts[2],
        new_firsts[3],
        new_firsts[4],
        new_firsts[5],
        new_firsts[6],
        new_firsts[7],
        new_seconds[0],
        new_seconds[1],
        new_seconds[2],
        new_seconds[3],
        new_seconds[4],
        new_seconds[5],
        new_seconds[6],
        new_seconds[7],
        new_weights[0],
        new_weights[1],
        new_weights[2],
        new_weights[3],
        new_weights[4],
        new_weights[5],
        new_weights[6],
        new_weights[7],
    )


def dot(a, b):
    return jnp.dot(a, b, preferred_element_type=jnp.float32)


def dot_nt(a, b, precision=None):
    return lax.dot_general(
        a, b, (((1,), (1,)), ((), ())), precision=precision, preferred_element_type=jnp.float32
    )


def dot_tn(a, b, precision=None):
    return lax.dot_general(
        a, b, (((0,), (0,)), ((), ())), precision=precision, preferred_element_type=jnp.float32
    )


def norm_parts(values):
    center = values - jnp.mean(values, axis=-1, keepdims=True)
    scale = lax.rsqrt(jnp.mean(center * center, axis=-1, keepdims=True) + norm_eps)
    return center * scale, scale


def norm_back(normed, scale, grad):
    inner = jnp.mean(grad * normed, axis=-1, keepdims=True)
    return scale * (grad - jnp.mean(grad, axis=-1, keepdims=True) - normed * inner)


gelu_c = 0.7978845608028654


def gelu_tanh(u):
    return jnp.tanh(gelu_c * (u + 0.044715 * (u * u * u)))


def iota(shape, axis):
    return lax.broadcasted_iota(jnp.int32, shape, axis)


def one_update(master, first, second, grad, clip):
    clipped = grad * clip
    first_new = beta_one * first + (1.0 - beta_one) * clipped
    second_new = beta_two * second + (1.0 - beta_two) * clipped * clipped
    one, two = 1.0 / (1.0 - beta_one**STEP), 1.0 / (1.0 - beta_two**STEP)
    update = (first_new * one) / (jnp.sqrt(second_new * two) + adam_eps)
    return first_new, second_new, update + decay_rate * master


def square_sum(values):
    return jnp.sum(values * values, axis=(0, 1), keepdims=True)


KINDS = ("patch", "table", "gains", "head", "qkv", "out", "up", "down")
EXT, QKV, UP0, UP1, HEAD, OUT, DN0, DN1 = range(8)
LEFT, RIGHT, ON_LEFT, ON_RIGHT = "left", "right", "on_left", "on_right"
ROWS = 208
N_HID = 4


def step_kernel(sizes, names, *refs):
    npatch, seq_len, classes, total_images = sizes
    r = types.SimpleNamespace(**dict(zip(names, refs)))
    bfloat, single = jnp.bfloat16, jnp.float32
    dp, h, z = (lax.axis_index(a) for a in ALL)
    core, y = lax.rem(dp, 2), dp // 2
    y_dp, core_dp = (1 - y) * 2 + core, y * 2 + (1 - core)
    x_dev, y_dev, core_dev = (dp, 1 - h, z), (y_dp, h, z), (core_dp, h, z)
    z_up = [lax.rem(z + k, N_HID) for k in range(N_HID)]
    z_down = [lax.rem(z + N_HID - k, N_HID) for k in range(N_HID)]
    z_dev = [(dp, h, z_up[k]) for k in range(N_HID)]
    group = [(h, y, z_up[k]) for k in range(1, N_HID)]
    for gh, gy in ((1 - h, y), (h, 1 - y), (1 - h, 1 - y)):
        group.extend((gh, gy, z_up[k]) for k in range(N_HID))
    source = [(h, y, z_down[k]) for k in range(1, N_HID)]
    for gh, gy in ((1 - h, y), (h, 1 - y), (1 - h, 1 - y)):
        source.extend((gh, gy, z_down[k]) for k in range(N_HID))
    group_dev = [(gy * 2 + core, gh, gz) for gh, gy, gz in group]

    barrier = pltpu.get_barrier_semaphore()
    for device in [core_dev] + group_dev:
        pl.semaphore_signal(barrier, inc=1, device_id=device, device_id_type=MESH)

    loads = {}
    order = ["w_up", "w_patch", "w_table", "w_gains"]
    order += ["w_" + k for k in KINDS if "w_" + k not in order] + ["patches"]
    order += [p + k for p in ("m_", "v_") for k in KINDS]

    def load(names):
        for name in names:
            loads[name] = pltpu.make_async_copy(
                getattr(r, "h_" + name), getattr(r, name), r.lsem.at[order.index(name)]
            )
            loads[name].start()

    load(order[0:9])
    stores = []

    def store(name):
        copy = pltpu.make_async_copy(
            getattr(r, name), getattr(r, "h_" + name), r.lsem.at[len(order) + len(stores)]
        )
        copy.start()
        stores.append(copy)

    ssem, rsem = r.ssem, r.rsem
    count = [0]
    sends = {}
    last = N_HID - 1
    holds = {}
    for d in range(1, N_HID):
        holds[LEFT, d] = z >= d
        holds[RIGHT, d] = z + d <= last
        holds[ON_RIGHT, d] = (z >= d) & (z < last)
        holds[ON_LEFT, d] = (z + d <= last) & (z > 0)
    holds[ON_RIGHT, 0] = z < last
    holds[ON_LEFT, 0] = z > 0
    next_z = {LEFT: (dp, h, z_up[1]), RIGHT: (dp, h, z_down[1])}

    def send(source, target, device, key=None):
        number = count[0]
        count[0] += 1
        copy = pltpu.make_async_remote_copy(
            src_ref=source,
            dst_ref=target,
            send_sem=ssem.at[number],
            recv_sem=rsem.at[number],
            device_id=device,
            device_id_type=MESH,
        )
        if key is None:
            copy.start()
        else:
            pl.when(holds[key])(copy.start)
        sends.setdefault(key, []).append(copy)
        return number

    def arrive(target, number, device):
        pltpu.make_async_remote_copy(
            src_ref=target,
            dst_ref=target,
            send_sem=ssem.at[number],
            recv_sem=rsem.at[number],
            device_id=device,
            device_id_type=MESH,
        ).wait_recv()

    gext, gqkv, gout, gup, gdn, ghd = r.gext, r.gqkv, r.gout, r.gup, r.gdn, r.ghd
    x0, x1, px = r.x0, r.x1, r.px
    kept = types.SimpleNamespace()

    def pack_ext():
        x1[0:24, :] = jnp.zeros((24, 512), single)
        for name in order[1:4]:
            loads[name].wait()
        x1[0:24, 256 : 256 + seq_len] = r.w_table[...]
        pick = (iota((4, 256), 1) == iota((4, 256), 0) + seq_len).astype(bfloat)
        table_part = x1[0:24, 256:512] + dot_tn(r.w_gains[...].astype(bfloat), pick)
        wp = r.w_patch[...]
        gext[dp, z] = jnp.concatenate(
            [wp[:, 0:512], jnp.concatenate([wp[:, 512:768], table_part], axis=1)], axis=0
        ).astype(bfloat)

    def pack_patches():
        row, col = iota((ROWS, 256), 0), iota((ROWS, 256), 1)
        spot = jnp.where((row == col) & (row < seq_len), 1.0, 0.0).astype(bfloat)
        px[0, :, 768:1024] = spot
        px[1, :, 768:1024] = spot
        px[0, ROWS - 16 : ROWS, 0:768] = jnp.zeros((16, 768), bfloat)
        loads["patches"].wait()
        px[0, 0:npatch, 0:768] = r.patches[0]

    def pack_qkv():
        loads["w_qkv"].wait()
        gqkv[:, z // 2, dp, lax.rem(z, 2)] = r.w_qkv[...].astype(bfloat)

    def pack_up():
        loads["w_up"].wait()
        gup[z, :, dp] = r.w_up[...].astype(bfloat).reshape(2, 96, 384)

    def pack_head():
        loads["w_head"].wait()
        x0[0:24, :] = r.w_head[:, 0:512]
        x1[0:24, :] = jnp.zeros((24, 512), single)
        x1[0:24, 0 : classes - 512] = r.w_head[:, 512:classes]
        ghd[h, dp, z] = jnp.concatenate([x0[0:24, :], x1[0:24, :]], axis=0).astype(bfloat)

    def pack_out():
        loads["w_out"].wait()
        gout[dp, z] = jnp.zeros((96, 256), bfloat)
        gout[dp, z, :, 0:192] = r.w_out[...].astype(bfloat)

    def pack_down():
        loads["w_down"].wait()
        gdn[z, :, y, core] = r.w_down[...].astype(bfloat).reshape(2, 96, 384)

    def at_ext(d, w):
        return gext.at[d, w]

    def at_qkv(d, w):
        return gqkv.at[:, w // 2, d, lax.rem(w, 2)]

    def at_out(d, w):
        return gout.at[d, w]

    def at_up(half):
        return lambda d, w: gup.at[w, half, d]

    def at_dn(half):
        return lambda d, w: gdn.at[w, half, d // 2, lax.rem(d, 2)]

    def at_hd(d, w):
        return ghd.at[h, d, w]

    slot = {
        EXT: at_ext,
        QKV: at_qkv,
        OUT: at_out,
        UP0: at_up(0),
        UP1: at_up(1),
        DN0: at_dn(0),
        DN1: at_dn(1),
        HEAD: at_hd,
    }
    lines = {
        EXT: lambda d: gext.at[d],
        QKV: lambda d: gqkv.at[:, :, d],
        OUT: lambda d: gout.at[d],
        UP0: lambda d: gup.at[:, 0, d],
        UP1: lambda d: gup.at[:, 1, d],
        DN0: lambda d: gdn.at[:, 0, d // 2, lax.rem(d, 2)],
        DN1: lambda d: gdn.at[:, 1, d // 2, lax.rem(d, 2)],
        HEAD: lambda d: ghd.at[h, d],
    }
    tags = {}

    def own_z(name):
        own = slot[name](dp, z)
        tags[name, LEFT, 1] = send(own, own, next_z[LEFT], (ON_RIGHT, 0))
        tags[name, RIGHT, 1] = send(own, own, next_z[RIGHT], (ON_LEFT, 0))

    def own_y(name):
        own = slot[name](dp, z)
        tags[name, "y", 0] = send(own, own, y_dev)

    def pass_z(name, d):
        for side, on, theirs in ((LEFT, ON_RIGHT, z_down[d]), (RIGHT, ON_LEFT, z_up[d])):
            block = slot[name](dp, theirs)
            number = tags[name, side, d]
            pl.when(holds[side, d])(functools.partial(arrive, block, number, y_dev))
            if d < last:
                tags[name, side, d + 1] = send(block, block, next_z[side], (on, d))
            tags[name, "y", side, d] = send(block, block, y_dev, (side, d))
        if d == last and name != HEAD:
            line = lines[name](dp)
            tags[name, "c", 0] = send(line, line, core_dev)

    def pair_own():
        arrive(slot[DN0](y_dp, z), tags[DN0, "y", 0], y_dev)
        own = gdn.at[z, 0, :, core]
        tags[DN0, LEFT, 1] = send(own, own, next_z[LEFT], (ON_RIGHT, 0))
        tags[DN0, RIGHT, 1] = send(own, own, next_z[RIGHT], (ON_LEFT, 0))

    def pair_z(d):
        for side, on, theirs in ((LEFT, ON_RIGHT, z_down[d]), (RIGHT, ON_LEFT, z_up[d])):
            block = gdn.at[theirs, 0, :, core]
            number = tags[DN0, side, d]
            pl.when(holds[side, d])(functools.partial(arrive, block, number, y_dev))
            if d < last:
                tags[DN0, side, d + 1] = send(block, block, next_z[side], (on, d))
        if d == last:
            block = gdn.at[:, 0, :, core]
            tags[DN0, "c", 0] = send(block, block, core_dev)

    def pair_complete():
        arrive(gdn.at[:, 0, :, 1 - core], tags[DN0, "c", 0], core_dev)

    def pass_core(name):
        at = slot[name]
        arrive(at(y_dp, z), tags[name, "y", 0], y_dev)
        for d in range(1, N_HID):
            for side, theirs in ((LEFT, z_down[d]), (RIGHT, z_up[d])):
                number = tags[name, "y", side, d]
                pl.when(holds[side, d])(functools.partial(arrive, at(y_dp, theirs), number, y_dev))
        line = lines[name](y_dp)
        if name != HEAD:
            tags[name, "c", 1] = send(line, line, core_dev)
        else:
            own = lines[name](dp)
            tags[name, "x", 0] = send(own, own, x_dev)
            tags[name, "x", 1] = send(line, line, x_dev)

    def complete(name):
        far = (1 - y) * 2 + (1 - core)
        arrive(lines[name](core_dp), tags[name, "c", 0], core_dev)
        arrive(lines[name](far), tags[name, "c", 1], core_dev)

    def head_core():
        for i, d in enumerate((dp, y_dp)):
            arrive(ghd.at[1 - h, d], tags[HEAD, "x", i], x_dev)
        for i, d in enumerate((dp, y_dp)):
            block = ghd.at[:, d]
            tags[HEAD, "c", i] = send(block, block, core_dev)

    def head_complete():
        far = (1 - y) * 2 + (1 - core)
        for i, d in enumerate((core_dp, far)):
            arrive(ghd.at[:, d], tags[HEAD, "c", i], core_dev)

    def send_images():
        images = px.at[0, :, pl.ds(0, 768)]
        tags["px"] = send(images, px.at[1, :, pl.ds(0, 768)], x_dev)

    ga, st = r.ga, r.st
    rows_of = (iota((8, 512), 1) == iota((8, 512), 0) + (256 + seq_len)) & (iota((8, 512), 0) < 4)

    def unpack(block_of, low, high):
        for d in range(4):
            for w in range(N_HID):
                s = (d * N_HID + w) * 24
                block = block_of(d, w).astype(single)
                low[s : s + 24, :] = block[0:24]
                high[s : s + 24, :] = block[24:48]

    def embed(i):
        if i == 0:
            unpack(lambda d, w: gext[d, w], x0, x1)
            ga[h] = dot_nt(rows_of.astype(bfloat), x1[...].astype(bfloat))
            tags["ga"] = send(ga.at[h], ga.at[h], x_dev)
        else:
            arrive(px.at[1, :, pl.ds(0, 768)], tags["px"], x_dev)
        low, high = x0[...].astype(bfloat), x1[...].astype(bfloat)
        made = dot_nt(px[i, :, 0:512], low) + dot_nt(px[i, :, 512:1024], high)
        st[h, i] = made.astype(bfloat)
        tags["st", i] = send(st.at[h, i], st.at[h, 1 - i], x_dev)

    def gain_row(i):
        return jnp.concatenate([ga[0, i : i + 1, :], ga[1, i : i + 1, :]], axis=1)

    def head_gain(i):
        pieces = []
        both = [ga[0, i : i + 1, :], ga[1, i : i + 1, :]]
        for d in range(4):
            pieces.extend(half[:, d * 96 : d * 96 + 96] for half in both)
        low = jnp.concatenate(pieces[0:4], axis=1)
        high = jnp.concatenate(pieces[4:8], axis=1)
        return jnp.where(h == 0, low, high)

    nb, nbt = r.nb, r.nbt

    def block_norm():
        arrive(ga.at[1 - h], tags["ga"], x_dev)
        arrive(st.at[1 - h, 1], tags["st", 0], x_dev)
        arrive(st.at[1 - h, 0], tags["st", 1], x_dev)
        gain = gain_row(0)
        for i in range(2):
            stream = jnp.concatenate([st[0, i], st[1, i]], axis=1).astype(single)
            nb[i * ROWS : (i + 1) * ROWS, :] = (norm_parts(stream)[0] * gain).astype(bfloat)

    nq, sq, bd = r.nq, r.sq, r.bd
    q_ref, k_ref, v_ref = r.q, r.k, r.v

    def head_mean(values):
        return dot(values.astype(bfloat), bd[...])

    def project(c):
        mixed = dot(nb[...], gqkv[c].reshape(768, 384))
        if c == 0:
            same = iota((384, 384), 0) // HD == iota((384, 384), 1) // HD
            bd[...] = jnp.where(same, 1.0 / HD, 0.0).astype(bfloat)
        if c < 2:
            top = mixed.astype(bfloat).astype(single)
            center = mixed - (head_mean(top) + head_mean(mixed - top))
            scale = lax.rsqrt(head_mean(center * center) + norm_eps)
            normed = center * scale
            nq[c] = normed
            sq[c] = scale
            mixed = normed * head_gain(2 + c)
        out = (q_ref, k_ref, v_ref)[c]
        mixed = mixed.astype(bfloat)
        for n in range(6):
            part = mixed[:, n * HD : (n + 1) * HD]
            out[2 * n] = part[0:ROWS]
            out[2 * n + 1] = part[ROWS : 2 * ROWS]

    pr, hof = r.pr, r.hof
    dead = iota((ROWS, ROWS), 1) >= seq_len

    def attend(pair, carry):
        for i in range(2):
            made = []
            for side in range(2):
                n = 4 * pair + 2 * side + i
                scores = dot_nt(q_ref[n], k_ref[n]) * HD ** (-0.5)
                scores = jnp.where(dead, -1e30, scores)
                scores = scores - jnp.max(scores, axis=-1, keepdims=True)
                weights = jnp.exp(scores)
                probs = weights / jnp.sum(weights, axis=-1, keepdims=True)
                pr[n] = probs
                made.append(dot(probs.astype(bfloat), v_ref[n]))
            both = jnp.concatenate(made, axis=1).astype(bfloat)
            hof[i * ROWS : (i + 1) * ROWS, pl.ds(pl.multiple_of(pair * 128, 128), 128)] = both
        return carry

    us, hb, br = r.us, r.hb, r.br

    def rise(w, carry):
        upper = dot(nb[...], gup[w].reshape(768, 384))
        us[w] = upper
        hb[w] = (0.5 * upper * (1.0 + gelu_tanh(upper))).astype(bfloat)
        return carry

    def project_out():
        lefts, rights = [], []
        for d in range(4):
            part = dot(hof[...], gout[d].reshape(384, 256))
            lefts.append(part[:, 0:96])
            rights.append(part[:, 96:192])
        br[:, 0:384] = jnp.concatenate(lefts, axis=1)
        br[:, 384:768] = jnp.concatenate(rights, axis=1)

    def turn_normed():
        nbt[...] = nb[...].T

    brs, brr = r.brs, r.brr

    def fall(half):
        lanes = slice(half * 384, half * 384 + 384)

        def add(w, carry):
            br[:, lanes] += dot_nt(hb[w], gdn[w, half].reshape(384, 384))
            return carry

        lax.fori_loop(0, N_HID, add, 0)

    def share(half, i):
        lanes = slice(half * 384, half * 384 + 384)
        brs[half, i] = br[i * ROWS : (i + 1) * ROWS, lanes].astype(bfloat)
        tags["br", half, i] = send(brs.at[half, i], brr.at[half, 1 - i], x_dev)

    hw = r.hw

    def unpack_head():
        for a in range(2):
            unpack(lambda d, w: ghd[a, d, w], x0, x1)
            hw[0, a * 384 : a * 384 + 384, :] = x0[...].astype(bfloat)
            hw[1, a * 384 : a * 384 + 384, :] = x1[...].astype(bfloat)

    def stream_out(i):
        for half in range(2):
            arrive(brr.at[half, i], tags["br", half, 1 - i], x_dev)
        stream = jnp.concatenate([st[0, i], st[1, i]], axis=1).astype(single)
        theirs = jnp.concatenate([brr[0, i], brr[1, i]], axis=1).astype(single)
        return norm_parts(stream + (br[i * ROWS : (i + 1) * ROWS, :] + theirs))

    pl.semaphore_wait(barrier, 1 + len(group_dev))
    pack_up()
    own_z(UP1)
    own_y(UP1)
    pack_ext()
    own_z(EXT)
    own_z(UP0)
    own_y(UP0)
    pack_patches()
    pack_head()
    pack_down()
    own_y(DN0)
    pass_z(UP1, 1)
    pass_z(EXT, 1)
    send_images()
    pass_z(UP0, 1)
    own_y(EXT)
    own_z(HEAD)
    pass_z(EXT, 2)
    pass_z(UP1, 2)
    pack_qkv()
    own_y(QKV)
    own_z(QKV)
    pass_z(EXT, 3)
    pack_out()
    own_z(OUT)
    pass_z(HEAD, 1)
    pass_z(UP1, 3)
    pair_own()
    pass_z(UP0, 2)
    pass_core(EXT)
    complete(EXT)
    pass_z(QKV, 1)
    embed(0)
    load(order[9:])
    pass_z(HEAD, 2)
    embed(1)
    pass_z(UP0, 3)
    pass_core(UP1)
    own_y(HEAD)
    pass_z(QKV, 2)
    pass_z(OUT, 1)
    pass_core(UP0)
    own_z(DN1)
    pass_z(HEAD, 3)
    pass_z(QKV, 3)
    complete(UP0)
    complete(UP1)
    pair_z(1)
    own_y(OUT)
    pass_z(OUT, 2)
    block_norm()
    lax.fori_loop(0, 2, rise, 0)
    lax.fori_loop(2, 4, rise, 0)
    pass_z(DN1, 1)
    pass_core(HEAD)
    pass_core(QKV)
    pass_z(OUT, 3)
    own_y(DN1)
    pair_z(2)
    complete(QKV)
    project(0)
    project(1)
    project(2)
    lax.fori_loop(0, 1, attend, 0)
    lax.fori_loop(1, 2, attend, 0)
    pass_core(OUT)
    pass_z(DN1, 2)
    pair_z(3)
    lax.fori_loop(2, 3, attend, 0)
    complete(OUT)
    project_out()
    pair_complete()
    fall(0)
    share(0, 1)
    share(0, 0)
    pass_z(DN1, 3)
    pass_core(DN1)
    complete(DN1)
    fall(1)
    share(1, 1)
    share(1, 0)
    head_core()
    head_complete()
    unpack_head()
    turn_normed()
    block_gain, q_gain, k_gain = gain_row(0), head_gain(2), head_gain(3)

    out_n, out_scale = stream_out(0)
    is_patch = iota((ROWS, 1), 0) < npatch
    final_gain = gain_row(1)
    n_sum = jnp.sum(jnp.where(is_patch, out_n, 0.0), axis=0, keepdims=True)
    pooled = n_sum * final_gain / npatch
    pooled_b = pooled.astype(bfloat)
    heads_b = [hw[0], hw[1]]
    pooled_8 = jnp.broadcast_to(pooled_b, (16, 768))
    logits = jnp.concatenate([dot(pooled_8, m)[0:1] for m in heads_b], axis=1)
    lane = iota((1, 1024), 1)
    logits = jnp.where(lane < classes, logits, -1e30)
    top = jnp.max(logits, axis=-1, keepdims=True)
    log_total = top + jnp.log(jnp.sum(jnp.exp(logits - top), axis=-1, keepdims=True))
    onehot = jnp.where(lane == r.labels[h * N_HID + z], 1.0, 0.0)
    term = log_total - jnp.sum(jnp.where(lane < classes, logits, 0.0) * onehot, axis=-1, keepdims=True)
    d_logits = (jnp.exp(logits - log_total) - onehot) / total_images
    hi = d_logits.astype(bfloat).astype(single)
    both = jnp.concatenate([hi, d_logits - hi, jnp.zeros((14, 1024), single)], axis=0).astype(bfloat)
    back = dot_nt(both[:, 0:512], heads_b[0]) + dot_nt(both[:, 512:1024], heads_b[1])
    d_pooled = (back[0:1] + back[1:2]) / npatch
    d_row = d_pooled * final_gain
    rw = r.rw
    rw[0] = jnp.broadcast_to(d_row, (8, 768))
    tag_rw = send(rw.at[0], rw.at[1], x_dev)
    ds, db, dbt = r.ds, r.db, r.dbt
    d_stream = jnp.where(is_patch, norm_back(out_n, out_scale, d_row), 0.0)
    ds[...] = d_stream
    db[0] = d_stream.astype(bfloat)
    dbt[:, 0:ROWS] = d_stream.T.astype(bfloat)
    d_final_gain = d_pooled * n_sum
    al = r.al
    pooled_f = pooled_b.astype(single)
    al[core, h, y, z] = jnp.concatenate(
        [d_logits[:, q * 256 : q * 256 + 256] for q in range(4)]
        + [pooled_f[:, q * 256 : q * 256 + 256] for q in range(3)]
        + [jnp.zeros((1, 256), single)],
        axis=0,
    )
    own = al.at[core, h, y, z]
    tag_al = [send(own, own, device) for device in group_dev]
    out_n, out_scale = stream_out(1)
    arrive(rw.at[1], tag_rw, x_dev)
    d_stream = jnp.where(is_patch, norm_back(out_n, out_scale, rw[1, 0:1, :]), 0.0)
    db[1] = d_stream.astype(bfloat)
    dbt[:, ROWS : 2 * ROWS] = d_stream.T.astype(bfloat)
    db2 = db[...].reshape(2 * ROWS, 768)

    rff, f1, f2, ft, f3 = r.rff, r.f1, r.f2, r.ft, r.f3
    dn, dm = br, r.dm
    kept = types.SimpleNamespace(fresh=True, gains=[])

    def add_in(part):
        if kept.fresh:
            dn[...] = part
        else:
            dn[...] += part
        kept.fresh = False

    def ff_send(m, k):
        tags["ff", m, k] = send(rff.at[k, m, :, :, 1 - core], f1.at[k, m], core_dev)

    def ff_down(k):
        rff[k, 0] = dot(dbt[...], hb[z_up[k]]).astype(bfloat).reshape(2, 2, 2, 96, 384)
        ff_send(0, k)

    def ff_up(k):
        w = z_up[k]
        upper = us[w]
        t = gelu_tanh(upper)
        slope = 0.5 * (1.0 + t) + 0.5 * upper * (1.0 - t * t) * gelu_c * (
            1.0 + 3 * 0.044715 * (upper * upper)
        )
        d_upper = (dot(db2, gdn[w].reshape(768, 384)) * slope).astype(bfloat)
        us[w] = d_upper.astype(single)
        rff[k, 1] = dot(nbt[...], d_upper).astype(bfloat).reshape(2, 2, 2, 96, 384)
        ff_send(1, k)

    def ff_in(k):
        w = z_up[k]
        add_in(dot_nt(us[w].astype(bfloat), gup[w].reshape(768, 384)))

    def ff_y(m, k):
        arrive(f1.at[k, m], tags["ff", m, k], core_dev)
        f1[k, m] = f1[k, m] + rff[k, m, :, :, core]
        tags["fy", m, k] = send(f1.at[k, m, :, 1 - y], f2.at[k, m], y_dev)

    def ff_z(m, k):
        arrive(f2.at[k, m], tags["fy", m, k], y_dev)
        if k:
            ft[k - 1, m] = f1[k, m, :, y] + f2[k, m]
            tags["fz", m, k] = send(ft.at[k - 1, m], f3.at[k - 1, m], z_dev[k])

    def ff_end():
        for m, name in enumerate(("g_down", "g_up")):
            total = f1[0, m, :, y].astype(single) + f2[0, m].astype(single)
            for k in range(1, N_HID):
                arrive(f3.at[k - 1, m], tags["fz", m, k], z_dev[k])
                total = total + f3[k - 1, m].astype(single)
            getattr(r, name)[...] = total.reshape(192, 384)
            store(name)

    def pass_rows():
        for i, place in enumerate(source):
            arrive(al.at[(core, *place)], tag_al[i], core_dev)
        tags["al"] = send(al.at[core], al.at[core], core_dev)

    rout, o1, o2, ot, o3, pc = r.rout, r.o1, r.o2, r.ot, r.o3, r.pc

    def cut_branch():
        for d in range(4):
            low = db2[:, d * 96 : d * 96 + 96]
            high = db2[:, 384 + d * 96 : 384 + d * 96 + 96]
            pc[d] = jnp.concatenate([low, high], axis=1)

    def out_grad():
        hot = hof[...].T
        for d in range(4):
            rout[:, d // 2, d % 2] = jnp.zeros((N_HID, 96, 256), bfloat)
            grad = dot(hot, pc[d]).astype(bfloat).reshape(N_HID, 96, 192)
            rout[:, d // 2, d % 2, :, 0:192] = grad
        tags["o1"] = send(rout.at[:, :, 1 - core], o1, core_dev)

    dh = r.dh

    def out_back():
        d_heads = None
        for d in range(4):
            part = dot_nt(pc[d], gout[d].reshape(384, 256)[:, 0:192])
            d_heads = part if d_heads is None else d_heads + part
        d_heads = d_heads.astype(bfloat)
        for n in range(6):
            part = d_heads[:, n * HD : (n + 1) * HD]
            dh[2 * n] = part[0:ROWS]
            dh[2 * n + 1] = part[ROWS : 2 * ROWS]

    def out_y():
        arrive(o1, tags["o1"], core_dev)
        o1[...] = o1[...] + rout[:, :, core]
        tags["o2"] = send(o1.at[:, 1 - y], o2, y_dev)

    def out_z():
        arrive(o2, tags["o2"], y_dev)
        ot[...] = o1[:, y] + o2[...]
        tags["o3"] = [send(ot.at[z_up[k]], o3.at[k - 1], z_dev[k]) for k in range(1, N_HID)]

    def out_end():
        total = ot[z].astype(single)
        for k in range(1, N_HID):
            arrive(o3.at[k - 1], tags["o3"][k - 1], z_dev[k])
            total = total + o3[k - 1].astype(single)
        r.g_out[...] = total[:, 0:192]
        store("g_out")

    dqkv = r.dqkv

    def attend_back(pair, carry):
        for i in range(2):
            made = ([], [], [])
            for side in range(2):
                n = 4 * pair + 2 * side + i
                probs = pr[n]
                d_out = dh[n]
                d_probs = dot_nt(d_out, v_ref[n])
                inner = jnp.sum(probs * d_probs, axis=-1, keepdims=True)
                d_scores = (probs * (d_probs - inner)).astype(bfloat)
                made[0].append(dot(d_scores, k_ref[n]) * HD ** (-0.5))
                made[1].append(dot_tn(d_scores, q_ref[n]) * HD ** (-0.5))
                made[2].append(dot_tn(probs.astype(bfloat), d_out))
            for c in range(3):
                both = jnp.concatenate(made[c], axis=1)
                lanes = pl.ds(pl.multiple_of(pair * 128, 128), 128)
                dqkv[c, i * ROWS : (i + 1) * ROWS, lanes] = both
        return carry

    rqkv, q1, q2, qt, q3 = r.rqkv, r.q1, r.q2, r.qt, r.q3

    def mix_back():
        for c, gain in enumerate((q_gain, k_gain, None)):
            grad = dqkv[c]
            if gain is not None:
                normed = nq[c]
                kept.gains.append(jnp.sum(grad * normed, axis=0, keepdims=True))
                grad = grad * gain
                grad = sq[c] * (grad - head_mean(grad) - normed * head_mean(grad * normed))
            dm[c] = grad.astype(bfloat)
            add_in(dot_nt(dm[c], gqkv[c].reshape(768, 384)))

    dns, dnr = r.dns, r.dnr

    def send_in():
        dns[...] = dn[ROWS : 2 * ROWS, :].astype(bfloat)
        tags["dn"] = send(dns, dnr, x_dev)

    def qkv_grad(c):
        rqkv[c] = dot(nbt[...], dm[c]).astype(bfloat).reshape(2, 2, 2, 2, 48, 384)
        tags["q1", c] = send(rqkv.at[c, :, :, 1 - core], q1.at[c], core_dev)

    def qkv_y(c):
        arrive(q1.at[c], tags["q1", c], core_dev)
        q1[c] = q1[c] + rqkv[c, :, :, core]
        tags["q2", c] = send(q1.at[c, :, 1 - y], q2.at[c], y_dev)

    def qkv_z(c):
        arrive(q2.at[c], tags["q2", c], y_dev)
        qt[c] = q1[c, :, y] + q2[c]
        for k in range(1, N_HID):
            block = qt.at[c, z_up[k] // 2, lax.rem(z_up[k], 2)]
            tags["q3", c, k] = send(block, q3.at[k - 1, c], z_dev[k])

    def qkv_end():
        for c in range(3):
            total = qt[c, z // 2, lax.rem(z, 2)].astype(single)
            for k in range(1, N_HID):
                arrive(q3.at[k - 1, c], tags["q3", c, k], z_dev[k])
                total = total + q3[k - 1, c].astype(single)
            r.g_qkv[c] = total
        store("g_qkv")

    def head_grad():
        arrive(al.at[1 - core], tags["al"], core_dev)
        rows_all = al[...].reshape(32, 8, 256)
        d_logits_all = jnp.concatenate([rows_all[:, q, :] for q in range(4)], axis=1)
        pooled_all = jnp.concatenate([rows_all[:, 4 + q, :] for q in range(3)], axis=1)
        start = ((h * 4 + dp) * N_HID + z) * 24
        chosen = (iota((24, 768), 1) == iota((24, 768), 0) + start).astype(bfloat)
        mine = dot_nt(chosen, pooled_all.astype(bfloat))
        g_head = jnp.dot(mine, d_logits_all, precision=highest, preferred_element_type=single)
        r.g_head[...] = g_head[:, 0:classes]
        store("g_head")

    dx, gg = r.dx, r.gg

    def spread(row):
        blank = jnp.zeros((1, 192), single)
        halves = []
        for a in range(2):
            part = jnp.concatenate([row[:, a * 96 : a * 96 + 96], row[:, 192 + a * 96 : 288 + a * 96]], axis=1)
            halves.append(
                jnp.where(
                    h == 0,
                    jnp.concatenate([part, blank], axis=1),
                    jnp.concatenate([blank, part], axis=1),
                )
            )
        return jnp.concatenate(halves, axis=1)

    def norm_in():
        arrive(dnr, tags["dn"], x_dev)
        d_normed = dn[0:ROWS, :] + dnr[...].astype(single)
        block_n, block_scale = norm_parts(jnp.concatenate([st[0, 0], st[1, 0]], axis=1).astype(single))
        d_block_gain = jnp.sum(d_normed * block_n, axis=0, keepdims=True)
        d_in = ds[...] + norm_back(block_n, block_scale, d_normed * block_gain)
        low, high = d_in[:, 0:384], d_in[:, 384:768]
        dx[2] = jnp.where(h == 0, high, low).astype(bfloat)
        tags["dx"] = send(dx.at[2], dx.at[1], x_dev)
        dx[0] = jnp.where(h == 0, low, high).astype(bfloat)
        d_gains = jnp.concatenate(
            [d_block_gain, d_final_gain, spread(kept.gains[0]), spread(kept.gains[1])]
            + [jnp.zeros((4, 768), single)],
            axis=0,
        )
        low, high = d_gains[:, 0:384], d_gains[:, 384:768]
        gg[0] = jnp.where(h == 0, low, high)
        gg[2] = jnp.where(h == 0, high, low)
        tags["gg"] = send(gg.at[2], gg.at[1], x_dev)

    rext, e1, e2, et, e3 = r.rext, r.e1, r.e2, r.et, r.e3

    def ext_grad():
        arrive(dx.at[1], tags["dx"], x_dev)
        arrive(gg.at[1], tags["gg"], x_dev)
        dxt = jnp.concatenate([dx[0].astype(single), dx[1].astype(single)], axis=0).T.astype(bfloat)
        px2 = px[...].reshape(2 * ROWS, 1024)
        d_gains = (gg[0] + gg[1]).astype(bfloat)
        x0[...] = dot(dxt, px2[:, 0:512])
        x1[...] = dot(dxt, px2[:, 512:1024]) + dot_tn(d_gains, rows_of.astype(bfloat))
        for d in range(4):
            for w in range(N_HID):
                s = (d * N_HID + w) * 24
                rext[d // 2, d % 2, w] = jnp.concatenate(
                    [x0[s : s + 24, :], x1[s : s + 24, :]], axis=0
                ).astype(bfloat)
        tags["e1"] = send(rext.at[:, 1 - core], e1, core_dev)

    def ext_y():
        arrive(e1, tags["e1"], core_dev)
        e1[...] = e1[...] + rext[:, core]
        tags["e2"] = send(e1.at[1 - y], e2, y_dev)

    def ext_z():
        arrive(e2, tags["e2"], y_dev)
        et[...] = e1[y] + e2[...]
        tags["e3"] = [send(et.at[z_up[k]], e3.at[k - 1], z_dev[k]) for k in range(1, N_HID)]

    def ext_end():
        total = et[z].astype(single)
        for k in range(1, N_HID):
            arrive(e3.at[k - 1], tags["e3"][k - 1], z_dev[k])
            total = total + e3[k - 1].astype(single)
        r.g_patch[:, 0:512] = total[0:24]
        r.g_patch[:, 512:768] = total[24:48, 0:256]
        r.g_table[...] = total[24:48, 256 : 256 + seq_len]
        columns = total[24:48, 256:512]
        pick_f = (iota((8, 256), 1) == iota((8, 256), 0) + seq_len).astype(single)
        r.g_gains[...] = dot_nt(pick_f, columns, precision=highest)[0:4]
        for name in ("g_patch", "g_table", "g_gains"):
            store(name)

    ff_down(2)
    ff_up(3)
    ff_y(0, 2)
    cut_branch()
    out_back()
    ff_down(1)
    ff_up(1)
    ff_y(0, 1)
    pass_rows()
    ff_y(1, 3)
    ff_up(2)
    ff_z(0, 2)
    ff_in(2)
    out_grad()
    ff_up(0)
    ff_in(0)
    ff_z(0, 1)
    ff_y(1, 2)
    lax.fori_loop(0, 1, attend_back, 0)
    lax.fori_loop(1, 2, attend_back, 0)
    ff_y(1, 1)
    ff_z(1, 3)
    ff_down(0)
    ff_in(3)
    ff_in(1)
    ff_down(3)
    out_y()
    lax.fori_loop(2, 3, attend_back, 0)
    ff_y(0, 3)
    ff_z(1, 1)
    ff_z(1, 2)
    mix_back()
    send_in()
    qkv_grad(0)
    qkv_y(0)
    qkv_grad(2)
    qkv_grad(1)
    qkv_y(2)
    out_z()
    qkv_y(1)
    ff_y(1, 0)
    norm_in()
    ff_z(0, 3)
    qkv_z(2)
    ext_grad()
    qkv_z(1)
    qkv_z(0)
    ext_y()
    head_grad()
    ext_z()
    ff_y(0, 0)
    ff_z(0, 0)
    qkv_end()
    ff_z(1, 0)
    out_end()
    ff_end()

    def read(prefix, kind):
        values = getattr(r, prefix + kind)[...]
        return values.reshape(-1, values.shape[-1])
    lane = iota((8, 128), 1)
    own = jnp.zeros((8, 128), single)
    grad_square = jnp.zeros((1, 1), single)
    for n, kind in enumerate(KINDS):
        own = jnp.where(lane == 8 + n, square_sum(read("w_", kind)), own)
        if n > 2:
            grad_square = grad_square + square_sum(read("g_", kind))
    ext_end()

    own = jnp.where(lane == 0, term, own)
    for kind in KINDS[0:3]:
        grad_square = grad_square + square_sum(read("g_", kind))
    own = jnp.where(lane == 1, grad_square, own)

    def all_sum(vector, pair, every):
        pair[0] = vector
        tag = send(pair.at[0], pair.at[1], core_dev)
        arrive(pair.at[1], tag, core_dev)
        every[h, y, z] = pair[0] + pair[1]
        mine = every.at[h, y, z]
        numbers = [send(mine, mine, device) for device in group_dev]
        for i, place in enumerate(source):
            arrive(every.at[place], numbers[i], core_dev)
        return jnp.sum(every[...].reshape(16, 8, 128), axis=0)

    sums = all_sum(own, r.l1, r.v1)
    grad_norm = jnp.sqrt(jnp.sum(jnp.where(lane == 1, sums, 0.0), axis=1, keepdims=True))[0:1]
    clip = jnp.minimum(1.0, clip_at / grad_norm)
    own = jnp.zeros((8, 128), single)
    for name in order[9:]:
        loads[name].wait()
    for n, kind in enumerate(KINDS):
        update = one_update(read("w_", kind), read("m_", kind), read("v_", kind), read("g_", kind), clip)[2]
        own = jnp.where(lane == 8 + n, square_sum(update), own)
    updates = all_sum(own, r.l2, r.v2)
    result = jnp.sqrt(sums) / jnp.sqrt(updates)
    result = jnp.where(lane == 0, sums, result)
    result = jnp.where(lane == 1, grad_norm, result)
    result = jnp.where(lane == 2, clip, result)
    r.scalars[...] = result
    store("scalars")
    for copy in stores:
        copy.wait()
    for key, copies in sends.items():

        def settle(copies=copies):
            for copy in copies:
                copy.wait_send()

        if key is None:
            settle()
        else:
            pl.when(holds[key])(settle)


def write_kernel(names, *refs):
    r = types.SimpleNamespace(**dict(zip(names, refs)))
    lane = iota((8, 128), 1)
    inputs = ["scalars"] + [p + k for k in KINDS for p in ("w_", "m_", "v_", "g_")]
    loads = {}
    for number, name in enumerate(inputs):
        loads[name] = pltpu.make_async_copy(
            getattr(r, "h_" + name), getattr(r, name), r.lsem.at[number]
        )
        loads[name].start()
    loads["scalars"].wait()

    def pick(n):
        return jnp.sum(jnp.where(lane == n, r.scalars[...], 0.0), axis=1, keepdims=True)[0:1]

    clip = pick(2)
    r.o_loss[...] = pick(0)
    r.o_norm[...] = pick(1)
    stores = []
    for n, kind in enumerate(KINDS):
        for p in ("w_", "m_", "v_", "g_"):
            loads[p + kind].wait()
        master = getattr(r, "w_" + kind)[...]
        grad = getattr(r, "g_" + kind)[...]
        ratio, c = pick(8 + n), clip
        if len(master.shape) == 3:
            c, ratio = clip[None], ratio[None]
        first, second, update = one_update(
            master, getattr(r, "m_" + kind)[...], getattr(r, "v_" + kind)[...], grad, c
        )
        results = (first, second, master - learn_rate * ratio * update)
        for p, value in zip(("nm_", "nv_", "nw_"), results):
            getattr(r, p + kind)[...] = value
            copy = pltpu.make_async_copy(
                getattr(r, p + kind),
                getattr(r, "h_" + p + kind),
                r.lsem.at[len(inputs) + len(stores)],
            )
            copy.start()
            stores.append(copy)
    for copy in stores:
        copy.wait()


def fast_device(patches, labels, *state):
    bfloat, single = jnp.bfloat16, jnp.float32

    def turn(kind, value):
        if kind in ("patch", "table", "down"):
            return value.T
        if kind == "qkv":
            return value.transpose(1, 0, 2)
        return value

    flat = [turn(KINDS[i % 8], value) for i, value in enumerate(state)]
    hbm = pl.BlockSpec(memory_space=pl.ANY)
    smem = pl.BlockSpec(memory_space=pltpu.SMEM)
    in_names = ["patches"] + [p + k for p in ("w_", "m_", "v_") for k in KINDS]
    out_names = ["g_" + k for k in KINDS] + ["scalars"]
    scratch = dict(
        px=((2, ROWS, 1024), bfloat),
        gext=((4, 4, 48, 512), bfloat),
        gqkv=((3, 2, 4, 2, 48, 384), bfloat),
        gout=((4, 4, 96, 256), bfloat),
        gup=((4, 2, 4, 96, 384), bfloat),
        gdn=((4, 2, 2, 2, 96, 384), bfloat),
        ghd=((2, 4, 4, 48, 512), bfloat),
        x0=((384, 512), single),
        x1=((384, 512), single),
        hw=((2, 768, 512), bfloat),
        ga=((2, 8, 384), single),
        st=((2, 2, ROWS, 384), bfloat),
        nb=((2 * ROWS, 768), bfloat),
        nbt=((768, 2 * ROWS), bfloat),
        nq=((2, 2 * ROWS, 384), single),
        sq=((2, 2 * ROWS, 384), single),
        bd=((384, 384), bfloat),
        q=((12, ROWS, HD), bfloat),
        k=((12, ROWS, HD), bfloat),
        v=((12, ROWS, HD), bfloat),
        pr=((12, ROWS, ROWS), single),
        hof=((2 * ROWS, 384), bfloat),
        us=((4, 2 * ROWS, 384), single),
        hb=((4, 2 * ROWS, 384), bfloat),
        br=((2 * ROWS, 768), single),
        brs=((2, 2, ROWS, 384), bfloat),
        brr=((2, 2, ROWS, 384), bfloat),
        rw=((2, 8, 768), single),
        ds=((ROWS, 768), single),
        db=((2, ROWS, 768), bfloat),
        dbt=((768, 2 * ROWS), bfloat),
        al=((2, 2, 2, 4, 8, 256), single),
        rff=((4, 2, 2, 2, 2, 96, 384), bfloat),
        f1=((4, 2, 2, 2, 96, 384), bfloat),
        f2=((4, 2, 2, 96, 384), bfloat),
        ft=((3, 2, 2, 96, 384), bfloat),
        f3=((3, 2, 2, 96, 384), bfloat),
        rout=((4, 2, 2, 96, 256), bfloat),
        o1=((4, 2, 96, 256), bfloat),
        o2=((4, 96, 256), bfloat),
        ot=((4, 96, 256), bfloat),
        o3=((3, 96, 256), bfloat),
        dh=((12, ROWS, HD), bfloat),
        dm=((3, 2 * ROWS, 384), bfloat),
        pc=((4, 2 * ROWS, 192), bfloat),
        dqkv=((3, 2 * ROWS, 384), single),
        rqkv=((3, 2, 2, 2, 2, 48, 384), bfloat),
        q1=((3, 2, 2, 2, 48, 384), bfloat),
        q2=((3, 2, 2, 48, 384), bfloat),
        qt=((3, 2, 2, 48, 384), bfloat),
        q3=((3, 3, 48, 384), bfloat),
        dns=((ROWS, 768), bfloat),
        dnr=((ROWS, 768), bfloat),
        dx=((3, ROWS, 384), bfloat),
        gg=((3, 8, 384), single),
        rext=((2, 2, 4, 48, 512), bfloat),
        e1=((2, 4, 48, 512), bfloat),
        e2=((4, 48, 512), bfloat),
        et=((4, 48, 512), bfloat),
        e3=((3, 48, 512), bfloat),
        l1=((2, 8, 128), single),
        l2=((2, 8, 128), single),
        v1=((2, 2, 4, 8, 128), single),
        v2=((2, 2, 4, 8, 128), single),
    )
    semaphores = 320
    shapes = [flat[i].shape for i in range(8)]
    npatch, seq_len, classes = patches.shape[1], flat[1].shape[1], flat[3].shape[1]
    total_images = labels.shape[0] * lax.axis_size("dp")
    sizes = (npatch, seq_len, classes, total_images)
    held = [(patches.shape, bfloat)] + [(s, single) for s in shapes * 4] + [((8, 128), single)]
    names = ["labels"] + ["h_" + n for n in in_names + out_names] + in_names + out_names
    names += list(scratch) + ["ssem", "rsem", "lsem"]
    found = pl.pallas_call(
        functools.partial(step_kernel, sizes, names),
        out_shape=[jax.ShapeDtypeStruct(s, single) for s in shapes]
        + [jax.ShapeDtypeStruct((8, 128), single)],
        in_specs=[smem] + [hbm] * 25,
        out_specs=[hbm] * 9,
        scratch_shapes=[pltpu.VMEM(s, t) for s, t in held + list(scratch.values())]
        + [pltpu.SemaphoreType.DMA((semaphores,))] * 2
        + [pltpu.SemaphoreType.DMA((len(held),))],
        compiler_params=pltpu.CompilerParams(
            collective_id=0, has_side_effects=True, vmem_limit_bytes=62 * 2**20
        ),
        name="train_step",
    )(labels, patches, *flat)
    grads, scalars = found[:8], found[8]
    in_names = ["scalars"] + [p + k for p in ("w_", "m_", "v_", "g_") for k in KINDS]
    out_names = [p + k for p in ("nm_", "nv_", "nw_") for k in KINDS]
    held = [((8, 128), single)] + [(s, single) for s in shapes * 7]
    names = ["h_" + n for n in in_names + out_names] + ["o_loss", "o_norm"]
    names += in_names + out_names + ["lsem"]
    written = pl.pallas_call(
        functools.partial(write_kernel, names),
        out_shape=[jax.ShapeDtypeStruct(s, single) for s in shapes * 3 + [(1, 1), (1, 1)]],
        in_specs=[hbm] * 33,
        out_specs=[hbm] * 24 + [pl.BlockSpec(memory_space=pltpu.VMEM)] * 2,
        scratch_shapes=[pltpu.VMEM(s, t) for s, t in held]
        + [pltpu.SemaphoreType.DMA((len(held),))],
        compiler_params=pltpu.CompilerParams(vmem_limit_bytes=62 * 2**20),
        name="write_step",
    )(scalars, *flat, *grads)
    back = [turn(KINDS[i % 8], value) for i, value in enumerate(written[:24])]
    return (written[24].reshape(()), written[25].reshape(()), *back)


def fits(mesh):
    return tuple(mesh.shape[a] for a in ALL) == (4, 2, N_HID)


def solution(mesh):
    placed = (
        P(ALL, None, None),
        P("dp"),
        P(None, ALL),
        P(None, ALL),
        P(None, ALL),
        P(ALL, None),
        P(DATA, None, "heads"),
        P(MODEL, "dp"),
        P("dp", MODEL),
        P(MODEL, "dp"),
        P(None, ALL),
        P(None, ALL),
        P(None, ALL),
        P(ALL, None),
        P(DATA, None, "heads"),
        P(MODEL, "dp"),
        P("dp", MODEL),
        P(MODEL, "dp"),
        P(None, ALL),
        P(None, ALL),
        P(None, ALL),
        P(ALL, None),
        P(DATA, None, "heads"),
        P(MODEL, "dp"),
        P("dp", MODEL),
        P(MODEL, "dp"),
    )
    return jax.shard_map(
        fast_device if fits(mesh) else per_device,
        mesh=mesh,
        in_specs=placed,
        out_specs=(
            P(),
            P(),
            P(None, ALL),
            P(None, ALL),
            P(None, ALL),
            P(ALL, None),
            P(DATA, None, "heads"),
            P(MODEL, "dp"),
            P("dp", MODEL),
            P(MODEL, "dp"),
            P(None, ALL),
            P(None, ALL),
            P(None, ALL),
            P(ALL, None),
            P(DATA, None, "heads"),
            P(MODEL, "dp"),
            P("dp", MODEL),
            P(MODEL, "dp"),
            P(None, ALL),
            P(None, ALL),
            P(None, ALL),
            P(ALL, None),
            P(DATA, None, "heads"),
            P(MODEL, "dp"),
            P("dp", MODEL),
            P(MODEL, "dp"),
        ),
        check_vma=False,
    )
```

```python
import functools
import types

import jax
import jax.numpy as jnp
from jax import lax
from jax.experimental import pallas as pl
from jax.experimental.pallas import tpu as pltpu
from jax.sharding import PartitionSpec as P

HD = 64
PD = 768
STEP = 10
MESH = pl.DeviceIdType.MESH
ALL = ("dp", "heads", "hidden")
DATA = ("dp", "hidden")
MODEL = ("heads", "hidden")


beta_one = 0.9
beta_two = 0.999
adam_eps = 1e-08
decay_rate = 0.01
learn_rate = 0.5
clip_at = 0.001
norm_eps = 1e-06
highest = lax.Precision.HIGHEST


def layer_norm(values):
    center = values - jnp.mean(values, axis=-1, keepdims=True)
    return center * lax.rsqrt(jnp.mean(center * center, axis=-1, keepdims=True) + norm_eps)


def head_loss(stream_out, targets, final_gain, head_weight, npatch, total_images):
    normed_out, norm_back = jax.vjp(layer_norm, stream_out)
    final = normed_out * final_gain
    pooled_b = jnp.mean(final[:, :npatch], axis=1).astype(jnp.bfloat16)
    logits = jnp.dot(pooled_b, head_weight, preferred_element_type=jnp.float32)
    log_total = jax.nn.logsumexp(logits, axis=-1)
    onehot = (targets[:, None] == lax.broadcasted_iota(jnp.int32, logits.shape, 1)).astype(
        jnp.float32
    )
    terms = log_total - jnp.sum(logits * onehot, axis=-1)
    d_logits = (jnp.exp(logits - log_total[:, None]) - onehot) / total_images
    d_pooled = jnp.dot(d_logits, head_weight.astype(jnp.float32).T, precision=highest)
    count, seq_len, width = stream_out.shape
    spread = jnp.broadcast_to(d_pooled[:, None, :] / npatch, (count, npatch, width))
    d_final = jnp.concatenate(
        [spread, jnp.zeros((count, seq_len - npatch, width), jnp.float32)], axis=1
    )
    d_stream = norm_back(d_final * final_gain)[0]
    d_gain_rows = jnp.sum(d_final * normed_out, axis=1)
    return (terms, pooled_b, d_logits, d_stream, d_gain_rows)


def per_device(
    patches,
    labels,
    w_patch,
    table,
    gains,
    w_head,
    w_qkv,
    w_out,
    w_up,
    w_down,
    first_patch,
    first_table,
    first_gains,
    first_head,
    first_qkv,
    first_out,
    first_up,
    first_down,
    second_patch,
    second_table,
    second_gains,
    second_head,
    second_qkv,
    second_out,
    second_up,
    second_down,
):
    masters = [w_patch, table, gains, w_head, w_qkv, w_out, w_up, w_down]
    firsts = [
        first_patch,
        first_table,
        first_gains,
        first_head,
        first_qkv,
        first_out,
        first_up,
        first_down,
    ]
    seconds = [
        second_patch,
        second_table,
        second_gains,
        second_head,
        second_qkv,
        second_out,
        second_up,
        second_down,
    ]
    bfloat = jnp.bfloat16
    single = jnp.float32
    patch_b, table_b, gains_b, head_b = (
        lax.all_gather(w_patch.astype(bfloat), ALL, axis=1, tiled=True),
        lax.all_gather(table.astype(bfloat), ALL, axis=1, tiled=True),
        lax.all_gather(gains.astype(bfloat), ALL, axis=1, tiled=True),
        lax.all_gather(w_head.astype(bfloat), ALL, axis=0, tiled=True),
    )
    qkv_b = lax.all_gather(w_qkv.astype(bfloat), DATA, axis=0, tiled=True)
    out_b, up_b, down_b = (
        lax.all_gather(w_out.astype(bfloat), "dp", axis=1, tiled=True),
        lax.all_gather(w_up.astype(bfloat), "dp", axis=0, tiled=True),
        lax.all_gather(w_down.astype(bfloat), "dp", axis=1, tiled=True),
    )
    gain_vals = gains_b.astype(single)
    table_vals = table_b.astype(single)
    n_hidden = lax.axis_size("hidden")
    n_own = patches.shape[0]
    npatch = patches.shape[1]
    seq_len = table_b.shape[0]
    width = patch_b.shape[1]
    group_width = qkv_b.shape[2]
    group_heads = group_width // HD
    own_index = lax.axis_index("heads") * n_hidden + lax.axis_index("hidden")
    total_images = labels.shape[0] * lax.axis_size("dp")
    embedded = jnp.dot(patches.reshape(n_own * npatch, PD), patch_b, preferred_element_type=single)
    embedded = embedded.reshape(n_own, npatch, width) + table_vals[:npatch]
    registers = jnp.broadcast_to(table_vals[npatch:], (n_own, seq_len - npatch, width))
    stream_own = jnp.concatenate([embedded, registers], axis=1).astype(bfloat)
    stream_in = lax.all_gather(stream_own, MODEL, axis=0, tiled=True)
    n_img = stream_in.shape[0]
    row_count = n_img * seq_len
    stream_flat = stream_in.astype(single).reshape(row_count, width)
    normed_b = (layer_norm(stream_flat) * gain_vals[0]).astype(bfloat)
    n_att = n_img // n_hidden
    att_start = lax.axis_index("hidden") * n_att
    normed_att = lax.dynamic_slice_in_dim(
        normed_b.reshape(n_img, seq_len, width), att_start, n_att, 0
    )
    query_gain = lax.dynamic_slice_in_dim(
        gain_vals[2], lax.axis_index("heads") * group_width, group_width, 0
    ).reshape(group_heads, HD)
    key_gain = lax.dynamic_slice_in_dim(
        gain_vals[3], lax.axis_index("heads") * group_width, group_width, 0
    ).reshape(group_heads, HD)
    mixed = jnp.einsum("bsd,dcf->bscf", normed_att, qkv_b, preferred_element_type=single)
    mixed = mixed.reshape(n_att, seq_len, 3, group_heads, HD)
    query_norm, query_back = jax.vjp(layer_norm, mixed[:, :, 0])
    key_norm, key_back = jax.vjp(layer_norm, mixed[:, :, 1])
    queries = (query_norm * query_gain).astype(bfloat)
    keys = (key_norm * key_gain).astype(bfloat)
    values = mixed[:, :, 2].astype(bfloat)
    scale = HD ** (-0.5)
    scores = jnp.einsum("bqhd,bkhd->bhqk", queries, keys, preferred_element_type=single) * scale
    probs = jax.nn.softmax(scores, axis=-1)
    probs_b = probs.astype(bfloat)
    heads_out = jnp.einsum("bhqk,bkhd->bqhd", probs_b, values, preferred_element_type=single)
    heads_out = heads_out.astype(bfloat).reshape(n_att * seq_len, group_width)
    columns = lax.all_to_all(heads_out, "hidden", split_axis=1, concat_axis=0, tiled=True)
    attn_part = jnp.dot(columns, out_b, preferred_element_type=single)
    upper = jnp.dot(normed_b, up_b, preferred_element_type=single)
    activated, gelu_back = jax.vjp(jax.nn.gelu, upper)
    activated_b = activated.astype(bfloat)
    partial_sum = attn_part + jnp.dot(activated_b, down_b, preferred_element_type=single)
    total = lax.psum(partial_sum, MODEL)
    stream_out = (stream_flat + total).reshape(n_img, seq_len, width)
    terms, pooled_b, d_logits, d_stream, d_gain_rows = head_loss(
        stream_out, labels, gain_vals[1], head_b, npatch, total_images
    )
    loss_terms = lax.dynamic_slice_in_dim(terms, own_index * n_own, n_own, 0)
    pooled_own = lax.dynamic_slice_in_dim(pooled_b, own_index * n_own, n_own, 0)
    logits_own = lax.dynamic_slice_in_dim(d_logits, own_index * n_own, n_own, 0)
    d_head = jnp.dot(pooled_own.astype(single).T, logits_own, precision=highest)
    d_final_gain = jnp.sum(
        lax.dynamic_slice_in_dim(d_gain_rows, own_index * n_own, n_own, 0), axis=0
    )
    d_stream_own = lax.dynamic_slice_in_dim(d_stream, own_index * n_own, n_own, 0)
    d_branch = d_stream.reshape(row_count, width).astype(bfloat)
    d_activated = jnp.dot(d_branch, down_b.T, preferred_element_type=single)
    d_upper = gelu_back(d_activated)[0].astype(bfloat)
    d_down = jnp.dot(activated_b.T, d_branch, preferred_element_type=single)
    d_up = jnp.dot(normed_b.T, d_upper, preferred_element_type=single)
    d_normed = jnp.dot(d_upper, up_b.T, preferred_element_type=single)
    d_out = jnp.dot(columns.T, d_branch, preferred_element_type=single)
    d_columns = jnp.dot(d_branch, out_b.T, preferred_element_type=single).astype(bfloat)
    d_heads = lax.all_to_all(d_columns, "hidden", split_axis=0, concat_axis=1, tiled=True).reshape(
        n_att, seq_len, group_heads, HD
    )
    d_probs = jnp.einsum("bqhd,bkhd->bhqk", d_heads, values, preferred_element_type=single)
    d_values = jnp.einsum("bhqk,bqhd->bkhd", probs_b, d_heads, preferred_element_type=single)
    d_scores = (probs * (d_probs - jnp.sum(probs * d_probs, axis=-1, keepdims=True))).astype(bfloat)
    d_query_norm = (
        jnp.einsum("bhqk,bkhd->bqhd", d_scores, keys, preferred_element_type=single) * scale
    )
    d_key_norm = (
        jnp.einsum("bhqk,bqhd->bkhd", d_scores, queries, preferred_element_type=single) * scale
    )
    d_queries = query_back(d_query_norm * query_gain)[0]
    d_keys = key_back(d_key_norm * key_gain)[0]
    d_query_gain = jnp.sum(d_query_norm * query_norm, axis=(0, 1)).reshape(group_width)
    d_key_gain = jnp.sum(d_key_norm * key_norm, axis=(0, 1)).reshape(group_width)
    d_mixed = (
        jnp.stack([d_queries, d_keys, d_values], axis=2)
        .astype(bfloat)
        .reshape(n_att, seq_len, 3, group_width)
    )
    d_qkv = jnp.einsum("bsd,bscf->dcf", normed_att, d_mixed, preferred_element_type=single)
    d_att_in = jnp.einsum("bscf,dcf->bsd", d_mixed, qkv_b, preferred_element_type=single)
    d_normed = d_normed.reshape(n_img, seq_len, width)
    d_normed = lax.dynamic_update_slice_in_dim(
        d_normed, lax.dynamic_slice_in_dim(d_normed, att_start, n_att, 0) + d_att_in, att_start, 0
    )
    d_normed_own = lax.psum_scatter(
        d_normed.reshape(row_count, width).astype(jnp.bfloat16),
        MODEL,
        scatter_dimension=0,
        tiled=True,
    ).astype(jnp.float32)
    d_normed_own = d_normed_own.reshape(n_own, seq_len, width)
    normed_own, block_back = jax.vjp(layer_norm, stream_own.astype(single))
    d_stream_in = d_stream_own + block_back(d_normed_own * gain_vals[0])[0]
    d_block_gain = jnp.sum(d_normed_own * normed_own, axis=(0, 1))
    d_patch = jnp.dot(
        patches.reshape(n_own * npatch, PD).astype(single).T,
        d_stream_in[:, :npatch].reshape(n_own * npatch, width),
        precision=highest,
    )
    d_table = jnp.sum(d_stream_in, axis=0)
    zero_row = jnp.zeros((width,), single)
    gain_offset = lax.axis_index("heads") * group_width
    d_gains = jnp.stack(
        [
            d_block_gain,
            d_final_gain,
            lax.dynamic_update_slice_in_dim(zero_row, d_query_gain, gain_offset, 0),
            lax.dynamic_update_slice_in_dim(zero_row, d_key_gain, gain_offset, 0),
        ]
    )
    grad_patch, grad_table, grad_gains, grad_head = (
        lax.psum_scatter(d_patch, ALL, scatter_dimension=1, tiled=True),
        lax.psum_scatter(d_table, ALL, scatter_dimension=1, tiled=True),
        lax.psum_scatter(d_gains, ALL, scatter_dimension=1, tiled=True),
        lax.psum_scatter(d_head, ALL, scatter_dimension=0, tiled=True),
    )
    grad_qkv = lax.psum_scatter(d_qkv, DATA, scatter_dimension=0, tiled=True)
    grad_out, grad_up, grad_down = (
        lax.psum_scatter(d_out.astype(jnp.bfloat16), "dp", scatter_dimension=1, tiled=True).astype(
            jnp.float32
        ),
        lax.psum_scatter(d_up.astype(jnp.bfloat16), "dp", scatter_dimension=0, tiled=True).astype(
            jnp.float32
        ),
        lax.psum_scatter(d_down.astype(jnp.bfloat16), "dp", scatter_dimension=1, tiled=True).astype(
            jnp.float32
        ),
    )
    grads = [grad_patch, grad_table, grad_gains, grad_head, grad_qkv, grad_out, grad_up, grad_down]
    grad_squares = jnp.stack([jnp.sum(grad * grad) for grad in grads])
    weight_squares = jnp.stack([jnp.sum(master * master) for master in masters])
    grad_squares, weight_squares, loss_sum = lax.psum(
        (grad_squares, weight_squares, jnp.sum(loss_terms)), ALL
    )
    grad_norm = jnp.sqrt(jnp.sum(grad_squares))
    clip = jnp.minimum(1.0, clip_at / grad_norm)
    new_firsts, new_seconds, updates = ([], [], [])
    for master, first, second, grad in zip(masters, firsts, seconds, grads):
        clipped = grad * clip
        first_new = beta_one * first + (1.0 - beta_one) * clipped
        second_new = beta_two * second + (1.0 - beta_two) * clipped * clipped
        update = (
            first_new
            / (1.0 - beta_one**STEP)
            / (jnp.sqrt(second_new / (1.0 - beta_two**STEP)) + adam_eps)
        )
        updates.append(update + decay_rate * master)
        new_firsts.append(first_new)
        new_seconds.append(second_new)
    update_squares = lax.psum(
        jnp.stack([jnp.sum(update * update) for update in updates]), ALL
    )
    ratios = jnp.sqrt(weight_squares) / jnp.sqrt(update_squares)
    new_weights = [
        master - learn_rate * ratios[number] * update
        for number, (master, update) in enumerate(zip(masters, updates))
    ]
    return (
        loss_sum,
        grad_norm,
        new_firsts[0],
        new_firsts[1],
        new_firsts[2],
        new_firsts[3],
        new_firsts[4],
        new_firsts[5],
        new_firsts[6],
        new_firsts[7],
        new_seconds[0],
        new_seconds[1],
        new_seconds[2],
        new_seconds[3],
        new_seconds[4],
        new_seconds[5],
        new_seconds[6],
        new_seconds[7],
        new_weights[0],
        new_weights[1],
        new_weights[2],
        new_weights[3],
        new_weights[4],
        new_weights[5],
        new_weights[6],
        new_weights[7],
    )


def dot(a, b):
    return jnp.dot(a, b, preferred_element_type=jnp.float32)


def dot_nt(a, b, precision=None):
    return lax.dot_general(
        a, b, (((1,), (1,)), ((), ())), precision=precision, preferred_element_type=jnp.float32
    )


def dot_tn(a, b, precision=None):
    return lax.dot_general(
        a, b, (((0,), (0,)), ((), ())), precision=precision, preferred_element_type=jnp.float32
    )


def norm_parts(values):
    center = values - jnp.mean(values, axis=-1, keepdims=True)
    scale = lax.rsqrt(jnp.mean(center * center, axis=-1, keepdims=True) + norm_eps)
    return center * scale, scale


def norm_back(normed, scale, grad):
    inner = jnp.mean(grad * normed, axis=-1, keepdims=True)
    return scale * (grad - jnp.mean(grad, axis=-1, keepdims=True) - normed * inner)


gelu_c = 0.7978845608028654


def gelu_tanh(u):
    return jnp.tanh(gelu_c * (u + 0.044715 * (u * u * u)))


def iota(shape, axis):
    return lax.broadcasted_iota(jnp.int32, shape, axis)


def one_update(master, first, second, grad, clip):
    clipped = grad * clip
    first_new = beta_one * first + (1.0 - beta_one) * clipped
    second_new = beta_two * second + (1.0 - beta_two) * clipped * clipped
    one, two = 1.0 / (1.0 - beta_one**STEP), 1.0 / (1.0 - beta_two**STEP)
    update = (first_new * one) / (jnp.sqrt(second_new * two) + adam_eps)
    return first_new, second_new, update + decay_rate * master


def square_sum(values):
    return jnp.sum(values * values, axis=(0, 1), keepdims=True)


KINDS = ("patch", "table", "gains", "head", "qkv", "out", "up", "down")
EXT, QKV, UP0, UP1, HEAD, OUT, DN0, DN1 = range(8)
LEFT, RIGHT, ON_LEFT, ON_RIGHT = "left", "right", "on_left", "on_right"
ROWS = 208
N_HID = 4


def step_kernel(sizes, names, *refs):
    npatch, seq_len, classes, total_images = sizes
    r = types.SimpleNamespace(**dict(zip(names, refs)))
    bfloat, single = jnp.bfloat16, jnp.float32
    dp, h, z = (lax.axis_index(a) for a in ALL)
    core, y = lax.rem(dp, 2), dp // 2
    y_dp, core_dp = (1 - y) * 2 + core, y * 2 + (1 - core)
    x_dev, y_dev, core_dev = (dp, 1 - h, z), (y_dp, h, z), (core_dp, h, z)
    z_up = [lax.rem(z + k, N_HID) for k in range(N_HID)]
    z_down = [lax.rem(z + N_HID - k, N_HID) for k in range(N_HID)]
    z_dev = [(dp, h, z_up[k]) for k in range(N_HID)]
    group = [(h, y, z_up[k]) for k in range(1, N_HID)]
    for gh, gy in ((1 - h, y), (h, 1 - y), (1 - h, 1 - y)):
        group.extend((gh, gy, z_up[k]) for k in range(N_HID))
    source = [(h, y, z_down[k]) for k in range(1, N_HID)]
    for gh, gy in ((1 - h, y), (h, 1 - y), (1 - h, 1 - y)):
        source.extend((gh, gy, z_down[k]) for k in range(N_HID))
    group_dev = [(gy * 2 + core, gh, gz) for gh, gy, gz in group]

    barrier = pltpu.get_barrier_semaphore()
    for device in [core_dev] + group_dev:
        pl.semaphore_signal(barrier, inc=1, device_id=device, device_id_type=MESH)

    loads = {}
    order = ["w_up", "w_patch", "w_table", "w_gains"]
    order += ["w_" + k for k in KINDS if "w_" + k not in order] + ["patches"]
    order += [p + k for p in ("m_", "v_") for k in KINDS]

    def load(names):
        for name in names:
            loads[name] = pltpu.make_async_copy(
                getattr(r, "h_" + name), getattr(r, name), r.lsem.at[order.index(name)]
            )
            loads[name].start()

    load(order[0:9])
    stores = []

    def store(name):
        copy = pltpu.make_async_copy(
            getattr(r, name), getattr(r, "h_" + name), r.lsem.at[len(order) + len(stores)]
        )
        copy.start()
        stores.append(copy)

    ssem, rsem = r.ssem, r.rsem
    count = [0]
    sends = {}
    last = N_HID - 1
    holds = {}
    for d in range(1, N_HID):
        holds[LEFT, d] = z >= d
        holds[RIGHT, d] = z + d <= last
        holds[ON_RIGHT, d] = (z >= d) & (z < last)
        holds[ON_LEFT, d] = (z + d <= last) & (z > 0)
    holds[ON_RIGHT, 0] = z < last
    holds[ON_LEFT, 0] = z > 0
    next_z = {LEFT: (dp, h, z_up[1]), RIGHT: (dp, h, z_down[1])}

    def send(source, target, device, key=None):
        number = count[0]
        count[0] += 1
        copy = pltpu.make_async_remote_copy(
            src_ref=source,
            dst_ref=target,
            send_sem=ssem.at[number],
            recv_sem=rsem.at[number],
            device_id=device,
            device_id_type=MESH,
        )
        if key is None:
            copy.start()
        else:
            pl.when(holds[key])(copy.start)
        sends.setdefault(key, []).append(copy)
        return number

    def arrive(target, number, device):
        pltpu.make_async_remote_copy(
            src_ref=target,
            dst_ref=target,
            send_sem=ssem.at[number],
            recv_sem=rsem.at[number],
            device_id=device,
            device_id_type=MESH,
        ).wait_recv()

    gext, gqkv, gout, gup, gdn, ghd = r.gext, r.gqkv, r.gout, r.gup, r.gdn, r.ghd
    x0, x1, px = r.x0, r.x1, r.px
    kept = types.SimpleNamespace()

    def pack_ext():
        x1[0:24, :] = jnp.zeros((24, 512), single)
        for name in order[1:4]:
            loads[name].wait()
        x1[0:24, 256 : 256 + seq_len] = r.w_table[...]
        pick = (iota((4, 256), 1) == iota((4, 256), 0) + seq_len).astype(bfloat)
        table_part = x1[0:24, 256:512] + dot_tn(r.w_gains[...].astype(bfloat), pick)
        wp = r.w_patch[...]
        gext[dp, z] = jnp.concatenate(
            [wp[:, 0:512], jnp.concatenate([wp[:, 512:768], table_part], axis=1)], axis=0
        ).astype(bfloat)

    def pack_patches():
        row, col = iota((ROWS, 256), 0), iota((ROWS, 256), 1)
        spot = jnp.where((row == col) & (row < seq_len), 1.0, 0.0).astype(bfloat)
        px[0, :, 768:1024] = spot
        px[1, :, 768:1024] = spot
        px[0, ROWS - 16 : ROWS, 0:768] = jnp.zeros((16, 768), bfloat)
        loads["patches"].wait()
        px[0, 0:npatch, 0:768] = r.patches[0]

    def pack_qkv():
        loads["w_qkv"].wait()
        gqkv[:, z // 2, dp, lax.rem(z, 2)] = r.w_qkv[...].astype(bfloat)

    def pack_up():
        loads["w_up"].wait()
        gup[z, :, dp] = r.w_up[...].astype(bfloat).reshape(2, 96, 384)

    def pack_head():
        loads["w_head"].wait()
        x0[0:24, :] = r.w_head[:, 0:512]
        x1[0:24, :] = jnp.zeros((24, 512), single)
        x1[0:24, 0 : classes - 512] = r.w_head[:, 512:classes]
        ghd[h, dp, z] = jnp.concatenate([x0[0:24, :], x1[0:24, :]], axis=0).astype(bfloat)

    def pack_out():
        loads["w_out"].wait()
        gout[dp, z] = jnp.zeros((96, 256), bfloat)
        gout[dp, z, :, 0:192] = r.w_out[...].astype(bfloat)

    def pack_down():
        loads["w_down"].wait()
        gdn[z, :, y, core] = r.w_down[...].astype(bfloat).reshape(2, 96, 384)

    def at_ext(d, w):
        return gext.at[d, w]

    def at_qkv(d, w):
        return gqkv.at[:, w // 2, d, lax.rem(w, 2)]

    def at_out(d, w):
        return gout.at[d, w]

    def at_up(half):
        return lambda d, w: gup.at[w, half, d]

    def at_dn(half):
        return lambda d, w: gdn.at[w, half, d // 2, lax.rem(d, 2)]

    def at_hd(d, w):
        return ghd.at[h, d, w]

    slot = {
        EXT: at_ext,
        QKV: at_qkv,
        OUT: at_out,
        UP0: at_up(0),
        UP1: at_up(1),
        DN0: at_dn(0),
        DN1: at_dn(1),
        HEAD: at_hd,
    }
    lines = {
        EXT: lambda d: gext.at[d],
        QKV: lambda d: gqkv.at[:, :, d],
        OUT: lambda d: gout.at[d],
        UP0: lambda d: gup.at[:, 0, d],
        UP1: lambda d: gup.at[:, 1, d],
        DN0: lambda d: gdn.at[:, 0, d // 2, lax.rem(d, 2)],
        DN1: lambda d: gdn.at[:, 1, d // 2, lax.rem(d, 2)],
        HEAD: lambda d: ghd.at[h, d],
    }
    tags = {}

    def own_z(name):
        own = slot[name](dp, z)
        tags[name, LEFT, 1] = send(own, own, next_z[LEFT], (ON_RIGHT, 0))
        tags[name, RIGHT, 1] = send(own, own, next_z[RIGHT], (ON_LEFT, 0))

    def own_y(name):
        own = slot[name](dp, z)
        tags[name, "y", 0] = send(own, own, y_dev)

    def pass_z(name, d):
        for side, on, theirs in ((LEFT, ON_RIGHT, z_down[d]), (RIGHT, ON_LEFT, z_up[d])):
            block = slot[name](dp, theirs)
            number = tags[name, side, d]
            pl.when(holds[side, d])(functools.partial(arrive, block, number, y_dev))
            if d < last:
                tags[name, side, d + 1] = send(block, block, next_z[side], (on, d))
            tags[name, "y", side, d] = send(block, block, y_dev, (side, d))
        if d == last and name != HEAD:
            line = lines[name](dp)
            tags[name, "c", 0] = send(line, line, core_dev)

    def pair_own():
        arrive(slot[DN0](y_dp, z), tags[DN0, "y", 0], y_dev)
        own = gdn.at[z, 0, :, core]
        tags[DN0, LEFT, 1] = send(own, own, next_z[LEFT], (ON_RIGHT, 0))
        tags[DN0, RIGHT, 1] = send(own, own, next_z[RIGHT], (ON_LEFT, 0))

    def pair_z(d):
        for side, on, theirs in ((LEFT, ON_RIGHT, z_down[d]), (RIGHT, ON_LEFT, z_up[d])):
            block = gdn.at[theirs, 0, :, core]
            number = tags[DN0, side, d]
            pl.when(holds[side, d])(functools.partial(arrive, block, number, y_dev))
            if d < last:
                tags[DN0, side, d + 1] = send(block, block, next_z[side], (on, d))
        if d == last:
            block = gdn.at[:, 0, :, core]
            tags[DN0, "c", 0] = send(block, block, core_dev)

    def pair_complete():
        arrive(gdn.at[:, 0, :, 1 - core], tags[DN0, "c", 0], core_dev)

    def pass_core(name):
        at = slot[name]
        arrive(at(y_dp, z), tags[name, "y", 0], y_dev)
        for d in range(1, N_HID):
            for side, theirs in ((LEFT, z_down[d]), (RIGHT, z_up[d])):
                number = tags[name, "y", side, d]
                pl.when(holds[side, d])(functools.partial(arrive, at(y_dp, theirs), number, y_dev))
        line = lines[name](y_dp)
        if name != HEAD:
            tags[name, "c", 1] = send(line, line, core_dev)
        else:
            own = lines[name](dp)
            tags[name, "x", 0] = send(own, own, x_dev)
            tags[name, "x", 1] = send(line, line, x_dev)

    def complete(name):
        far = (1 - y) * 2 + (1 - core)
        arrive(lines[name](core_dp), tags[name, "c", 0], core_dev)
        arrive(lines[name](far), tags[name, "c", 1], core_dev)

    def head_core():
        for i, d in enumerate((dp, y_dp)):
            arrive(ghd.at[1 - h, d], tags[HEAD, "x", i], x_dev)
        for i, d in enumerate((dp, y_dp)):
            block = ghd.at[:, d]
            tags[HEAD, "c", i] = send(block, block, core_dev)

    def head_complete():
        far = (1 - y) * 2 + (1 - core)
        for i, d in enumerate((core_dp, far)):
            arrive(ghd.at[:, d], tags[HEAD, "c", i], core_dev)

    def send_images():
        images = px.at[0, :, pl.ds(0, 768)]
        tags["px"] = send(images, px.at[1, :, pl.ds(0, 768)], x_dev)

    ga, st = r.ga, r.st
    rows_of = (iota((8, 512), 1) == iota((8, 512), 0) + (256 + seq_len)) & (iota((8, 512), 0) < 4)

    def unpack(block_of, low, high):
        for d in range(4):
            for w in range(N_HID):
                s = (d * N_HID + w) * 24
                block = block_of(d, w).astype(single)
                low[s : s + 24, :] = block[0:24]
                high[s : s + 24, :] = block[24:48]

    def embed(i):
        if i == 0:
            unpack(lambda d, w: gext[d, w], x0, x1)
            ga[h] = dot_nt(rows_of.astype(bfloat), x1[...].astype(bfloat))
            tags["ga"] = send(ga.at[h], ga.at[h], x_dev)
        else:
            arrive(px.at[1, :, pl.ds(0, 768)], tags["px"], x_dev)
        low, high = x0[...].astype(bfloat), x1[...].astype(bfloat)
        made = dot_nt(px[i, :, 0:512], low) + dot_nt(px[i, :, 512:1024], high)
        st[h, i] = made.astype(bfloat)
        tags["st", i] = send(st.at[h, i], st.at[h, 1 - i], x_dev)

    def gain_row(i):
        return jnp.concatenate([ga[0, i : i + 1, :], ga[1, i : i + 1, :]], axis=1)

    def head_gain(i):
        pieces = []
        both = [ga[0, i : i + 1, :], ga[1, i : i + 1, :]]
        for d in range(4):
            pieces.extend(half[:, d * 96 : d * 96 + 96] for half in both)
        low = jnp.concatenate(pieces[0:4], axis=1)
        high = jnp.concatenate(pieces[4:8], axis=1)
        return jnp.where(h == 0, low, high)

    nb, nbt = r.nb, r.nbt

    def block_norm():
        arrive(ga.at[1 - h], tags["ga"], x_dev)
        arrive(st.at[1 - h, 1], tags["st", 0], x_dev)
        arrive(st.at[1 - h, 0], tags["st", 1], x_dev)
        gain = gain_row(0)
        for i in range(2):
            stream = jnp.concatenate([st[0, i], st[1, i]], axis=1).astype(single)
            nb[i * ROWS : (i + 1) * ROWS, :] = (norm_parts(stream)[0] * gain).astype(bfloat)

    nq, sq, bd = r.nq, r.sq, r.bd
    q_ref, k_ref, v_ref = r.q, r.k, r.v

    def head_mean(values):
        return dot(values.astype(bfloat), bd[...])

    def project(c):
        mixed = dot(nb[...], gqkv[c].reshape(768, 384))
        if c == 0:
            same = iota((384, 384), 0) // HD == iota((384, 384), 1) // HD
            bd[...] = jnp.where(same, 1.0 / HD, 0.0).astype(bfloat)
        if c < 2:
            top = mixed.astype(bfloat).astype(single)
            center = mixed - (head_mean(top) + head_mean(mixed - top))
            scale = lax.rsqrt(head_mean(center * center) + norm_eps)
            normed = center * scale
            nq[c] = normed
            sq[c] = scale
            mixed = normed * head_gain(2 + c)
        out = (q_ref, k_ref, v_ref)[c]
        mixed = mixed.astype(bfloat)
        for n in range(6):
            part = mixed[:, n * HD : (n + 1) * HD]
            out[2 * n] = part[0:ROWS]
            out[2 * n + 1] = part[ROWS : 2 * ROWS]

    pr, hof = r.pr, r.hof
    dead = iota((ROWS, ROWS), 1) >= seq_len

    def attend(pair, carry):
        for i in range(2):
            made = []
            for side in range(2):
                n = 4 * pair + 2 * side + i
                scores = dot_nt(q_ref[n], k_ref[n]) * HD ** (-0.5)
                scores = jnp.where(dead, -1e30, scores)
                scores = scores - jnp.max(scores, axis=-1, keepdims=True)
                weights = jnp.exp(scores)
                probs = weights / jnp.sum(weights, axis=-1, keepdims=True)
                pr[n] = probs
                made.append(dot(probs.astype(bfloat), v_ref[n]))
            both = jnp.concatenate(made, axis=1).astype(bfloat)
            hof[i * ROWS : (i + 1) * ROWS, pl.ds(pl.multiple_of(pair * 128, 128), 128)] = both
        return carry

    us, hb, br = r.us, r.hb, r.br

    def rise(w, carry):
        upper = dot(nb[...], gup[w].reshape(768, 384))
        us[w] = upper
        hb[w] = (0.5 * upper * (1.0 + gelu_tanh(upper))).astype(bfloat)
        return carry

    def project_out():
        lefts, rights = [], []
        for d in range(4):
            part = dot(hof[...], gout[d].reshape(384, 256))
            lefts.append(part[:, 0:96])
            rights.append(part[:, 96:192])
        br[:, 0:384] = jnp.concatenate(lefts, axis=1)
        br[:, 384:768] = jnp.concatenate(rights, axis=1)

    def turn_normed():
        nbt[...] = nb[...].T

    brs, brr = r.brs, r.brr

    def fall(half):
        lanes = slice(half * 384, half * 384 + 384)

        def add(w, carry):
            br[:, lanes] += dot_nt(hb[w], gdn[w, half].reshape(384, 384))
            return carry

        lax.fori_loop(0, N_HID, add, 0)

    def share(half, i):
        lanes = slice(half * 384, half * 384 + 384)
        brs[half, i] = br[i * ROWS : (i + 1) * ROWS, lanes].astype(bfloat)
        tags["br", half, i] = send(brs.at[half, i], brr.at[half, 1 - i], x_dev)

    hw = r.hw

    def unpack_head():
        for a in range(2):
            unpack(lambda d, w: ghd[a, d, w], x0, x1)
            hw[0, a * 384 : a * 384 + 384, :] = x0[...].astype(bfloat)
            hw[1, a * 384 : a * 384 + 384, :] = x1[...].astype(bfloat)

    def stream_out(i):
        for half in range(2):
            arrive(brr.at[half, i], tags["br", half, 1 - i], x_dev)
        stream = jnp.concatenate([st[0, i], st[1, i]], axis=1).astype(single)
        theirs = jnp.concatenate([brr[0, i], brr[1, i]], axis=1).astype(single)
        return norm_parts(stream + (br[i * ROWS : (i + 1) * ROWS, :] + theirs))

    pl.semaphore_wait(barrier, 1 + len(group_dev))
    pack_up()
    own_z(UP1)
    own_y(UP1)
    pack_ext()
    own_z(EXT)
    own_z(UP0)
    own_y(UP0)
    pack_patches()
    pack_head()
    pack_down()
    own_y(DN0)
    pass_z(UP1, 1)
    pass_z(EXT, 1)
    send_images()
    pass_z(UP0, 1)
    own_y(EXT)
    own_z(HEAD)
    pass_z(EXT, 2)
    pass_z(UP1, 2)
    pack_qkv()
    own_y(QKV)
    own_z(QKV)
    pass_z(EXT, 3)
    pack_out()
    own_z(OUT)
    pass_z(HEAD, 1)
    pass_z(UP1, 3)
    pair_own()
    pass_z(UP0, 2)
    pass_core(EXT)
    complete(EXT)
    pass_z(QKV, 1)
    embed(0)
    load(order[9:])
    pass_z(HEAD, 2)
    embed(1)
    pass_z(UP0, 3)
    pass_core(UP1)
    own_y(HEAD)
    pass_z(QKV, 2)
    pass_z(OUT, 1)
    pass_core(UP0)
    own_z(DN1)
    pass_z(HEAD, 3)
    pass_z(QKV, 3)
    complete(UP0)
    complete(UP1)
    pair_z(1)
    own_y(OUT)
    pass_z(OUT, 2)
    block_norm()
    lax.fori_loop(0, 2, rise, 0)
    lax.fori_loop(2, 4, rise, 0)
    pass_z(DN1, 1)
    pass_core(HEAD)
    pass_core(QKV)
    pass_z(OUT, 3)
    own_y(DN1)
    pair_z(2)
    complete(QKV)
    project(0)
    project(1)
    project(2)
    lax.fori_loop(0, 1, attend, 0)
    lax.fori_loop(1, 2, attend, 0)
    pass_core(OUT)
    pass_z(DN1, 2)
    pair_z(3)
    lax.fori_loop(2, 3, attend, 0)
    complete(OUT)
    project_out()
    pair_complete()
    fall(0)
    share(0, 1)
    share(0, 0)
    pass_z(DN1, 3)
    pass_core(DN1)
    complete(DN1)
    fall(1)
    share(1, 1)
    share(1, 0)
    head_core()
    head_complete()
    unpack_head()
    turn_normed()
    block_gain, q_gain, k_gain = gain_row(0), head_gain(2), head_gain(3)

    out_n, out_scale = stream_out(0)
    is_patch = iota((ROWS, 1), 0) < npatch
    final_gain = gain_row(1)
    n_sum = jnp.sum(jnp.where(is_patch, out_n, 0.0), axis=0, keepdims=True)
    pooled = n_sum * final_gain / npatch
    pooled_b = pooled.astype(bfloat)
    heads_b = [hw[0], hw[1]]
    pooled_8 = jnp.broadcast_to(pooled_b, (16, 768))
    logits = jnp.concatenate([dot(pooled_8, m)[0:1] for m in heads_b], axis=1)
    lane = iota((1, 1024), 1)
    logits = jnp.where(lane < classes, logits, -1e30)
    top = jnp.max(logits, axis=-1, keepdims=True)
    log_total = top + jnp.log(jnp.sum(jnp.exp(logits - top), axis=-1, keepdims=True))
    onehot = jnp.where(lane == r.labels[h * N_HID + z], 1.0, 0.0)
    term = log_total - jnp.sum(jnp.where(lane < classes, logits, 0.0) * onehot, axis=-1, keepdims=True)
    d_logits = (jnp.exp(logits - log_total) - onehot) / total_images
    hi = d_logits.astype(bfloat).astype(single)
    both = jnp.concatenate([hi, d_logits - hi, jnp.zeros((14, 1024), single)], axis=0).astype(bfloat)
    back = dot_nt(both[:, 0:512], heads_b[0]) + dot_nt(both[:, 512:1024], heads_b[1])
    d_pooled = (back[0:1] + back[1:2]) / npatch
    d_row = d_pooled * final_gain
    rw = r.rw
    rw[0] = jnp.broadcast_to(d_row, (8, 768))
    tag_rw = send(rw.at[0], rw.at[1], x_dev)
    ds, db, dbt = r.ds, r.db, r.dbt
    d_stream = jnp.where(is_patch, norm_back(out_n, out_scale, d_row), 0.0)
    ds[...] = d_stream
    db[0] = d_stream.astype(bfloat)
    dbt[:, 0:ROWS] = d_stream.T.astype(bfloat)
    d_final_gain = d_pooled * n_sum
    al = r.al
    pooled_f = pooled_b.astype(single)
    al[core, h, y, z] = jnp.concatenate(
        [d_logits[:, q * 256 : q * 256 + 256] for q in range(4)]
        + [pooled_f[:, q * 256 : q * 256 + 256] for q in range(3)]
        + [jnp.zeros((1, 256), single)],
        axis=0,
    )
    own = al.at[core, h, y, z]
    tag_al = [send(own, own, device) for device in group_dev]
    out_n, out_scale = stream_out(1)
    arrive(rw.at[1], tag_rw, x_dev)
    d_stream = jnp.where(is_patch, norm_back(out_n, out_scale, rw[1, 0:1, :]), 0.0)
    db[1] = d_stream.astype(bfloat)
    dbt[:, ROWS : 2 * ROWS] = d_stream.T.astype(bfloat)
    db2 = db[...].reshape(2 * ROWS, 768)

    rff, f1, f2, ft, f3 = r.rff, r.f1, r.f2, r.ft, r.f3
    dn, dm = br, r.dm
    kept = types.SimpleNamespace(fresh=True, gains=[])

    def add_in(part):
        if kept.fresh:
            dn[...] = part
        else:
            dn[...] += part
        kept.fresh = False

    def ff_send(m, k):
        tags["ff", m, k] = send(rff.at[k, m, :, :, 1 - core], f1.at[k, m], core_dev)

    def ff_down(k):
        rff[k, 0] = dot(dbt[...], hb[z_up[k]]).astype(bfloat).reshape(2, 2, 2, 96, 384)
        ff_send(0, k)

    def ff_up(k):
        w = z_up[k]
        upper = us[w]
        t = gelu_tanh(upper)
        slope = 0.5 * (1.0 + t) + 0.5 * upper * (1.0 - t * t) * gelu_c * (
            1.0 + 3 * 0.044715 * (upper * upper)
        )
        d_upper = (dot(db2, gdn[w].reshape(768, 384)) * slope).astype(bfloat)
        us[w] = d_upper.astype(single)
        rff[k, 1] = dot(nbt[...], d_upper).astype(bfloat).reshape(2, 2, 2, 96, 384)
        ff_send(1, k)

    def ff_in(k):
        w = z_up[k]
        add_in(dot_nt(us[w].astype(bfloat), gup[w].reshape(768, 384)))

    def ff_y(m, k):
        arrive(f1.at[k, m], tags["ff", m, k], core_dev)
        f1[k, m] = f1[k, m] + rff[k, m, :, :, core]
        tags["fy", m, k] = send(f1.at[k, m, :, 1 - y], f2.at[k, m], y_dev)

    def ff_z(m, k):
        arrive(f2.at[k, m], tags["fy", m, k], y_dev)
        if k:
            ft[k - 1, m] = f1[k, m, :, y] + f2[k, m]
            tags["fz", m, k] = send(ft.at[k - 1, m], f3.at[k - 1, m], z_dev[k])

    def ff_end():
        for m, name in enumerate(("g_down", "g_up")):
            total = f1[0, m, :, y].astype(single) + f2[0, m].astype(single)
            for k in range(1, N_HID):
                arrive(f3.at[k - 1, m], tags["fz", m, k], z_dev[k])
                total = total + f3[k - 1, m].astype(single)
            getattr(r, name)[...] = total.reshape(192, 384)
            store(name)

    def pass_rows():
        for i, place in enumerate(source):
            arrive(al.at[(core, *place)], tag_al[i], core_dev)
        tags["al"] = send(al.at[core], al.at[core], core_dev)

    rout, o1, o2, ot, o3, pc = r.rout, r.o1, r.o2, r.ot, r.o3, r.pc

    def cut_branch():
        for d in range(4):
            low = db2[:, d * 96 : d * 96 + 96]
            high = db2[:, 384 + d * 96 : 384 + d * 96 + 96]
            pc[d] = jnp.concatenate([low, high], axis=1)

    def out_grad():
        hot = hof[...].T
        for d in range(4):
            rout[:, d // 2, d % 2] = jnp.zeros((N_HID, 96, 256), bfloat)
            grad = dot(hot, pc[d]).astype(bfloat).reshape(N_HID, 96, 192)
            rout[:, d // 2, d % 2, :, 0:192] = grad
        tags["o1"] = send(rout.at[:, :, 1 - core], o1, core_dev)

    dh = r.dh

    def out_back():
        d_heads = None
        for d in range(4):
            part = dot_nt(pc[d], gout[d].reshape(384, 256)[:, 0:192])
            d_heads = part if d_heads is None else d_heads + part
        d_heads = d_heads.astype(bfloat)
        for n in range(6):
            part = d_heads[:, n * HD : (n + 1) * HD]
            dh[2 * n] = part[0:ROWS]
            dh[2 * n + 1] = part[ROWS : 2 * ROWS]

    def out_y():
        arrive(o1, tags["o1"], core_dev)
        o1[...] = o1[...] + rout[:, :, core]
        tags["o2"] = send(o1.at[:, 1 - y], o2, y_dev)

    def out_z():
        arrive(o2, tags["o2"], y_dev)
        ot[...] = o1[:, y] + o2[...]
        tags["o3"] = [send(ot.at[z_up[k]], o3.at[k - 1], z_dev[k]) for k in range(1, N_HID)]

    def out_end():
        total = ot[z].astype(single)
        for k in range(1, N_HID):
            arrive(o3.at[k - 1], tags["o3"][k - 1], z_dev[k])
            total = total + o3[k - 1].astype(single)
        r.g_out[...] = total[:, 0:192]
        store("g_out")

    dqkv = r.dqkv

    def attend_back(pair, carry):
        for i in range(2):
            made = ([], [], [])
            for side in range(2):
                n = 4 * pair + 2 * side + i
                probs = pr[n]
                d_out = dh[n]
                d_probs = dot_nt(d_out, v_ref[n])
                inner = jnp.sum(probs * d_probs, axis=-1, keepdims=True)
                d_scores = (probs * (d_probs - inner)).astype(bfloat)
                made[0].append(dot(d_scores, k_ref[n]) * HD ** (-0.5))
                made[1].append(dot_tn(d_scores, q_ref[n]) * HD ** (-0.5))
                made[2].append(dot_tn(probs.astype(bfloat), d_out))
            for c in range(3):
                both = jnp.concatenate(made[c], axis=1)
                lanes = pl.ds(pl.multiple_of(pair * 128, 128), 128)
                dqkv[c, i * ROWS : (i + 1) * ROWS, lanes] = both
        return carry

    rqkv, q1, q2, qt, q3 = r.rqkv, r.q1, r.q2, r.qt, r.q3

    def mix_back():
        for c, gain in enumerate((q_gain, k_gain, None)):
            grad = dqkv[c]
            if gain is not None:
                normed = nq[c]
                kept.gains.append(jnp.sum(grad * normed, axis=0, keepdims=True))
                grad = grad * gain
                grad = sq[c] * (grad - head_mean(grad) - normed * head_mean(grad * normed))
            dm[c] = grad.astype(bfloat)
            add_in(dot_nt(dm[c], gqkv[c].reshape(768, 384)))

    dns, dnr = r.dns, r.dnr

    def send_in():
        dns[...] = dn[ROWS : 2 * ROWS, :].astype(bfloat)
        tags["dn"] = send(dns, dnr, x_dev)

    def qkv_grad(c):
        rqkv[c] = dot(nbt[...], dm[c]).astype(bfloat).reshape(2, 2, 2, 2, 48, 384)
        tags["q1", c] = send(rqkv.at[c, :, :, 1 - core], q1.at[c], core_dev)

    def qkv_y(c):
        arrive(q1.at[c], tags["q1", c], core_dev)
        q1[c] = q1[c] + rqkv[c, :, :, core]
        tags["q2", c] = send(q1.at[c, :, 1 - y], q2.at[c], y_dev)

    def qkv_z(c):
        arrive(q2.at[c], tags["q2", c], y_dev)
        qt[c] = q1[c, :, y] + q2[c]
        for k in range(1, N_HID):
            block = qt.at[c, z_up[k] // 2, lax.rem(z_up[k], 2)]
            tags["q3", c, k] = send(block, q3.at[k - 1, c], z_dev[k])

    def qkv_end():
        for c in range(3):
            total = qt[c, z // 2, lax.rem(z, 2)].astype(single)
            for k in range(1, N_HID):
                arrive(q3.at[k - 1, c], tags["q3", c, k], z_dev[k])
                total = total + q3[k - 1, c].astype(single)
            r.g_qkv[c] = total
        store("g_qkv")

    def head_grad():
        arrive(al.at[1 - core], tags["al"], core_dev)
        rows_all = al[...].reshape(32, 8, 256)
        d_logits_all = jnp.concatenate([rows_all[:, q, :] for q in range(4)], axis=1)
        pooled_all = jnp.concatenate([rows_all[:, 4 + q, :] for q in range(3)], axis=1)
        start = ((h * 4 + dp) * N_HID + z) * 24
        chosen = (iota((24, 768), 1) == iota((24, 768), 0) + start).astype(bfloat)
        mine = dot_nt(chosen, pooled_all.astype(bfloat))
        g_head = jnp.dot(mine, d_logits_all, precision=highest, preferred_element_type=single)
        r.g_head[...] = g_head[:, 0:classes]
        store("g_head")

    dx, gg = r.dx, r.gg

    def spread(row):
        blank = jnp.zeros((1, 192), single)
        halves = []
        for a in range(2):
            part = jnp.concatenate([row[:, a * 96 : a * 96 + 96], row[:, 192 + a * 96 : 288 + a * 96]], axis=1)
            halves.append(
                jnp.where(
                    h == 0,
                    jnp.concatenate([part, blank], axis=1),
                    jnp.concatenate([blank, part], axis=1),
                )
            )
        return jnp.concatenate(halves, axis=1)

    def norm_in():
        arrive(dnr, tags["dn"], x_dev)
        d_normed = dn[0:ROWS, :] + dnr[...].astype(single)
        block_n, block_scale = norm_parts(jnp.concatenate([st[0, 0], st[1, 0]], axis=1).astype(single))
        d_block_gain = jnp.sum(d_normed * block_n, axis=0, keepdims=True)
        d_in = ds[...] + norm_back(block_n, block_scale, d_normed * block_gain)
        low, high = d_in[:, 0:384], d_in[:, 384:768]
        dx[2] = jnp.where(h == 0, high, low).astype(bfloat)
        tags["dx"] = send(dx.at[2], dx.at[1], x_dev)
        dx[0] = jnp.where(h == 0, low, high).astype(bfloat)
        d_gains = jnp.concatenate(
            [d_block_gain, d_final_gain, spread(kept.gains[0]), spread(kept.gains[1])]
            + [jnp.zeros((4, 768), single)],
            axis=0,
        )
        low, high = d_gains[:, 0:384], d_gains[:, 384:768]
        gg[0] = jnp.where(h == 0, low, high)
        gg[2] = jnp.where(h == 0, high, low)
        tags["gg"] = send(gg.at[2], gg.at[1], x_dev)

    rext, e1, e2, et, e3 = r.rext, r.e1, r.e2, r.et, r.e3

    def ext_grad():
        arrive(dx.at[1], tags["dx"], x_dev)
        arrive(gg.at[1], tags["gg"], x_dev)
        dxt = jnp.concatenate([dx[0].astype(single), dx[1].astype(single)], axis=0).T.astype(bfloat)
        px2 = px[...].reshape(2 * ROWS, 1024)
        d_gains = (gg[0] + gg[1]).astype(bfloat)
        x0[...] = dot(dxt, px2[:, 0:512])
        x1[...] = dot(dxt, px2[:, 512:1024]) + dot_tn(d_gains, rows_of.astype(bfloat))
        for d in range(4):
            for w in range(N_HID):
                s = (d * N_HID + w) * 24
                rext[d // 2, d % 2, w] = jnp.concatenate(
                    [x0[s : s + 24, :], x1[s : s + 24, :]], axis=0
                ).astype(bfloat)
        tags["e1"] = send(rext.at[:, 1 - core], e1, core_dev)

    def ext_y():
        arrive(e1, tags["e1"], core_dev)
        e1[...] = e1[...] + rext[:, core]
        tags["e2"] = send(e1.at[1 - y], e2, y_dev)

    def ext_z():
        arrive(e2, tags["e2"], y_dev)
        et[...] = e1[y] + e2[...]
        tags["e3"] = [send(et.at[z_up[k]], e3.at[k - 1], z_dev[k]) for k in range(1, N_HID)]

    def ext_end():
        total = et[z].astype(single)
        for k in range(1, N_HID):
            arrive(e3.at[k - 1], tags["e3"][k - 1], z_dev[k])
            total = total + e3[k - 1].astype(single)
        r.g_patch[:, 0:512] = total[0:24]
        r.g_patch[:, 512:768] = total[24:48, 0:256]
        r.g_table[...] = total[24:48, 256 : 256 + seq_len]
        columns = total[24:48, 256:512]
        pick_f = (iota((8, 256), 1) == iota((8, 256), 0) + seq_len).astype(single)
        r.g_gains[...] = dot_nt(pick_f, columns, precision=highest)[0:4]
        for name in ("g_patch", "g_table", "g_gains"):
            store(name)

    ff_down(2)
    ff_up(3)
    ff_y(0, 2)
    cut_branch()
    out_back()
    ff_down(1)
    ff_up(1)
    ff_y(0, 1)
    pass_rows()
    ff_y(1, 3)
    ff_up(2)
    ff_z(0, 2)
    ff_in(2)
    out_grad()
    ff_up(0)
    ff_in(0)
    ff_z(0, 1)
    ff_y(1, 2)
    lax.fori_loop(0, 1, attend_back, 0)
    lax.fori_loop(1, 2, attend_back, 0)
    ff_y(1, 1)
    ff_z(1, 3)
    ff_down(0)
    ff_in(3)
    ff_in(1)
    ff_down(3)
    out_y()
    lax.fori_loop(2, 3, attend_back, 0)
    ff_y(0, 3)
    ff_z(1, 1)
    ff_z(1, 2)
    mix_back()
    send_in()
    qkv_grad(0)
    qkv_y(0)
    qkv_grad(2)
    qkv_grad(1)
    qkv_y(2)
    out_z()
    qkv_y(1)
    ff_y(1, 0)
    norm_in()
    ff_z(0, 3)
    qkv_z(2)
    ext_grad()
    qkv_z(1)
    qkv_z(0)
    ext_y()
    head_grad()
    ext_z()
    ff_y(0, 0)
    ff_z(0, 0)
    qkv_end()
    ff_z(1, 0)
    out_end()
    ff_end()

    def read(prefix, kind):
        values = getattr(r, prefix + kind)[...]
        return values.reshape(-1, values.shape[-1])
    lane = iota((8, 128), 1)
    own = jnp.zeros((8, 128), single)
    grad_square = jnp.zeros((1, 1), single)
    for n, kind in enumerate(KINDS):
        own = jnp.where(lane == 8 + n, square_sum(read("w_", kind)), own)
        if n > 2:
            grad_square = grad_square + square_sum(read("g_", kind))
    ext_end()

    own = jnp.where(lane == 0, term, own)
    for kind in KINDS[0:3]:
        grad_square = grad_square + square_sum(read("g_", kind))
    own = jnp.where(lane == 1, grad_square, own)

    def all_sum(vector, pair, every):
        pair[0] = vector[0:1]
        tag = send(pair.at[0], pair.at[1], core_dev)
        arrive(pair.at[1], tag, core_dev)
        every[h, y, z] = pair[0] + pair[1]
        mine = every.at[h, y, z]
        numbers = [send(mine, mine, device) for device in group_dev]
        for i, place in enumerate(source):
            arrive(every.at[place], numbers[i], core_dev)
        total = jnp.sum(every[...].reshape(16, 1, 128), axis=0)
        return jnp.broadcast_to(total, (8, 128))

    sums = all_sum(own, r.l1, r.v1)
    grad_norm = jnp.sqrt(jnp.sum(jnp.where(lane == 1, sums, 0.0), axis=1, keepdims=True))[0:1]
    clip = jnp.minimum(1.0, clip_at / grad_norm)
    own = jnp.zeros((8, 128), single)
    for name in order[9:]:
        loads[name].wait()
    for n, kind in enumerate(KINDS):
        update = one_update(read("w_", kind), read("m_", kind), read("v_", kind), read("g_", kind), clip)[2]
        own = jnp.where(lane == 8 + n, square_sum(update), own)
    updates = all_sum(own, r.l2, r.v2)
    result = jnp.sqrt(sums) / jnp.sqrt(updates)
    result = jnp.where(lane == 0, sums, result)
    result = jnp.where(lane == 1, grad_norm, result)
    result = jnp.where(lane == 2, clip, result)
    r.scalars[...] = result
    store("scalars")
    for copy in stores:
        copy.wait()
    for key, copies in sends.items():

        def settle(copies=copies):
            for copy in copies:
                copy.wait_send()

        if key is None:
            settle()
        else:
            pl.when(holds[key])(settle)


def write_kernel(names, *refs):
    r = types.SimpleNamespace(**dict(zip(names, refs)))
    lane = iota((8, 128), 1)
    turns = (3, 4, 6, 7, 0, 5, 1, 2)
    inputs = ["scalars"] + [p + KINDS[n] for n in turns for p in ("w_", "m_", "v_", "g_")]
    loads = {}
    for number, name in enumerate(inputs):
        loads[name] = pltpu.make_async_copy(
            getattr(r, "h_" + name), getattr(r, name), r.lsem.at[number]
        )
        loads[name].start()
    loads["scalars"].wait()

    def pick(n):
        return jnp.sum(jnp.where(lane == n, r.scalars[...], 0.0), axis=1, keepdims=True)[0:1]

    clip = pick(2)
    r.o_loss[...] = pick(0)
    r.o_norm[...] = pick(1)
    stores = []
    for n in turns:
        kind = KINDS[n]
        for p in ("w_", "m_", "v_", "g_"):
            loads[p + kind].wait()
        master = getattr(r, "w_" + kind)[...]
        grad = getattr(r, "g_" + kind)[...]
        ratio, c = pick(8 + n), clip
        if len(master.shape) == 3:
            c, ratio = clip[None], ratio[None]
        first, second, update = one_update(
            master, getattr(r, "m_" + kind)[...], getattr(r, "v_" + kind)[...], grad, c
        )
        results = (first, second, master - learn_rate * ratio * update)
        for p, value in zip(("nm_", "nv_", "nw_"), results):
            getattr(r, p + kind)[...] = value
            copy = pltpu.make_async_copy(
                getattr(r, p + kind),
                getattr(r, "h_" + p + kind),
                r.lsem.at[len(inputs) + len(stores)],
            )
            copy.start()
            stores.append(copy)
    for copy in stores:
        copy.wait()


def fast_device(patches, labels, *state):
    bfloat, single = jnp.bfloat16, jnp.float32

    def turn(kind, value):
        if kind in ("patch", "table", "down"):
            return value.T
        if kind == "qkv":
            return value.transpose(1, 0, 2)
        return value

    flat = [turn(KINDS[i % 8], value) for i, value in enumerate(state)]
    hbm = pl.BlockSpec(memory_space=pl.ANY)
    smem = pl.BlockSpec(memory_space=pltpu.SMEM)
    in_names = ["patches"] + [p + k for p in ("w_", "m_", "v_") for k in KINDS]
    out_names = ["g_" + k for k in KINDS] + ["scalars"]
    scratch = dict(
        px=((2, ROWS, 1024), bfloat),
        gext=((4, 4, 48, 512), bfloat),
        gqkv=((3, 2, 4, 2, 48, 384), bfloat),
        gout=((4, 4, 96, 256), bfloat),
        gup=((4, 2, 4, 96, 384), bfloat),
        gdn=((4, 2, 2, 2, 96, 384), bfloat),
        ghd=((2, 4, 4, 48, 512), bfloat),
        x0=((384, 512), single),
        x1=((384, 512), single),
        hw=((2, 768, 512), bfloat),
        ga=((2, 8, 384), single),
        st=((2, 2, ROWS, 384), bfloat),
        nb=((2 * ROWS, 768), bfloat),
        nbt=((768, 2 * ROWS), bfloat),
        nq=((2, 2 * ROWS, 384), single),
        sq=((2, 2 * ROWS, 384), single),
        bd=((384, 384), bfloat),
        q=((12, ROWS, HD), bfloat),
        k=((12, ROWS, HD), bfloat),
        v=((12, ROWS, HD), bfloat),
        pr=((12, ROWS, ROWS), single),
        hof=((2 * ROWS, 384), bfloat),
        us=((4, 2 * ROWS, 384), single),
        hb=((4, 2 * ROWS, 384), bfloat),
        br=((2 * ROWS, 768), single),
        brs=((2, 2, ROWS, 384), bfloat),
        brr=((2, 2, ROWS, 384), bfloat),
        rw=((2, 8, 768), single),
        ds=((ROWS, 768), single),
        db=((2, ROWS, 768), bfloat),
        dbt=((768, 2 * ROWS), bfloat),
        al=((2, 2, 2, 4, 8, 256), single),
        rff=((4, 2, 2, 2, 2, 96, 384), bfloat),
        f1=((4, 2, 2, 2, 96, 384), bfloat),
        f2=((4, 2, 2, 96, 384), bfloat),
        ft=((3, 2, 2, 96, 384), bfloat),
        f3=((3, 2, 2, 96, 384), bfloat),
        rout=((4, 2, 2, 96, 256), bfloat),
        o1=((4, 2, 96, 256), bfloat),
        o2=((4, 96, 256), bfloat),
        ot=((4, 96, 256), bfloat),
        o3=((3, 96, 256), bfloat),
        dh=((12, ROWS, HD), bfloat),
        dm=((3, 2 * ROWS, 384), bfloat),
        pc=((4, 2 * ROWS, 192), bfloat),
        dqkv=((3, 2 * ROWS, 384), single),
        rqkv=((3, 2, 2, 2, 2, 48, 384), bfloat),
        q1=((3, 2, 2, 2, 48, 384), bfloat),
        q2=((3, 2, 2, 48, 384), bfloat),
        qt=((3, 2, 2, 48, 384), bfloat),
        q3=((3, 3, 48, 384), bfloat),
        dns=((ROWS, 768), bfloat),
        dnr=((ROWS, 768), bfloat),
        dx=((3, ROWS, 384), bfloat),
        gg=((3, 8, 384), single),
        rext=((2, 2, 4, 48, 512), bfloat),
        e1=((2, 4, 48, 512), bfloat),
        e2=((4, 48, 512), bfloat),
        et=((4, 48, 512), bfloat),
        e3=((3, 48, 512), bfloat),
        l1=((2, 1, 128), single),
        l2=((2, 1, 128), single),
        v1=((2, 2, 4, 1, 128), single),
        v2=((2, 2, 4, 1, 128), single),
    )
    semaphores = 320
    shapes = [flat[i].shape for i in range(8)]
    npatch, seq_len, classes = patches.shape[1], flat[1].shape[1], flat[3].shape[1]
    total_images = labels.shape[0] * lax.axis_size("dp")
    sizes = (npatch, seq_len, classes, total_images)
    held = [(patches.shape, bfloat)] + [(s, single) for s in shapes * 4] + [((8, 128), single)]
    names = ["labels"] + ["h_" + n for n in in_names + out_names] + in_names + out_names
    names += list(scratch) + ["ssem", "rsem", "lsem"]
    found = pl.pallas_call(
        functools.partial(step_kernel, sizes, names),
        out_shape=[jax.ShapeDtypeStruct(s, single) for s in shapes]
        + [jax.ShapeDtypeStruct((8, 128), single)],
        in_specs=[smem] + [hbm] * 25,
        out_specs=[hbm] * 9,
        scratch_shapes=[pltpu.VMEM(s, t) for s, t in held + list(scratch.values())]
        + [pltpu.SemaphoreType.DMA((semaphores,))] * 2
        + [pltpu.SemaphoreType.DMA((len(held),))],
        compiler_params=pltpu.CompilerParams(
            collective_id=0, has_side_effects=True, vmem_limit_bytes=62 * 2**20
        ),
        name="train_step",
    )(labels, patches, *flat)
    grads, scalars = found[:8], found[8]
    in_names = ["scalars"] + [p + k for p in ("w_", "m_", "v_", "g_") for k in KINDS]
    out_names = [p + k for p in ("nm_", "nv_", "nw_") for k in KINDS]
    held = [((8, 128), single)] + [(s, single) for s in shapes * 7]
    names = ["h_" + n for n in in_names + out_names] + ["o_loss", "o_norm"]
    names += in_names + out_names + ["lsem"]
    written = pl.pallas_call(
        functools.partial(write_kernel, names),
        out_shape=[jax.ShapeDtypeStruct(s, single) for s in shapes * 3 + [(1, 1), (1, 1)]],
        in_specs=[hbm] * 33,
        out_specs=[hbm] * 24 + [pl.BlockSpec(memory_space=pltpu.VMEM)] * 2,
        scratch_shapes=[pltpu.VMEM(s, t) for s, t in held]
        + [pltpu.SemaphoreType.DMA((len(held),))],
        compiler_params=pltpu.CompilerParams(vmem_limit_bytes=62 * 2**20),
        name="write_step",
    )(scalars, *flat, *grads)
    back = [turn(KINDS[i % 8], value) for i, value in enumerate(written[:24])]
    return (written[24].reshape(()), written[25].reshape(()), *back)


def fits(mesh):
    return tuple(mesh.shape[a] for a in ALL) == (4, 2, N_HID)


def solution(mesh):
    placed = (
        P(ALL, None, None),
        P("dp"),
        P(None, ALL),
        P(None, ALL),
        P(None, ALL),
        P(ALL, None),
        P(DATA, None, "heads"),
        P(MODEL, "dp"),
        P("dp", MODEL),
        P(MODEL, "dp"),
        P(None, ALL),
        P(None, ALL),
        P(None, ALL),
        P(ALL, None),
        P(DATA, None, "heads"),
        P(MODEL, "dp"),
        P("dp", MODEL),
        P(MODEL, "dp"),
        P(None, ALL),
        P(None, ALL),
        P(None, ALL),
        P(ALL, None),
        P(DATA, None, "heads"),
        P(MODEL, "dp"),
        P("dp", MODEL),
        P(MODEL, "dp"),
    )
    return jax.shard_map(
        fast_device if fits(mesh) else per_device,
        mesh=mesh,
        in_specs=placed,
        out_specs=(
            P(),
            P(),
            P(None, ALL),
            P(None, ALL),
            P(None, ALL),
            P(ALL, None),
            P(DATA, None, "heads"),
            P(MODEL, "dp"),
            P("dp", MODEL),
            P(MODEL, "dp"),
            P(None, ALL),
            P(None, ALL),
            P(None, ALL),
            P(ALL, None),
            P(DATA, None, "heads"),
            P(MODEL, "dp"),
            P("dp", MODEL),
            P(MODEL, "dp"),
            P(None, ALL),
            P(None, ALL),
            P(None, ALL),
            P(ALL, None),
            P(DATA, None, "heads"),
            P(MODEL, "dp"),
            P("dp", MODEL),
            P(MODEL, "dp"),
        ),
        check_vma=False,
    )
```
